32 devices in a mesh: seq: 2 (over x), fsdp: 16 (over z, y, core).
Axes of the slice: x: 2, y: 2, z: 4, core: 2. Of those that a mesh axis runs over, the one named last changes fastest.
Arguments:
- inputs: bfloat16 [48, 1296, 768], P('fsdp', 'seq'), may hold values from -6 to 6
- cotangent: bfloat16 [48, 1296, 768], P('fsdp', 'seq'), may hold values from -6 to 6
- first_gain: bfloat16 [768], P('fsdp'), may hold values from 0.5 to 1.5
- first_shift: bfloat16 [768], P('fsdp'), may hold values from -3 to 3
- qkv_weight: bfloat16 [768, 2304], P('fsdp'), may hold values from -0.3125 to 0.3125
- query_bias: bfloat16 [768], P('fsdp'), may hold values from -3 to 3
- value_bias: bfloat16 [768], P('fsdp'), may hold values from -3 to 3
- proj_weight: bfloat16 [768, 768], P('fsdp'), may hold values from -3.5 to 3.5
- proj_bias: bfloat16 [768], P('fsdp'), may hold values from -3 to 3
- second_gain: bfloat16 [768], P('fsdp'), may hold values from 0.5 to 1.5
- second_shift: bfloat16 [768], P('fsdp'), may hold values from -3 to 3
- hidden_weight: bfloat16 [768, 3072], P('fsdp'), may hold values from -0.21875 to 0.21875
- hidden_bias: bfloat16 [3072], P('fsdp'), may hold values from -3 to 3
- output_weight: bfloat16 [3072, 768], P('fsdp'), may hold values from -0.109375 to 0.109375
- output_bias: bfloat16 [768], P('fsdp'), may hold values from -3 to 3
Outputs:
- block_out: bfloat16 [48, 1296, 768], P('fsdp', 'seq')
- input_grad: bfloat16 [48, 1296, 768], P('fsdp', 'seq')
- grad_first_gain: float32 [768], P('fsdp')
- grad_first_shift: float32 [768], P('fsdp')
- grad_qkv_weight: float32 [768, 2304], P('fsdp')
- grad_query_bias: float32 [768], P('fsdp')
- grad_value_bias: float32 [768], P('fsdp')
- grad_proj_weight: float32 [768, 768], P('fsdp')
- grad_proj_bias: float32 [768], P('fsdp')
- grad_second_gain: float32 [768], P('fsdp')
- grad_second_shift: float32 [768], P('fsdp')
- grad_hidden_weight: float32 [768, 3072], P('fsdp')
- grad_hidden_bias: float32 [3072], P('fsdp')
- grad_output_weight: float32 [3072, 768], P('fsdp')
- grad_output_bias: float32 [768], P('fsdp')
The draws below stay inside these ranges and needn't reach their ends.
All inputs are finite; a program needn't handle non-finite values.
Results may differ from the reference program's by a relative error of at most 0.02.
Values may be sent and summed in bfloat16 or wider, within the bound.
No kernel may reach another device: no remote copies, remote signals or barrier semaphores. Data moves between devices by JAX's collectives and lax.ppermute only.
A program may use at most 384 MiB of HBM per device.

```python
import jax
import jax.numpy as jnp
from jax import lax

D = 768
HEADS = 12
HEAD_DIM = 64
FF = 3072
SEQ_LEN = 1296
IMAGES = 48


def block_levels(own_key, shape, shards, least, top_value):
    loudness, own = 1.0, jax.random.fold_in(own_key, 6)
    for position, parts in shards:
        steps = jnp.exp(jax.random.uniform(jax.random.fold_in(own, position), (parts,), jnp.float32, least / len(shards), top_value / len(shards)))
        loudness = loudness * jnp.repeat(steps, shape[position] // parts).reshape([-1 if axis == position else 1 for axis in range(len(shape))])
    return loudness


def gaussian(key, shape, deviation, bound, pieces=(), dtype=jnp.bfloat16):
    values = jax.random.normal(key, shape, jnp.float32) * deviation
    if len(pieces) > 0:
        values = block_levels(key, shape, pieces, -0.22, 0.18) * values
    return jnp.clip(values, min=-bound, max=bound).astype(dtype)


def setup_inputs(seed: int = 0) -> dict:
    key_list = jax.random.split(jax.random.key(seed), 16)
    inputs = gaussian(key_list[0], (IMAGES, SEQ_LEN, D), 1.0, 6.0, ((0, 16), (1, 2)))
    cotangent = gaussian(key_list[1], (IMAGES, SEQ_LEN, D), 1.0, 6.0, ((0, 16), (1, 2)))
    first_gain = jnp.clip(1.0 + 0.1 * jax.random.normal(key_list[2], (D,), jnp.float32), 0.5, 1.5).astype(jnp.bfloat16)
    first_shift = gaussian(key_list[3], (D,), 0.5, 3.0, ((0, 16),))
    qkv_weight = gaussian(key_list[4], (D, 3 * D), (D // 2) ** -0.5, 0.3125, ((0, 16),))
    query_bias = gaussian(key_list[5], (D,), 0.5, 3.0, ((0, 16),))
    value_bias = gaussian(key_list[6], (D,), 0.5, 3.0, ((0, 16),))
    proj_weight = gaussian(key_list[7], (D, D), (D // 256) ** -0.5, 3.5, ((0, 16),))
    proj_bias = gaussian(key_list[8], (D,), 0.5, 3.0, ((0, 16),))
    second_gain = jnp.clip(1.0 + 0.1 * jax.random.normal(key_list[9], (D,), jnp.float32), 0.5, 1.5).astype(jnp.bfloat16)
    second_shift = gaussian(key_list[10], (D,), 0.5, 3.0, ((0, 16),))
    hidden_weight = gaussian(key_list[11], (D, FF), D ** -0.5, 0.21875, ((0, 16),))
    hidden_bias = gaussian(key_list[12], (FF,), 0.5, 3.0, ((0, 16),))
    output_weight = gaussian(key_list[13], (FF, D), FF ** -0.5, 0.109375, ((0, 16),))
    output_bias = gaussian(key_list[14], (D,), 0.5, 3.0, ((0, 16),))
    return dict(inputs=inputs, cotangent=cotangent, first_gain=first_gain, first_shift=first_shift, qkv_weight=qkv_weight, query_bias=query_bias, value_bias=value_bias, proj_weight=proj_weight, proj_bias=proj_bias, second_gain=second_gain, second_shift=second_shift, hidden_weight=hidden_weight, hidden_bias=hidden_bias, output_weight=output_weight, output_bias=output_bias)


EPS = 1e-06

@jax.custom_vjp
def low(v):
    return lax.optimization_barrier(v.astype(jnp.bfloat16)).astype(jnp.float32)

@jax.custom_vjp
def low_back(v):
    return v

def low_keep(v):
    return (low(v), None)

def low_pass(kept, grad):
    return (grad,)

def back_keep(v):
    return (v, None)

def back_low(kept, grad):
    return (low(grad),)
low.defvjp(low_keep, low_pass)
low_back.defvjp(back_keep, back_low)

def normalize(rows, gain, shift):
    row_mean = lax.optimization_barrier(jnp.mean(rows, -1, keepdims=True))
    centred = rows - row_mean
    variance = lax.optimization_barrier(jnp.mean(centred * centred, -1, keepdims=True))
    return centred * lax.rsqrt(variance + EPS) * gain + shift

def matmul(left, right):
    return jnp.dot(left, right, precision=lax.Precision.HIGHEST, preferred_element_type=jnp.float32)

def block(image, params):
    gain_one, shift_one, full_qkv, bias_query, bias_value, full_proj, bias_proj, gain_two, shift_two, full_hidden, bias_hidden, full_output, bias_output = params
    normed = low(normalize(image, gain_one, shift_one))
    projected = matmul(normed, full_qkv)
    query = low(low_back(projected[:, :D] + bias_query)).reshape(SEQ_LEN, HEADS, HEAD_DIM)
    keys = low(low_back(projected[:, D:2 * D])).reshape(SEQ_LEN, HEADS, HEAD_DIM)
    values = low(low_back(projected[:, 2 * D:] + bias_value)).reshape(SEQ_LEN, HEADS, HEAD_DIM)
    scores = jnp.einsum('qhd,khd->hqk', query, keys, precision=lax.Precision.HIGHEST, preferred_element_type=jnp.float32) * HEAD_DIM ** (-0.5)
    scores = low_back(scores)
    row_max = lax.optimization_barrier(jnp.max(scores, -1, keepdims=True))
    exponent = jnp.exp(scores - row_max)
    probs = exponent / lax.optimization_barrier(jnp.sum(exponent, -1, keepdims=True))
    mixed = jnp.einsum('hqk,khd->qhd', low(probs), values, precision=lax.Precision.HIGHEST, preferred_element_type=jnp.float32).reshape(SEQ_LEN, D)
    mixed = low(low_back(mixed))
    attended = low_back(matmul(mixed, full_proj) + bias_proj)
    middle = image + attended
    normed_two = low(normalize(middle, gain_two, shift_two))
    hidden_pre = low_back(matmul(normed_two, full_hidden) + bias_hidden)
    activated = low(jax.nn.gelu(hidden_pre, approximate=False))
    branch = low_back(matmul(activated, full_output) + bias_output)
    return middle + branch

def reference(inputs, cotangent, first_gain, first_shift, qkv_weight, query_bias, value_bias, proj_weight, proj_bias, second_gain, second_shift, hidden_weight, hidden_bias, output_weight, output_bias):
    params = (first_gain.astype(jnp.float32), first_shift.astype(jnp.float32), qkv_weight.astype(jnp.float32), query_bias.astype(jnp.float32), value_bias.astype(jnp.float32), proj_weight.astype(jnp.float32), proj_bias.astype(jnp.float32), second_gain.astype(jnp.float32), second_shift.astype(jnp.float32), hidden_weight.astype(jnp.float32), hidden_bias.astype(jnp.float32), output_weight.astype(jnp.float32), output_bias.astype(jnp.float32))

    def one_image(totals, items):
        image, upstream = items
        result, pull = jax.vjp(block, image.astype(jnp.float32), params)
        grad_image, grad_params = pull(upstream.astype(jnp.float32))
        totals = jax.tree.map(jnp.add, totals, grad_params)
        return (totals, (result.astype(jnp.bfloat16), grad_image.astype(jnp.bfloat16)))
    zeros = jax.tree.map(jnp.zeros_like, params)
    totals, (outputs, grads) = lax.scan(one_image, zeros, (inputs, cotangent))
    return (outputs, grads, totals[0], totals[1], totals[2], totals[3], totals[4], totals[5], totals[6], totals[7], totals[8], totals[9], totals[10], totals[11], totals[12])
```

```python
import functools

import jax
import jax.numpy as jnp
from jax import lax
from jax.experimental import pallas as pl
from jax.experimental.pallas import tpu as pltpu
from jax.sharding import PartitionSpec as P

HEADS = 12
HEAD_DIM = 64


EPS = 1e-06


def normalize(rows, gain, shift):
    row_mean = jnp.mean(rows, -1, keepdims=True)
    centred = rows - row_mean
    variance = jnp.mean(centred * centred, -1, keepdims=True)
    scaled = lax.rsqrt(variance + EPS)
    unit = centred * scaled
    return (unit * gain + shift, unit, scaled)


def norm_back(grad_out, unit, scaled, gain):
    grad_unit = grad_out * gain
    first_mean = jnp.mean(grad_unit, -1, keepdims=True)
    second_mean = jnp.mean(grad_unit * unit, -1, keepdims=True)
    return scaled * (grad_unit - first_mean - unit * second_mean)


def gelu_exact(value):
    return jax.nn.gelu(value, approximate=False)


def column_sum(values):
    return jnp.sum(values.astype(jnp.float32), 0)


def general_body(
    inputs,
    cotangent,
    first_gain,
    first_shift,
    qkv_weight,
    query_bias,
    value_bias,
    proj_weight,
    proj_bias,
    second_gain,
    second_shift,
    hidden_weight,
    hidden_bias,
    output_weight,
    output_bias,
):
    images, local_len, width = inputs.shape
    row_count = images * local_len
    factor = HEAD_DIM ** (-0.5)
    (
        gain_one,
        shift_one,
        full_qkv,
        bias_query,
        bias_value,
        full_proj,
        bias_proj,
        gain_two,
        shift_two,
        full_hidden,
        bias_hidden,
        full_output,
        bias_output,
    ) = (
        lax.all_gather(first_gain, "fsdp", axis=0, tiled=True),
        lax.all_gather(first_shift, "fsdp", axis=0, tiled=True),
        lax.all_gather(qkv_weight, "fsdp", axis=0, tiled=True),
        lax.all_gather(query_bias, "fsdp", axis=0, tiled=True),
        lax.all_gather(value_bias, "fsdp", axis=0, tiled=True),
        lax.all_gather(proj_weight, "fsdp", axis=0, tiled=True),
        lax.all_gather(proj_bias, "fsdp", axis=0, tiled=True),
        lax.all_gather(second_gain, "fsdp", axis=0, tiled=True),
        lax.all_gather(second_shift, "fsdp", axis=0, tiled=True),
        lax.all_gather(hidden_weight, "fsdp", axis=0, tiled=True),
        lax.all_gather(hidden_bias, "fsdp", axis=0, tiled=True),
        lax.all_gather(output_weight, "fsdp", axis=0, tiled=True),
        lax.all_gather(output_bias, "fsdp", axis=0, tiled=True),
    )
    rows = inputs.reshape(row_count, width).astype(jnp.float32)
    normed, unit_one, scale_one = normalize(
        rows, gain_one.astype(jnp.float32), shift_one.astype(jnp.float32)
    )
    normed_low = normed.astype(jnp.bfloat16)
    projected = jnp.dot(normed_low, full_qkv, preferred_element_type=jnp.float32)
    head_shape = (images, local_len, HEADS, HEAD_DIM)
    query = (
        (projected[:, :width] + bias_query.astype(jnp.float32))
        .astype(jnp.bfloat16)
        .reshape(head_shape)
    )
    keys = projected[:, width : 2 * width].astype(jnp.bfloat16).reshape(head_shape)
    values = (
        (projected[:, 2 * width :] + bias_value.astype(jnp.float32))
        .astype(jnp.bfloat16)
        .reshape(head_shape)
    )
    all_keys, all_values = (
        lax.all_gather(keys, "seq", axis=1, tiled=True),
        lax.all_gather(values, "seq", axis=1, tiled=True),
    )

    def attend(items):
        query_one, key_one, value_one = items
        scores = (
            jnp.einsum("qhd,khd->hqk", query_one, key_one, preferred_element_type=jnp.float32)
            * factor
        )
        row_max = jnp.max(scores, -1, keepdims=True)
        exponent = jnp.exp(scores - row_max)
        row_total = jnp.sum(exponent, -1, keepdims=True)
        weights = (exponent / row_total).astype(jnp.bfloat16)
        mixed_one = jnp.einsum(
            "hqk,khd->qhd", weights, value_one, preferred_element_type=jnp.float32
        )
        return (mixed_one, (row_max + jnp.log(row_total))[..., 0])

    mixed, log_total = lax.map(attend, (query, all_keys, all_values))
    mixed_low = mixed.reshape(row_count, width).astype(jnp.bfloat16)
    attended = jnp.dot(mixed_low, full_proj, preferred_element_type=jnp.float32) + bias_proj.astype(
        jnp.float32
    )
    middle = rows + attended
    normed_two, unit_two, scale_two = normalize(
        middle, gain_two.astype(jnp.float32), shift_two.astype(jnp.float32)
    )
    normed_two_low = normed_two.astype(jnp.bfloat16)
    hidden_pre = jnp.dot(
        normed_two_low, full_hidden, preferred_element_type=jnp.float32
    ) + bias_hidden.astype(jnp.float32)
    activated = gelu_exact(hidden_pre).astype(jnp.bfloat16)
    branch = jnp.dot(
        activated, full_output, preferred_element_type=jnp.float32
    ) + bias_output.astype(jnp.float32)
    block_out = (middle + branch).astype(jnp.bfloat16).reshape(inputs.shape)
    upstream = cotangent.reshape(row_count, width).astype(jnp.float32)
    grad_branch = upstream.astype(jnp.bfloat16)
    grad_output_w = jnp.einsum(
        "rf,rd->fd", activated, grad_branch, preferred_element_type=jnp.float32
    )
    grad_output_b = column_sum(grad_branch)
    grad_act = jnp.einsum("rd,fd->rf", grad_branch, full_output, preferred_element_type=jnp.float32)
    unused_value, pull_gelu = jax.vjp(gelu_exact, hidden_pre)
    grad_hidden = pull_gelu(grad_act)[0].astype(jnp.bfloat16)
    grad_hidden_w = jnp.einsum(
        "rd,rf->df", normed_two_low, grad_hidden, preferred_element_type=jnp.float32
    )
    grad_hidden_b = column_sum(grad_hidden)
    grad_normed_two = jnp.einsum(
        "rf,df->rd", grad_hidden, full_hidden, preferred_element_type=jnp.float32
    )
    grad_gain_two = jnp.sum(grad_normed_two * unit_two, 0)
    grad_shift_two = jnp.sum(grad_normed_two, 0)
    grad_middle = upstream + norm_back(
        grad_normed_two, unit_two, scale_two, gain_two.astype(jnp.float32)
    )
    grad_attended = grad_middle.astype(jnp.bfloat16)
    grad_proj_w = jnp.einsum(
        "re,rd->ed", mixed_low, grad_attended, preferred_element_type=jnp.float32
    )
    grad_proj_b = column_sum(grad_attended)
    grad_mixed = jnp.einsum(
        "rd,ed->re", grad_attended, full_proj, preferred_element_type=jnp.float32
    )
    grad_mixed = grad_mixed.astype(jnp.bfloat16).reshape(head_shape)

    def attend_back(items):
        query_one, key_one, value_one, grad_one, log_one = items
        scores = (
            jnp.einsum("qhd,khd->hqk", query_one, key_one, preferred_element_type=jnp.float32)
            * factor
        )
        probs = jnp.exp(scores - log_one[..., None])
        grad_value = jnp.einsum(
            "hqk,qhd->khd", probs.astype(jnp.bfloat16), grad_one, preferred_element_type=jnp.float32
        )
        grad_probs = jnp.einsum(
            "qhd,khd->hqk", grad_one, value_one, preferred_element_type=jnp.float32
        )
        inner = jnp.sum(probs * grad_probs, -1, keepdims=True)
        grad_scores = (probs * (grad_probs - inner)).astype(jnp.bfloat16)
        grad_query = (
            jnp.einsum("hqk,khd->qhd", grad_scores, key_one, preferred_element_type=jnp.float32)
            * factor
        )
        grad_key = (
            jnp.einsum("hqk,qhd->khd", grad_scores, query_one, preferred_element_type=jnp.float32)
            * factor
        )
        return (grad_query, grad_key, grad_value)

    grad_query, grad_keys, grad_values = lax.map(
        attend_back, (query, all_keys, all_values, grad_mixed, log_total)
    )
    grad_keys, grad_values = (
        lax.psum_scatter(
            grad_keys.astype(jnp.bfloat16), "seq", scatter_dimension=1, tiled=True
        ).astype(jnp.float32),
        lax.psum_scatter(
            grad_values.astype(jnp.bfloat16), "seq", scatter_dimension=1, tiled=True
        ).astype(jnp.float32),
    )
    grad_qkv = jnp.concatenate(
        [
            grad_query.reshape(row_count, width),
            grad_keys.reshape(row_count, width),
            grad_values.reshape(row_count, width),
        ],
        -1,
    ).astype(jnp.bfloat16)
    grad_qkv_w = jnp.einsum("rd,rc->dc", normed_low, grad_qkv, preferred_element_type=jnp.float32)
    grad_query_b = column_sum(grad_qkv[:, :width])
    grad_value_b = column_sum(grad_qkv[:, 2 * width :])
    grad_normed = jnp.einsum("rc,dc->rd", grad_qkv, full_qkv, preferred_element_type=jnp.float32)
    grad_gain_one = jnp.sum(grad_normed * unit_one, 0)
    grad_shift_one = jnp.sum(grad_normed, 0)
    grad_rows = grad_middle + norm_back(
        grad_normed, unit_one, scale_one, gain_one.astype(jnp.float32)
    )
    input_grad = grad_rows.astype(jnp.bfloat16).reshape(inputs.shape)
    parts = (
        lax.psum_scatter(
            grad_gain_one.astype(jnp.bfloat16), "fsdp", scatter_dimension=0, tiled=True
        ).astype(jnp.float32),
        lax.psum_scatter(
            grad_shift_one.astype(jnp.bfloat16), "fsdp", scatter_dimension=0, tiled=True
        ).astype(jnp.float32),
        lax.psum_scatter(
            grad_qkv_w.astype(jnp.bfloat16), "fsdp", scatter_dimension=0, tiled=True
        ).astype(jnp.float32),
        lax.psum_scatter(
            grad_query_b.astype(jnp.bfloat16), "fsdp", scatter_dimension=0, tiled=True
        ).astype(jnp.float32),
        lax.psum_scatter(
            grad_value_b.astype(jnp.bfloat16), "fsdp", scatter_dimension=0, tiled=True
        ).astype(jnp.float32),
        lax.psum_scatter(
            grad_proj_w.astype(jnp.bfloat16), "fsdp", scatter_dimension=0, tiled=True
        ).astype(jnp.float32),
        lax.psum_scatter(
            grad_proj_b.astype(jnp.bfloat16), "fsdp", scatter_dimension=0, tiled=True
        ).astype(jnp.float32),
        lax.psum_scatter(
            grad_gain_two.astype(jnp.bfloat16), "fsdp", scatter_dimension=0, tiled=True
        ).astype(jnp.float32),
        lax.psum_scatter(
            grad_shift_two.astype(jnp.bfloat16), "fsdp", scatter_dimension=0, tiled=True
        ).astype(jnp.float32),
        lax.psum_scatter(
            grad_hidden_w.astype(jnp.bfloat16), "fsdp", scatter_dimension=0, tiled=True
        ).astype(jnp.float32),
        lax.psum_scatter(
            grad_hidden_b.astype(jnp.bfloat16), "fsdp", scatter_dimension=0, tiled=True
        ).astype(jnp.float32),
        lax.psum_scatter(
            grad_output_w.astype(jnp.bfloat16), "fsdp", scatter_dimension=0, tiled=True
        ).astype(jnp.float32),
        lax.psum_scatter(
            grad_output_b.astype(jnp.bfloat16), "fsdp", scatter_dimension=0, tiled=True
        ).astype(jnp.float32),
    )
    shares = (
        lax.psum(parts[0].astype(jnp.bfloat16), "seq").astype(jnp.float32),
        lax.psum(parts[1].astype(jnp.bfloat16), "seq").astype(jnp.float32),
        lax.psum(parts[2].astype(jnp.bfloat16), "seq").astype(jnp.float32),
        lax.psum(parts[3].astype(jnp.bfloat16), "seq").astype(jnp.float32),
        lax.psum(parts[4].astype(jnp.bfloat16), "seq").astype(jnp.float32),
        lax.psum(parts[5].astype(jnp.bfloat16), "seq").astype(jnp.float32),
        lax.psum(parts[6].astype(jnp.bfloat16), "seq").astype(jnp.float32),
        lax.psum(parts[7].astype(jnp.bfloat16), "seq").astype(jnp.float32),
        lax.psum(parts[8].astype(jnp.bfloat16), "seq").astype(jnp.float32),
        lax.psum(parts[9].astype(jnp.bfloat16), "seq").astype(jnp.float32),
        lax.psum(parts[10].astype(jnp.bfloat16), "seq").astype(jnp.float32),
        lax.psum(parts[11].astype(jnp.bfloat16), "seq").astype(jnp.float32),
        lax.psum(parts[12].astype(jnp.bfloat16), "seq").astype(jnp.float32),
    )
    return (
        block_out,
        input_grad,
        shares[0],
        shares[1],
        shares[2],
        shares[3],
        shares[4],
        shares[5],
        shares[6],
        shares[7],
        shares[8],
        shares[9],
        shares[10],
        shares[11],
        shares[12],
    )


F32 = jnp.float32
BF16 = jnp.bfloat16
VMEM_BYTES = 60 * 1024 * 1024
NT = (((1,), (1,)), ((), ()))


def mul(left, right):
    return jnp.dot(left, right, preferred_element_type=F32)


def mul_nt(left, right):
    return lax.dot_general(left, right, NT, preferred_element_type=F32)


def params(count):
    return pltpu.CompilerParams(
        dimension_semantics=("arbitrary",) * count, vmem_limit_bytes=VMEM_BYTES
    )


def whole(shape):
    return pl.BlockSpec(shape, lambda *ids: (0,) * len(shape), pipeline_mode=pl.Buffered(1))


def shaped(shape, dtype):
    return jax.ShapeDtypeStruct(shape, dtype)


def qkv_part(weight_ref, part):
    shards, unused_rows, width = weight_ref.shape
    rows = width // shards
    return weight_ref[:, part * rows : (part + 1) * rows, :].reshape(width, width)


def project_kernel(x_ref, weight_ref, gain_ref, shift_ref, bias_ref, qkv_ref, normed_ref):
    width = x_ref.shape[-1]
    normed, unused_unit, unused_scale = normalize(
        x_ref[0].astype(F32), gain_ref[...], shift_ref[...]
    )
    low = normed.astype(BF16)
    normed_ref[0] = low
    for part in range(3):
        value = mul(low, qkv_part(weight_ref, part)) + bias_ref[part : part + 1]
        if part == 0:
            value = value * HEAD_DIM ** (-0.5)
        qkv_ref[part, 0] = value.astype(BF16)


def project(units, weight, gain, shift, bias):
    count, size, width = units.shape
    return pl.pallas_call(
        project_kernel,
        grid=(count,),
        in_specs=[
            pl.BlockSpec((1, size, width), lambda u: (u, 0, 0)),
            whole(weight.shape),
            whole(gain.shape),
            whole(shift.shape),
            whole(bias.shape),
        ],
        out_specs=[
            pl.BlockSpec((3, 1, size, width), lambda u: (0, u, 0, 0)),
            pl.BlockSpec((1, size, width), lambda u: (u, 0, 0)),
        ],
        out_shape=[shaped((3, count, size, width), BF16), shaped((count, size, width), BF16)],
        compiler_params=params(1),
        cost_estimate=pl.CostEstimate(
            flops=2 * count * size * width * 3 * width,
            bytes_accessed=count * size * width * 10 + 6 * width * width,
            transcendentals=0,
        ),
        name="project",
    )(units, weight, gain, shift, bias)


def head_mask(size):
    return lax.broadcasted_iota(jnp.int32, (size, 2 * HEAD_DIM), 1) // HEAD_DIM


def mix_kernel(q_ref, ka_ref, va_ref, kb_ref, vb_ref, o_ref, lse_ref):
    query = q_ref[0, 0]
    lanes = head_mask(query.shape[0])
    keys = (ka_ref[0, 0], kb_ref[0, 0])
    turned = (va_ref[0, 0].T, vb_ref[0, 0].T)
    outs = []
    for head in range(2):
        one = jnp.where(lanes == head, query, jnp.zeros_like(query))
        scores = [mul_nt(key, one) for key in keys]
        top = jnp.maximum(
            jnp.max(scores[0], 0, keepdims=True), jnp.max(scores[1], 0, keepdims=True)
        )
        grown = [jnp.exp(score - top) for score in scores]
        total = jnp.sum(grown[0], 0, keepdims=True) + jnp.sum(grown[1], 0, keepdims=True)
        span = slice(head * HEAD_DIM, (head + 1) * HEAD_DIM)
        mixed = mul(turned[0][span], grown[0].astype(BF16)) + mul(
            turned[1][span], grown[1].astype(BF16)
        )
        outs.append(mixed / total)
        lse_ref[0, 0, head : head + 1] = top + jnp.log(total)
    o_ref[0] = jnp.concatenate(outs, 0).T.astype(BF16)


def attend_specs(size, key_places):
    lanes = 2 * HEAD_DIM
    specs = []
    for source, part, unit in key_places:
        specs.append(
            pl.BlockSpec((1, 1, size, lanes), lambda h, u, part=part, unit=unit: (part, unit, 0, h))
        )
    return specs


def mix(qkv, first_unit, unit_count, key_places):
    size, width = qkv.shape[2:]
    lanes = 2 * HEAD_DIM
    pairs = width // lanes
    flops = 4 * unit_count * size * 2 * size * width
    return pl.pallas_call(
        mix_kernel,
        grid=(pairs, unit_count),
        in_specs=[pl.BlockSpec((1, 1, size, lanes), lambda h, u: (0, first_unit + u, 0, h))]
        + attend_specs(size, key_places),
        out_specs=[
            pl.BlockSpec((1, size, lanes), lambda h, u: (u, 0, h)),
            pl.BlockSpec((1, 1, 8, size), lambda h, u: (u, h, 0, 0)),
        ],
        out_shape=[
            shaped((unit_count, size, width), BF16),
            shaped((unit_count, pairs, 8, size), F32),
        ],
        compiler_params=params(2),
        cost_estimate=pl.CostEstimate(
            flops=4 * flops,
            bytes_accessed=unit_count * size * width * 8,
            transcendentals=unit_count * size * 2 * size * width // HEAD_DIM,
        ),
        name="mix",
    )(qkv, *[place[0] for place in key_places])


def mix_back_kernel(
    unit_count,
    q_ref,
    ka_ref,
    va_ref,
    kb_ref,
    vb_ref,
    o_ref,
    do_ref,
    lse_ref,
    dq_ref,
    dkv_ref,
    dk_acc,
    dv_acc,
):
    step = pl.program_id(1)
    query = q_ref[0, 0]
    grad = do_ref[0]
    size = query.shape[0]
    lanes = head_mask(size)
    keys = (ka_ref[0, 0], kb_ref[0, 0])
    values = (va_ref[0, 0], vb_ref[0, 0])
    turned = (keys[0].T, keys[1].T)
    product = grad.astype(F32) * o_ref[0].astype(F32)
    high = product.astype(BF16)
    rest = (product - high.astype(F32)).astype(BF16)
    chosen = (
        lax.broadcasted_iota(jnp.int32, (8, 2 * HEAD_DIM), 1) // HEAD_DIM
        == lax.broadcasted_iota(jnp.int32, (8, 2 * HEAD_DIM), 0)
    ).astype(BF16)
    inner = mul_nt(chosen, high) + mul_nt(chosen, rest)
    dks, dvs, dqs = [None, None], [None, None], []
    for head in range(2):
        mine = lanes == head
        one_query = jnp.where(mine, query, jnp.zeros_like(query))
        one_grad = jnp.where(mine, grad, jnp.zeros_like(grad))
        span = slice(head * HEAD_DIM, (head + 1) * HEAD_DIM)
        log_row = lse_ref[0, 0, head : head + 1]
        inner_row = inner[head : head + 1]
        dq = None
        for side in range(2):
            probs = jnp.exp(mul_nt(keys[side], one_query) - log_row)
            dv = mul(probs.astype(BF16), one_grad)
            change = mul_nt(values[side], one_grad)
            scored = (probs * (change - inner_row)).astype(BF16)
            dk = mul(scored, one_query)
            part = mul(turned[side][span], scored)
            dq = part if dq is None else dq + part
            dks[side] = dk if head == 0 else dks[side] + dk
            dvs[side] = dv if head == 0 else dvs[side] + dv
        dqs.append(dq)
    dq_ref[0] = (jnp.concatenate(dqs, 0).T * HEAD_DIM ** (-0.5)).astype(BF16)
    if unit_count == 1:
        for side in range(2):
            dkv_ref[0, side] = dks[side].astype(BF16)
            dkv_ref[1, side] = dvs[side].astype(BF16)
        return

    @pl.when(step == 0)
    def first():
        for side in range(2):
            dk_acc[side] = dks[side]
            dv_acc[side] = dvs[side]

    @pl.when(jnp.logical_and(step > 0, step < unit_count - 1))
    def between():
        for side in range(2):
            dk_acc[side] += dks[side]
            dv_acc[side] += dvs[side]

    @pl.when(step == unit_count - 1)
    def last():
        for side in range(2):
            dkv_ref[0, side] = (dk_acc[side] + dks[side]).astype(BF16)
            dkv_ref[1, side] = (dv_acc[side] + dvs[side]).astype(BF16)


def mix_back(qkv, first_unit, unit_count, key_places, mixed, grad_mixed, lse, out_units):
    size, width = qkv.shape[2:]
    lanes = 2 * HEAD_DIM
    pairs = width // lanes
    flops = 10 * unit_count * size * 2 * size * width
    return pl.pallas_call(
        functools.partial(mix_back_kernel, unit_count),
        grid=(pairs, unit_count),
        in_specs=[pl.BlockSpec((1, 1, size, lanes), lambda h, u: (0, first_unit + u, 0, h))]
        + attend_specs(size, key_places)
        + [
            pl.BlockSpec((1, size, lanes), lambda h, u: (u, 0, h)),
            pl.BlockSpec((1, size, lanes), lambda h, u: (first_unit + u, 0, h)),
            pl.BlockSpec((1, 1, 8, size), lambda h, u: (u, h, 0, 0)),
        ],
        out_specs=[
            pl.BlockSpec((1, size, lanes), lambda h, u: (u, 0, h)),
            pl.BlockSpec((2, 2, size, lanes), lambda h, u: (0, 0, 0, h)),
        ],
        out_shape=[
            shaped((out_units, size, width), BF16),
            shaped((2, max(out_units, 2), size, width), BF16),
        ],
        scratch_shapes=[pltpu.VMEM((2, size, lanes), F32)] * 2,
        compiler_params=params(2),
        cost_estimate=pl.CostEstimate(
            flops=4 * flops,
            bytes_accessed=unit_count * size * width * 16,
            transcendentals=unit_count * size * 2 * size * width // HEAD_DIM,
        ),
        name="mix_back",
    )(qkv, *[place[0] for place in key_places], mixed, grad_mixed, lse)


def gelu_pair(value):
    size = jnp.abs(value) * 0.5**0.5
    turn = 1.0 / (1.0 + 0.3275911 * size)
    bell = jnp.exp(-size * size)
    series = turn * (
        0.254829592
        + turn * (-0.284496736 + turn * (1.421413741 + turn * (-1.453152027 + turn * 1.061405429)))
    )
    tail = 0.5 * series * bell
    share = jnp.where(value >= 0, 1.0 - tail, tail)
    return value * share, share + value * (bell * 0.3989422804014327)


def column(values):
    return jnp.sum(values, 0, keepdims=True)


def feed_kernel(
    x_ref,
    oa_ref,
    ob_ref,
    cot_ref,
    weights_ref,
    gain_ref,
    shift_ref,
    proj_bias_ref,
    hidden_bias_ref,
    output_bias_ref,
    out_ref,
    dx_ref,
    do_ref,
    normed_ref,
    act_ref,
    dh_ref,
    dp_ref,
    sums_ref,
    hidden_sum_ref,
):
    step = pl.program_id(0)
    width = x_ref.shape[-1]
    shards, shard_rows = weights_ref.shape[:2]
    rows = width // shards
    parts = hidden_bias_ref.shape[-1] // width
    per_part = shards // parts

    @pl.when(step == 0)
    def clear():
        sums_ref[...] = jnp.zeros_like(sums_ref)
        hidden_sum_ref[...] = jnp.zeros_like(hidden_sum_ref)

    proj = weights_ref[:, 2 * parts * rows :, :].reshape(width, width)
    mixed = jnp.where(step < 2, oa_ref[0], ob_ref[0])
    middle = x_ref[0].astype(F32) + (mul(mixed, proj) + proj_bias_ref[...])
    gain = gain_ref[...]
    normed, unit, scale = normalize(middle, gain, shift_ref[...])
    low = normed.astype(BF16)
    normed_ref[0] = low
    upstream = cot_ref[0]
    branch = middle + output_bias_ref[...]
    grad_normed = None
    for part in range(parts):
        first = weights_ref[:, part * rows : (part + 1) * rows, :].reshape(width, width)
        second = weights_ref[
            part * per_part : (part + 1) * per_part, parts * rows : 2 * parts * rows, :
        ].reshape(width, width)
        span = slice(part * width, (part + 1) * width)
        hidden = mul(low, first) + hidden_bias_ref[:, span]
        active, slope = gelu_pair(hidden)
        active = active.astype(BF16)
        act_ref[0, :, span] = active
        branch = branch + mul(active, second)
        grad_hidden = mul_nt(upstream, second) * slope
        low_grad = grad_hidden.astype(BF16)
        dh_ref[0, :, span] = low_grad
        hidden_sum_ref[0:1, span] += column(low_grad.astype(F32))
        back = mul_nt(low_grad, first)
        grad_normed = back if grad_normed is None else grad_normed + back
    out_ref[0] = branch.astype(BF16)
    wide = upstream.astype(F32)
    grad_middle = wide + norm_back(grad_normed, unit, scale, gain)
    dx_ref[0] = grad_middle
    low_middle = grad_middle.astype(BF16)
    dp_ref[0] = low_middle
    do_ref[0] = mul_nt(low_middle, proj).astype(BF16)
    sums_ref[0:1] += column(wide)
    sums_ref[1:2] += column(grad_normed * unit)
    sums_ref[2:3] += column(grad_normed)
    sums_ref[3:4] += column(low_middle.astype(F32))


def feed(units, mixed_pair, mixed_one, cotangent, weights, gain, shift, proj_bias, hidden_bias, output_bias):
    count, size, width = units.shape
    inner = hidden_bias.shape[-1]

    def rows(columns):
        return pl.BlockSpec((1, size, columns), lambda u: (u, 0, 0))

    return pl.pallas_call(
        feed_kernel,
        grid=(count,),
        in_specs=[
            rows(width),
            pl.BlockSpec((1, size, width), lambda u: (jnp.minimum(u, 1), 0, 0)),
            pl.BlockSpec((1, size, width), lambda u: (0, 0, 0), pipeline_mode=pl.Buffered(1)),
            rows(width),
            whole(weights.shape),
            whole(gain.shape),
            whole(shift.shape),
            whole(proj_bias.shape),
            whole(hidden_bias.shape),
            whole(output_bias.shape),
        ],
        out_specs=[
            rows(width),
            rows(width),
            rows(width),
            rows(width),
            rows(inner),
            rows(inner),
            rows(width),
            pl.BlockSpec((8, width), lambda u: (0, 0)),
            pl.BlockSpec((8, inner), lambda u: (0, 0)),
        ],
        out_shape=[
            shaped((count, size, width), BF16),
            shaped((count, size, width), F32),
            shaped((count, size, width), BF16),
            shaped((count, size, width), BF16),
            shaped((count, size, inner), BF16),
            shaped((count, size, inner), BF16),
            shaped((count, size, width), BF16),
            shaped((8, width), F32),
            shaped((8, inner), F32),
        ],
        compiler_params=params(1),
        cost_estimate=pl.CostEstimate(
            flops=2 * count * size * width * (4 * inner + 2 * width),
            bytes_accessed=count * size * (width * 20 + inner * 4),
            transcendentals=2 * count * size * inner,
        ),
        name="feed",
    )(units, mixed_pair, mixed_one, cotangent, weights, gain, shift, proj_bias, hidden_bias, output_bias)


def weight_kernel(parts, shards, normed_ref, dh_ref, act_ref, dz_ref, o_ref, dp_ref, out_ref, left, right):
    step = pl.program_id(0)
    width = normed_ref.shape[-1]
    rows = width // shards
    per_part = shards // parts

    @pl.when(step == 0)
    def turn():
        left[...] = normed_ref[...].T
        right[...] = dz_ref[...].T

    for part in range(parts):

        @pl.when(step == part)
        def first():
            grad = mul(left[...], dh_ref[...])
            out_ref[:, part * rows : (part + 1) * rows, :] = grad.astype(BF16).reshape(
                shards, rows, width
            )

        @pl.when(step == parts + part)
        def second():
            grad = mul(right[...], act_ref[...]).T
            out_ref[
                part * per_part : (part + 1) * per_part, parts * rows : 2 * parts * rows, :
            ] = grad.astype(BF16).reshape(per_part, parts * rows, width)

    @pl.when(step == 2 * parts)
    def third():
        grad = mul(o_ref[...].T, dp_ref[...])
        out_ref[:, 2 * parts * rows :, :] = grad.astype(BF16).reshape(shards, rows, width)


def weight_grads(normed, grad_hidden, active, grad_branch, mixed, grad_attended, shards):
    count, width = normed.shape
    inner = active.shape[-1]
    parts = inner // width
    shard_rows = (2 * parts + 1) * (width // shards)
    return pl.pallas_call(
        functools.partial(weight_kernel, parts, shards),
        grid=(2 * parts + 1,),
        in_specs=[
            whole(normed.shape),
            pl.BlockSpec((count, width), lambda s: (0, jnp.minimum(s, parts - 1))),
            pl.BlockSpec((count, width), lambda s: (0, jnp.clip(s - parts, 0, parts - 1))),
            whole(grad_branch.shape),
            whole(mixed.shape),
            whole(grad_attended.shape),
        ],
        out_specs=whole((shards, shard_rows, width)),
        out_shape=shaped((shards, shard_rows, width), BF16),
        scratch_shapes=[pltpu.VMEM((width, count), BF16)] * 2,
        compiler_params=params(1),
        cost_estimate=pl.CostEstimate(
            flops=2 * count * width * (2 * inner + width),
            bytes_accessed=count * (8 * width + 4 * inner),
            transcendentals=0,
        ),
        name="weight_grads",
    )(normed, grad_hidden, active, grad_branch, mixed, grad_attended)


def qkv_weight_kernel(normed_ref, dq_ref, dkv_ref, out_ref, left):
    step = pl.program_id(0)

    @pl.when(step == 0)
    def query_part():
        left[...] = normed_ref[...].T
        out_ref[...] = mul(left[...], dq_ref[...]).astype(BF16)

    @pl.when(step > 0)
    def other_part():
        out_ref[...] = mul(left[...], dkv_ref[0]).astype(BF16)


def qkv_weight_grad(normed, dq, dkv):
    count, width = normed.shape
    return pl.pallas_call(
        qkv_weight_kernel,
        grid=(3,),
        in_specs=[
            whole(normed.shape),
            whole(dq.shape),
            pl.BlockSpec((1, count, width), lambda s: (jnp.maximum(s - 1, 0), 0, 0)),
        ],
        out_specs=pl.BlockSpec((width, width), lambda s: (0, s)),
        out_shape=shaped((width, 3 * width), BF16),
        scratch_shapes=[pltpu.VMEM((width, count), BF16)],
        compiler_params=params(1),
        cost_estimate=pl.CostEstimate(
            flops=6 * count * width * width,
            bytes_accessed=8 * count * width + 6 * width * width,
            transcendentals=0,
        ),
        name="qkv_weight_grad",
    )(normed, dq, dkv)


def input_kernel(x_ref, dx_ref, dq_ref, dkv_ref, weight_ref, gain_ref, shift_ref, out_ref, sums_ref):
    step = pl.program_id(0)
    width = x_ref.shape[-1]

    @pl.when(step == 0)
    def clear():
        sums_ref[...] = jnp.zeros_like(sums_ref)

    gain = gain_ref[...]
    unused, unit, scale = normalize(x_ref[0].astype(F32), gain, shift_ref[...])
    grad = mul_nt(dq_ref[0], qkv_part(weight_ref, 0))
    grad = grad + mul_nt(dkv_ref[0, 0], qkv_part(weight_ref, 1))
    grad = grad + mul_nt(dkv_ref[1, 0], qkv_part(weight_ref, 2))
    out_ref[0] = (dx_ref[0] + norm_back(grad, unit, scale, gain)).astype(BF16)
    sums_ref[0:1] += column(grad * unit)
    sums_ref[1:2] += column(grad)
    sums_ref[2:3] += column(dq_ref[0].astype(F32))
    sums_ref[3:4] += column(dkv_ref[1, 0].astype(F32))


def input_grads(units, grad_middle, dq, dkv, weight, gain, shift):
    count, size, width = units.shape
    rows = pl.BlockSpec((1, size, width), lambda u: (u, 0, 0))
    return pl.pallas_call(
        input_kernel,
        grid=(count,),
        in_specs=[
            rows,
            rows,
            rows,
            pl.BlockSpec((2, 1, size, width), lambda u: (0, u, 0, 0)),
            whole(weight.shape),
            whole(gain.shape),
            whole(shift.shape),
        ],
        out_specs=[rows, pl.BlockSpec((8, width), lambda u: (0, 0))],
        out_shape=[shaped((count, size, width), BF16), shaped((8, width), F32)],
        compiler_params=params(1),
        cost_estimate=pl.CostEstimate(
            flops=6 * count * size * width * width,
            bytes_accessed=count * size * width * 14,
            transcendentals=0,
        ),
        name="input_grads",
    )(units, grad_middle, dq, dkv, weight, gain, shift)


def tree_sum(value, axes):
    for axis, size in axes:
        reach = 1
        while reach < size:
            pairs = [(index, index ^ reach) for index in range(size)]
            value = value + lax.ppermute(value, axis, pairs)
            reach *= 2
    return value


def fast_body(fsdp_size, *args):
    (
        inputs,
        cotangent,
        first_gain,
        first_shift,
        qkv_weight,
        query_bias,
        value_bias,
        proj_weight,
        proj_bias,
        second_gain,
        second_shift,
        hidden_weight,
        hidden_bias,
        output_weight,
        output_bias,
    ) = args
    images, size, width = inputs.shape
    row_count = images * size
    side = lax.axis_index("seq")
    place = lax.axis_index("fsdp")
    swap_sides = [(0, 1), (1, 0)]
    swap_cores = [(index, index ^ 1) for index in range(fsdp_size)]
    swap_middle = []
    for index in range(0, fsdp_size, 2):
        swap_middle += [(fsdp_size + index, index + 1), (index + 1, fsdp_size + index)]
    stays = side == place % 2

    def middle_swap(value):
        return jnp.where(stays, value, lax.ppermute(value, ("seq", "fsdp"), swap_middle))

    def gather_units(values):
        got = lax.ppermute(
            lax.dynamic_index_in_dim(values, 2 * (1 - side), 0, False), "seq", swap_sides
        )
        kept = lax.dynamic_index_in_dim(values, 2 * side, 0, False)
        return jnp.stack([kept, got, middle_swap(values[1])])

    def return_units(values):
        got = lax.ppermute(values[1], "seq", swap_sides)
        centre = middle_swap(values[2])
        first = jnp.where(side == 0, values[0], got)
        last = jnp.where(side == 0, got, values[0])
        return jnp.stack([first, centre, last])

    parts = hidden_weight.shape[1] // width
    rows = hidden_weight.shape[0]
    small = [
        first_gain,
        first_shift,
        query_bias,
        value_bias,
        proj_bias,
        second_gain,
        second_shift,
        output_bias,
        hidden_bias,
    ]
    sizes = [value.shape[0] for value in small]
    starts = [sum(sizes[:index]) for index in range(len(sizes))]
    line = jnp.concatenate(small + [jnp.zeros((width - sum(sizes),), BF16)])
    head = jnp.concatenate(
        [qkv_weight[:, part * width : (part + 1) * width] for part in range(3)]
        + [jnp.broadcast_to(line[None], (16, width))],
        0,
    )
    full_head = lax.all_gather(head, "fsdp", axis=0)
    pack = jnp.concatenate(
        [hidden_weight[:, part * width : (part + 1) * width] for part in range(parts)]
        + [output_weight, proj_weight],
        0,
    )
    full_pack = lax.all_gather(pack, "fsdp", axis=0)
    all_small = full_head[:, 3 * rows].astype(F32)
    (
        gain_one,
        shift_one,
        bias_query,
        bias_value,
        bias_proj,
        gain_two,
        shift_two,
        bias_output,
        bias_hidden,
    ) = [
        all_small[:, start : start + count].reshape(1, fsdp_size * count)
        for start, count in zip(starts, sizes)
    ]

    units = gather_units(inputs)
    bias_qkv = jnp.concatenate([bias_query, jnp.zeros_like(bias_query), bias_value], 0)
    qkv, normed = project(units, full_head, gain_one, shift_one, bias_qkv)
    other = lax.ppermute(qkv[1:, 2], "fsdp", swap_cores)[:, None]
    places_pair = [(qkv, 1, 0), (qkv, 2, 0), (qkv, 1, 1), (qkv, 2, 1)]
    places_one = [(qkv, 1, 2), (qkv, 2, 2), (other, 0, 0), (other, 1, 0)]
    mixed_pair, lse_pair = mix(qkv, 0, 2, places_pair)
    mixed_one, lse_one = mix(qkv, 2, 1, places_one)
    grads_up = gather_units(cotangent)
    (
        out,
        grad_middle,
        grad_mixed,
        normed_two,
        active,
        grad_hidden,
        grad_attended,
        sums_two,
        sum_hidden,
    ) = feed(
        units,
        mixed_pair,
        mixed_one,
        grads_up,
        full_pack,
        gain_two,
        shift_two,
        bias_proj,
        bias_hidden,
        bias_output,
    )
    block_out = return_units(out)

    def flat(value):
        return value.reshape(row_count, value.shape[-1])

    grad_pack = weight_grads(
        flat(normed_two),
        flat(grad_hidden),
        flat(active),
        flat(grads_up),
        flat(jnp.concatenate([mixed_pair, mixed_one], 0)),
        flat(grad_attended),
        fsdp_size,
    )
    grad_mixed, grad_pack = lax.optimization_barrier((grad_mixed, grad_pack))
    shard_pack = lax.psum_scatter(grad_pack, "fsdp", scatter_dimension=0, tiled=False)
    dq_one, dkv_one = mix_back(qkv, 2, 1, places_one, mixed_one, grad_mixed, lse_one, 1)
    dkv_got = lax.ppermute(dkv_one[:, 1], "fsdp", swap_cores)
    dq, dkv = mix_back(qkv, 0, 2, places_pair, mixed_pair, grad_mixed, lse_pair, images)
    dq = dq.at[2].set(dq_one[0])
    dkv = dkv.at[:, 2].set((dkv_one[:, 0].astype(F32) + dkv_got.astype(F32)).astype(BF16))
    grad_qkv = qkv_weight_grad(flat(normed), flat(dq), dkv.reshape(2, row_count, width))
    shard_qkv = lax.psum_scatter(grad_qkv, "fsdp", scatter_dimension=0, tiled=True)
    grad_units, sums_one = input_grads(units, grad_middle, dq, dkv, full_head, gain_one, shift_one)
    input_grad = return_units(grad_units)

    small_grads = [
        sums_one[0],
        sums_one[1],
        sums_one[2],
        sums_one[3],
        sums_two[3],
        sums_two[1],
        sums_two[2],
        sums_two[0],
        sum_hidden[0],
    ]
    packed = jnp.concatenate([value.reshape(fsdp_size, -1) for value in small_grads], 1)
    packed = tree_sum(packed, [("fsdp", fsdp_size), ("seq", 2)])
    mine = lax.dynamic_index_in_dim(packed, place, 0, False)
    (
        grad_gain_one,
        grad_shift_one,
        grad_query_b,
        grad_value_b,
        grad_proj_b,
        grad_gain_two,
        grad_shift_two,
        grad_output_b,
        grad_hidden_b,
    ) = [mine[start : start + count] for start, count in zip(starts, sizes)]

    def both(value):
        return value.astype(F32) + lax.ppermute(value, "seq", swap_sides).astype(F32)

    shard_pack = both(shard_pack)
    grad_hidden_w = jnp.concatenate(
        [shard_pack[part * rows : (part + 1) * rows] for part in range(parts)], 1
    )
    grad_output_w = shard_pack[parts * rows : 2 * parts * rows]
    grad_proj_w = shard_pack[2 * parts * rows :]
    grad_qkv_w = both(shard_qkv)
    return (
        block_out,
        input_grad,
        grad_gain_one,
        grad_shift_one,
        grad_qkv_w,
        grad_query_b,
        grad_value_b,
        grad_proj_w,
        grad_proj_b,
        grad_gain_two,
        grad_shift_two,
        grad_hidden_w,
        grad_hidden_b,
        grad_output_w,
        grad_output_b,
    )


def pick_body(seq_size, fsdp_size):
    def body(*args):
        images, size, width = args[0].shape
        inner = args[11].shape[1]
        fits = (
            seq_size == 2
            and images == 3
            and fsdp_size > 1
            and fsdp_size & (fsdp_size - 1) == 0
            and size % 8 == 0
            and width % 128 == 0
            and (width // fsdp_size) % 16 == 0
            and inner % width == 0
            and 8 * (width // fsdp_size) + inner // fsdp_size <= width
            and fsdp_size % (inner // width) == 0
        )
        if fits:
            return fast_body(fsdp_size, *args)
        return general_body(*args)

    return body


def solution(mesh):
    shape = mesh.shape
    body = pick_body(shape["seq"], shape["fsdp"])
    return jax.shard_map(
        body,
        mesh=mesh,
        in_specs=(
            P("fsdp", "seq", None),
            P("fsdp", "seq", None),
            P("fsdp"),
            P("fsdp"),
            P("fsdp", None),
            P("fsdp"),
            P("fsdp"),
            P("fsdp", None),
            P("fsdp"),
            P("fsdp"),
            P("fsdp"),
            P("fsdp", None),
            P("fsdp"),
            P("fsdp", None),
            P("fsdp"),
        ),
        out_specs=(
            P("fsdp", "seq", None),
            P("fsdp", "seq", None),
            P("fsdp"),
            P("fsdp"),
            P("fsdp", None),
            P("fsdp"),
            P("fsdp"),
            P("fsdp", None),
            P("fsdp"),
            P("fsdp"),
            P("fsdp"),
            P("fsdp", None),
            P("fsdp"),
            P("fsdp", None),
            P("fsdp"),
        ),
        check_vma=False,
    )
```

```python
import functools

import jax
import jax.numpy as jnp
from jax import lax
from jax.experimental import pallas as pl
from jax.experimental.pallas import tpu as pltpu
from jax.sharding import PartitionSpec as P

HEADS = 12
HEAD_DIM = 64


EPS = 1e-06


def normalize(rows, gain, shift):
    row_mean = jnp.mean(rows, -1, keepdims=True)
    centred = rows - row_mean
    variance = jnp.mean(centred * centred, -1, keepdims=True)
    scaled = lax.rsqrt(variance + EPS)
    unit = centred * scaled
    return (unit * gain + shift, unit, scaled)


def norm_back(grad_out, unit, scaled, gain):
    grad_unit = grad_out * gain
    first_mean = jnp.mean(grad_unit, -1, keepdims=True)
    second_mean = jnp.mean(grad_unit * unit, -1, keepdims=True)
    return scaled * (grad_unit - first_mean - unit * second_mean)


def gelu_exact(value):
    return jax.nn.gelu(value, approximate=False)


def column_sum(values):
    return jnp.sum(values.astype(jnp.float32), 0)


def general_body(
    inputs,
    cotangent,
    first_gain,
    first_shift,
    qkv_weight,
    query_bias,
    value_bias,
    proj_weight,
    proj_bias,
    second_gain,
    second_shift,
    hidden_weight,
    hidden_bias,
    output_weight,
    output_bias,
):
    images, local_len, width = inputs.shape
    row_count = images * local_len
    factor = HEAD_DIM ** (-0.5)
    (
        gain_one,
        shift_one,
        full_qkv,
        bias_query,
        bias_value,
        full_proj,
        bias_proj,
        gain_two,
        shift_two,
        full_hidden,
        bias_hidden,
        full_output,
        bias_output,
    ) = (
        lax.all_gather(first_gain, "fsdp", axis=0, tiled=True),
        lax.all_gather(first_shift, "fsdp", axis=0, tiled=True),
        lax.all_gather(qkv_weight, "fsdp", axis=0, tiled=True),
        lax.all_gather(query_bias, "fsdp", axis=0, tiled=True),
        lax.all_gather(value_bias, "fsdp", axis=0, tiled=True),
        lax.all_gather(proj_weight, "fsdp", axis=0, tiled=True),
        lax.all_gather(proj_bias, "fsdp", axis=0, tiled=True),
        lax.all_gather(second_gain, "fsdp", axis=0, tiled=True),
        lax.all_gather(second_shift, "fsdp", axis=0, tiled=True),
        lax.all_gather(hidden_weight, "fsdp", axis=0, tiled=True),
        lax.all_gather(hidden_bias, "fsdp", axis=0, tiled=True),
        lax.all_gather(output_weight, "fsdp", axis=0, tiled=True),
        lax.all_gather(output_bias, "fsdp", axis=0, tiled=True),
    )
    rows = inputs.reshape(row_count, width).astype(jnp.float32)
    normed, unit_one, scale_one = normalize(
        rows, gain_one.astype(jnp.float32), shift_one.astype(jnp.float32)
    )
    normed_low = normed.astype(jnp.bfloat16)
    projected = jnp.dot(normed_low, full_qkv, preferred_element_type=jnp.float32)
    head_shape = (images, local_len, HEADS, HEAD_DIM)
    query = (
        (projected[:, :width] + bias_query.astype(jnp.float32))
        .astype(jnp.bfloat16)
        .reshape(head_shape)
    )
    keys = projected[:, width : 2 * width].astype(jnp.bfloat16).reshape(head_shape)
    values = (
        (projected[:, 2 * width :] + bias_value.astype(jnp.float32))
        .astype(jnp.bfloat16)
        .reshape(head_shape)
    )
    all_keys, all_values = (
        lax.all_gather(keys, "seq", axis=1, tiled=True),
        lax.all_gather(values, "seq", axis=1, tiled=True),
    )

    def attend(items):
        query_one, key_one, value_one = items
        scores = (
            jnp.einsum("qhd,khd->hqk", query_one, key_one, preferred_element_type=jnp.float32)
            * factor
        )
        row_max = jnp.max(scores, -1, keepdims=True)
        exponent = jnp.exp(scores - row_max)
        row_total = jnp.sum(exponent, -1, keepdims=True)
        weights = (exponent / row_total).astype(jnp.bfloat16)
        mixed_one = jnp.einsum(
            "hqk,khd->qhd", weights, value_one, preferred_element_type=jnp.float32
        )
        return (mixed_one, (row_max + jnp.log(row_total))[..., 0])

    mixed, log_total = lax.map(attend, (query, all_keys, all_values))
    mixed_low = mixed.reshape(row_count, width).astype(jnp.bfloat16)
    attended = jnp.dot(mixed_low, full_proj, preferred_element_type=jnp.float32) + bias_proj.astype(
        jnp.float32
    )
    middle = rows + attended
    normed_two, unit_two, scale_two = normalize(
        middle, gain_two.astype(jnp.float32), shift_two.astype(jnp.float32)
    )
    normed_two_low = normed_two.astype(jnp.bfloat16)
    hidden_pre = jnp.dot(
        normed_two_low, full_hidden, preferred_element_type=jnp.float32
    ) + bias_hidden.astype(jnp.float32)
    activated = gelu_exact(hidden_pre).astype(jnp.bfloat16)
    branch = jnp.dot(
        activated, full_output, preferred_element_type=jnp.float32
    ) + bias_output.astype(jnp.float32)
    block_out = (middle + branch).astype(jnp.bfloat16).reshape(inputs.shape)
    upstream = cotangent.reshape(row_count, width).astype(jnp.float32)
    grad_branch = upstream.astype(jnp.bfloat16)
    grad_output_w = jnp.einsum(
        "rf,rd->fd", activated, grad_branch, preferred_element_type=jnp.float32
    )
    grad_output_b = column_sum(grad_branch)
    grad_act = jnp.einsum("rd,fd->rf", grad_branch, full_output, preferred_element_type=jnp.float32)
    unused_value, pull_gelu = jax.vjp(gelu_exact, hidden_pre)
    grad_hidden = pull_gelu(grad_act)[0].astype(jnp.bfloat16)
    grad_hidden_w = jnp.einsum(
        "rd,rf->df", normed_two_low, grad_hidden, preferred_element_type=jnp.float32
    )
    grad_hidden_b = column_sum(grad_hidden)
    grad_normed_two = jnp.einsum(
        "rf,df->rd", grad_hidden, full_hidden, preferred_element_type=jnp.float32
    )
    grad_gain_two = jnp.sum(grad_normed_two * unit_two, 0)
    grad_shift_two = jnp.sum(grad_normed_two, 0)
    grad_middle = upstream + norm_back(
        grad_normed_two, unit_two, scale_two, gain_two.astype(jnp.float32)
    )
    grad_attended = grad_middle.astype(jnp.bfloat16)
    grad_proj_w = jnp.einsum(
        "re,rd->ed", mixed_low, grad_attended, preferred_element_type=jnp.float32
    )
    grad_proj_b = column_sum(grad_attended)
    grad_mixed = jnp.einsum(
        "rd,ed->re", grad_attended, full_proj, preferred_element_type=jnp.float32
    )
    grad_mixed = grad_mixed.astype(jnp.bfloat16).reshape(head_shape)

    def attend_back(items):
        query_one, key_one, value_one, grad_one, log_one = items
        scores = (
            jnp.einsum("qhd,khd->hqk", query_one, key_one, preferred_element_type=jnp.float32)
            * factor
        )
        probs = jnp.exp(scores - log_one[..., None])
        grad_value = jnp.einsum(
            "hqk,qhd->khd", probs.astype(jnp.bfloat16), grad_one, preferred_element_type=jnp.float32
        )
        grad_probs = jnp.einsum(
            "qhd,khd->hqk", grad_one, value_one, preferred_element_type=jnp.float32
        )
        inner = jnp.sum(probs * grad_probs, -1, keepdims=True)
        grad_scores = (probs * (grad_probs - inner)).astype(jnp.bfloat16)
        grad_query = (
            jnp.einsum("hqk,khd->qhd", grad_scores, key_one, preferred_element_type=jnp.float32)
            * factor
        )
        grad_key = (
            jnp.einsum("hqk,qhd->khd", grad_scores, query_one, preferred_element_type=jnp.float32)
            * factor
        )
        return (grad_query, grad_key, grad_value)

    grad_query, grad_keys, grad_values = lax.map(
        attend_back, (query, all_keys, all_values, grad_mixed, log_total)
    )
    grad_keys, grad_values = (
        lax.psum_scatter(
            grad_keys.astype(jnp.bfloat16), "seq", scatter_dimension=1, tiled=True
        ).astype(jnp.float32),
        lax.psum_scatter(
            grad_values.astype(jnp.bfloat16), "seq", scatter_dimension=1, tiled=True
        ).astype(jnp.float32),
    )
    grad_qkv = jnp.concatenate(
        [
            grad_query.reshape(row_count, width),
            grad_keys.reshape(row_count, width),
            grad_values.reshape(row_count, width),
        ],
        -1,
    ).astype(jnp.bfloat16)
    grad_qkv_w = jnp.einsum("rd,rc->dc", normed_low, grad_qkv, preferred_element_type=jnp.float32)
    grad_query_b = column_sum(grad_qkv[:, :width])
    grad_value_b = column_sum(grad_qkv[:, 2 * width :])
    grad_normed = jnp.einsum("rc,dc->rd", grad_qkv, full_qkv, preferred_element_type=jnp.float32)
    grad_gain_one = jnp.sum(grad_normed * unit_one, 0)
    grad_shift_one = jnp.sum(grad_normed, 0)
    grad_rows = grad_middle + norm_back(
        grad_normed, unit_one, scale_one, gain_one.astype(jnp.float32)
    )
    input_grad = grad_rows.astype(jnp.bfloat16).reshape(inputs.shape)
    parts = (
        lax.psum_scatter(
            grad_gain_one.astype(jnp.bfloat16), "fsdp", scatter_dimension=0, tiled=True
        ).astype(jnp.float32),
        lax.psum_scatter(
            grad_shift_one.astype(jnp.bfloat16), "fsdp", scatter_dimension=0, tiled=True
        ).astype(jnp.float32),
        lax.psum_scatter(
            grad_qkv_w.astype(jnp.bfloat16), "fsdp", scatter_dimension=0, tiled=True
        ).astype(jnp.float32),
        lax.psum_scatter(
            grad_query_b.astype(jnp.bfloat16), "fsdp", scatter_dimension=0, tiled=True
        ).astype(jnp.float32),
        lax.psum_scatter(
            grad_value_b.astype(jnp.bfloat16), "fsdp", scatter_dimension=0, tiled=True
        ).astype(jnp.float32),
        lax.psum_scatter(
            grad_proj_w.astype(jnp.bfloat16), "fsdp", scatter_dimension=0, tiled=True
        ).astype(jnp.float32),
        lax.psum_scatter(
            grad_proj_b.astype(jnp.bfloat16), "fsdp", scatter_dimension=0, tiled=True
        ).astype(jnp.float32),
        lax.psum_scatter(
            grad_gain_two.astype(jnp.bfloat16), "fsdp", scatter_dimension=0, tiled=True
        ).astype(jnp.float32),
        lax.psum_scatter(
            grad_shift_two.astype(jnp.bfloat16), "fsdp", scatter_dimension=0, tiled=True
        ).astype(jnp.float32),
        lax.psum_scatter(
            grad_hidden_w.astype(jnp.bfloat16), "fsdp", scatter_dimension=0, tiled=True
        ).astype(jnp.float32),
        lax.psum_scatter(
            grad_hidden_b.astype(jnp.bfloat16), "fsdp", scatter_dimension=0, tiled=True
        ).astype(jnp.float32),
        lax.psum_scatter(
            grad_output_w.astype(jnp.bfloat16), "fsdp", scatter_dimension=0, tiled=True
        ).astype(jnp.float32),
        lax.psum_scatter(
            grad_output_b.astype(jnp.bfloat16), "fsdp", scatter_dimension=0, tiled=True
        ).astype(jnp.float32),
    )
    shares = (
        lax.psum(parts[0].astype(jnp.bfloat16), "seq").astype(jnp.float32),
        lax.psum(parts[1].astype(jnp.bfloat16), "seq").astype(jnp.float32),
        lax.psum(parts[2].astype(jnp.bfloat16), "seq").astype(jnp.float32),
        lax.psum(parts[3].astype(jnp.bfloat16), "seq").astype(jnp.float32),
        lax.psum(parts[4].astype(jnp.bfloat16), "seq").astype(jnp.float32),
        lax.psum(parts[5].astype(jnp.bfloat16), "seq").astype(jnp.float32),
        lax.psum(parts[6].astype(jnp.bfloat16), "seq").astype(jnp.float32),
        lax.psum(parts[7].astype(jnp.bfloat16), "seq").astype(jnp.float32),
        lax.psum(parts[8].astype(jnp.bfloat16), "seq").astype(jnp.float32),
        lax.psum(parts[9].astype(jnp.bfloat16), "seq").astype(jnp.float32),
        lax.psum(parts[10].astype(jnp.bfloat16), "seq").astype(jnp.float32),
        lax.psum(parts[11].astype(jnp.bfloat16), "seq").astype(jnp.float32),
        lax.psum(parts[12].astype(jnp.bfloat16), "seq").astype(jnp.float32),
    )
    return (
        block_out,
        input_grad,
        shares[0],
        shares[1],
        shares[2],
        shares[3],
        shares[4],
        shares[5],
        shares[6],
        shares[7],
        shares[8],
        shares[9],
        shares[10],
        shares[11],
        shares[12],
    )


F32 = jnp.float32
BF16 = jnp.bfloat16
VMEM_BYTES = 60 * 1024 * 1024
NT = (((1,), (1,)), ((), ()))
LATE = pl.CostEstimate(flops=1000, bytes_accessed=1000, transcendentals=0)


def mul(left, right):
    return jnp.dot(left, right, preferred_element_type=F32)


def mul_nt(left, right):
    return lax.dot_general(left, right, NT, preferred_element_type=F32)


def params(count):
    return pltpu.CompilerParams(
        dimension_semantics=("arbitrary",) * count, vmem_limit_bytes=VMEM_BYTES
    )


def whole(shape):
    return pl.BlockSpec(shape, lambda *ids: (0,) * len(shape), pipeline_mode=pl.Buffered(1))


def shaped(shape, dtype):
    return jax.ShapeDtypeStruct(shape, dtype)


def qkv_part(weight_ref, part):
    width = weight_ref.shape[-1] // 3
    rows = width // weight_ref.shape[0]
    return weight_ref[:, :rows, part * width : (part + 1) * width].reshape(width, width)


def project_kernel(x_ref, weight_ref, gain_ref, shift_ref, bias_ref, qkv_ref, normed_ref):
    width = x_ref.shape[-1]
    normed, unused_unit, unused_scale = normalize(
        x_ref[0].astype(F32), gain_ref[...], shift_ref[...]
    )
    low = normed.astype(BF16)
    normed_ref[0] = low
    for part in range(3):
        value = mul(low, qkv_part(weight_ref, part)) + bias_ref[part : part + 1]
        if part == 0:
            value = value * HEAD_DIM ** (-0.5)
        qkv_ref[part, 0] = value.astype(BF16)


def project(units, weight, gain, shift, bias):
    count, size, width = units.shape
    return pl.pallas_call(
        project_kernel,
        grid=(count,),
        in_specs=[
            pl.BlockSpec((1, size, width), lambda u: (u, 0, 0)),
            whole(weight.shape),
            whole(gain.shape),
            whole(shift.shape),
            whole(bias.shape),
        ],
        out_specs=[
            pl.BlockSpec((3, 1, size, width), lambda u: (0, u, 0, 0)),
            pl.BlockSpec((1, size, width), lambda u: (u, 0, 0)),
        ],
        out_shape=[shaped((3, count, size, width), BF16), shaped((count, size, width), BF16)],
        compiler_params=params(1),
        cost_estimate=pl.CostEstimate(
            flops=2 * count * size * width * 3 * width,
            bytes_accessed=count * size * width * 10 + 6 * width * width,
            transcendentals=0,
        ),
        name="project",
    )(units, weight, gain, shift, bias)


def head_mask(size):
    return lax.broadcasted_iota(jnp.int32, (size, 2 * HEAD_DIM), 1) // HEAD_DIM


def mix_kernel(q_ref, ka_ref, va_ref, kb_ref, vb_ref, *rest):
    o_ref, lse_ref = rest[-2:]
    query = q_ref[0, 0]
    lanes = head_mask(query.shape[0])
    keys = (ka_ref[0, 0], kb_ref[0, 0])
    turned = (va_ref[0, 0].T, vb_ref[0, 0].T)
    outs = []
    for head in range(2):
        one = jnp.where(lanes == head, query, jnp.zeros_like(query))
        scores = [mul_nt(key, one) for key in keys]
        top = jnp.maximum(
            jnp.max(scores[0], 0, keepdims=True), jnp.max(scores[1], 0, keepdims=True)
        )
        grown = [jnp.exp(score - top) for score in scores]
        total = jnp.sum(grown[0], 0, keepdims=True) + jnp.sum(grown[1], 0, keepdims=True)
        span = slice(head * HEAD_DIM, (head + 1) * HEAD_DIM)
        mixed = mul(turned[0][span], grown[0].astype(BF16)) + mul(
            turned[1][span], grown[1].astype(BF16)
        )
        outs.append(mixed / total)
        lse_ref[0, 0, head : head + 1] = top + jnp.log(total)
    o_ref[0] = jnp.concatenate(outs, 0).T.astype(BF16)


def attend_specs(size, key_places):
    lanes = 2 * HEAD_DIM
    specs = []
    for source, part, unit in key_places:
        specs.append(
            pl.BlockSpec((1, 1, size, lanes), lambda h, u, part=part, unit=unit: (part, unit, 0, h))
        )
    return specs


def mix(qkv, first_unit, unit_count, key_places, earlier=None):
    size, width = qkv.shape[2:]
    lanes = 2 * HEAD_DIM
    pairs = width // lanes
    flops = 4 * unit_count * size * 2 * size * width
    return pl.pallas_call(
        mix_kernel,
        grid=(pairs, unit_count),
        in_specs=[pl.BlockSpec((1, 1, size, lanes), lambda h, u: (0, first_unit + u, 0, h))]
        + attend_specs(size, key_places)
        + [pl.BlockSpec(memory_space=pl.ANY)] * (earlier is not None),
        out_specs=[
            pl.BlockSpec((1, size, lanes), lambda h, u: (first_unit + u, 0, h)),
            pl.BlockSpec((1, 1, 8, size), lambda h, u: (u, h, 0, 0)),
        ],
        out_shape=[
            shaped((qkv.shape[1], size, width), BF16),
            shaped((unit_count, pairs, 8, size), F32),
        ],
        input_output_aliases={} if earlier is None else {5: 0},
        compiler_params=params(2),
        cost_estimate=pl.CostEstimate(
            flops=4 * flops,
            bytes_accessed=unit_count * size * width * 8,
            transcendentals=unit_count * size * 2 * size * width // HEAD_DIM,
        ),
        name="mix",
    )(qkv, *[place[0] for place in key_places], *([] if earlier is None else [earlier]))


def mix_back_kernel(
    unit_count,
    q_ref,
    ka_ref,
    va_ref,
    kb_ref,
    vb_ref,
    o_ref,
    do_ref,
    lse_ref,
    *rest,
):
    dq_ref, dkv_ref, dk_acc, dv_acc = rest[-4:]
    step = pl.program_id(1)
    query = q_ref[0, 0]
    grad = do_ref[0]
    size = query.shape[0]
    lanes = head_mask(size)
    keys = (ka_ref[0, 0], kb_ref[0, 0])
    values = (va_ref[0, 0], vb_ref[0, 0])
    turned = (keys[0].T, keys[1].T)
    product = grad.astype(F32) * o_ref[0].astype(F32)
    high = product.astype(BF16)
    rest = (product - high.astype(F32)).astype(BF16)
    chosen = (
        lax.broadcasted_iota(jnp.int32, (8, 2 * HEAD_DIM), 1) // HEAD_DIM
        == lax.broadcasted_iota(jnp.int32, (8, 2 * HEAD_DIM), 0)
    ).astype(BF16)
    inner = mul_nt(chosen, high) + mul_nt(chosen, rest)
    dks, dvs, dqs = [None, None], [None, None], []
    for head in range(2):
        mine = lanes == head
        one_query = jnp.where(mine, query, jnp.zeros_like(query))
        one_grad = jnp.where(mine, grad, jnp.zeros_like(grad))
        span = slice(head * HEAD_DIM, (head + 1) * HEAD_DIM)
        log_row = lse_ref[0, 0, head : head + 1]
        inner_row = inner[head : head + 1]
        dq = None
        for side in range(2):
            probs = jnp.exp(mul_nt(keys[side], one_query) - log_row)
            dv = mul(probs.astype(BF16), one_grad)
            change = mul_nt(values[side], one_grad)
            scored = (probs * (change - inner_row)).astype(BF16)
            dk = mul(scored, one_query)
            part = mul(turned[side][span], scored)
            dq = part if dq is None else dq + part
            dks[side] = dk if head == 0 else dks[side] + dk
            dvs[side] = dv if head == 0 else dvs[side] + dv
        dqs.append(dq)
    dq_ref[0] = (jnp.concatenate(dqs, 0).T * HEAD_DIM ** (-0.5)).astype(BF16)
    if unit_count == 1:
        for side in range(2):
            dkv_ref[0, side] = dks[side].astype(BF16)
            dkv_ref[1, side] = dvs[side].astype(BF16)
        return

    @pl.when(step == 0)
    def first():
        for side in range(2):
            dk_acc[side] = dks[side]
            dv_acc[side] = dvs[side]

    @pl.when(jnp.logical_and(step > 0, step < unit_count - 1))
    def between():
        for side in range(2):
            dk_acc[side] += dks[side]
            dv_acc[side] += dvs[side]

    @pl.when(step == unit_count - 1)
    def last():
        for side in range(2):
            dkv_ref[0, side] = (dk_acc[side] + dks[side]).astype(BF16)
            dkv_ref[1, side] = (dv_acc[side] + dvs[side]).astype(BF16)


def mix_back(qkv, first_unit, unit_count, key_places, mixed, grad_mixed, lse, earlier=None):
    size, width = qkv.shape[2:]
    lanes = 2 * HEAD_DIM
    pairs = width // lanes
    units = qkv.shape[1]
    return pl.pallas_call(
        functools.partial(mix_back_kernel, unit_count),
        grid=(pairs, unit_count),
        in_specs=[pl.BlockSpec((1, 1, size, lanes), lambda h, u: (0, first_unit + u, 0, h))]
        + attend_specs(size, key_places)
        + [
            pl.BlockSpec((1, size, lanes), lambda h, u: (first_unit + u, 0, h)),
            pl.BlockSpec((1, size, lanes), lambda h, u: (first_unit + u, 0, h)),
            pl.BlockSpec((1, 1, 8, size), lambda h, u: (u, h, 0, 0)),
        ]
        + [pl.BlockSpec(memory_space=pl.ANY)] * (earlier is not None),
        out_specs=[
            pl.BlockSpec((1, size, lanes), lambda h, u: (first_unit + u, 0, h)),
            pl.BlockSpec((2, 2, size, lanes), lambda h, u: (0, 0, 0, h)),
        ],
        out_shape=[
            shaped((units, size, width), BF16),
            shaped((2, 2 if earlier is None else units, size, width), BF16),
        ],
        input_output_aliases={} if earlier is None else {8: 0},
        scratch_shapes=[pltpu.VMEM((2, size, lanes), F32)] * 2,
        compiler_params=params(2),
        cost_estimate=LATE,
        name="mix_back",
    )(
        qkv,
        *[place[0] for place in key_places],
        mixed,
        grad_mixed,
        lse,
        *([] if earlier is None else [earlier]),
    )


def gelu_pair(value):
    size = jnp.abs(value) * 0.5**0.5
    turn = 1.0 / (1.0 + 0.3275911 * size)
    bell = jnp.exp(-size * size)
    series = turn * (
        0.254829592
        + turn * (-0.284496736 + turn * (1.421413741 + turn * (-1.453152027 + turn * 1.061405429)))
    )
    tail = 0.5 * series * bell
    share = jnp.where(value >= 0, 1.0 - tail, tail)
    return value * share, share + value * (bell * 0.3989422804014327)


def column(values):
    return jnp.sum(values, 0, keepdims=True)


def feed_kernel(
    x_ref,
    o_ref,
    cot_ref,
    weights_ref,
    gain_ref,
    shift_ref,
    proj_bias_ref,
    hidden_bias_ref,
    output_bias_ref,
    out_ref,
    dx_ref,
    do_ref,
    normed_ref,
    act_ref,
    dh_ref,
    dp_ref,
    sums_ref,
    hidden_sum_ref,
):
    step = pl.program_id(0)
    width = x_ref.shape[-1]
    shards, shard_rows = weights_ref.shape[:2]
    rows = width // shards
    parts = hidden_bias_ref.shape[-1] // width
    per_part = shards // parts

    @pl.when(step == 0)
    def clear():
        sums_ref[...] = jnp.zeros_like(sums_ref)
        hidden_sum_ref[...] = jnp.zeros_like(hidden_sum_ref)

    proj = weights_ref[:, 2 * parts * rows :, :].reshape(width, width)
    middle = x_ref[0].astype(F32) + (mul(o_ref[0], proj) + proj_bias_ref[...])
    gain = gain_ref[...]
    normed, unit, scale = normalize(middle, gain, shift_ref[...])
    low = normed.astype(BF16)
    normed_ref[0] = low
    upstream = cot_ref[0]
    branch = middle + output_bias_ref[...]
    grad_normed = None
    for part in range(parts):
        first = weights_ref[:, part * rows : (part + 1) * rows, :].reshape(width, width)
        second = weights_ref[
            part * per_part : (part + 1) * per_part, parts * rows : 2 * parts * rows, :
        ].reshape(width, width)
        span = slice(part * width, (part + 1) * width)
        hidden = mul(low, first) + hidden_bias_ref[:, span]
        active, slope = gelu_pair(hidden)
        active = active.astype(BF16)
        act_ref[0, :, span] = active
        branch = branch + mul(active, second)
        grad_hidden = mul_nt(upstream, second) * slope
        low_grad = grad_hidden.astype(BF16)
        dh_ref[0, :, span] = low_grad
        hidden_sum_ref[0:1, span] += column(low_grad.astype(F32))
        back = mul_nt(low_grad, first)
        grad_normed = back if grad_normed is None else grad_normed + back
    out_ref[0] = branch.astype(BF16)
    wide = upstream.astype(F32)
    grad_middle = wide + norm_back(grad_normed, unit, scale, gain)
    dx_ref[0] = grad_middle
    low_middle = grad_middle.astype(BF16)
    dp_ref[0] = low_middle
    do_ref[0] = mul_nt(low_middle, proj).astype(BF16)
    sums_ref[0:1] += column(wide)
    sums_ref[1:2] += column(grad_normed * unit)
    sums_ref[2:3] += column(grad_normed)
    sums_ref[3:4] += column(low_middle.astype(F32))


def feed(units, mixed, cotangent, weights, gain, shift, proj_bias, hidden_bias, output_bias):
    count, size, width = units.shape
    inner = hidden_bias.shape[-1]

    def rows(columns):
        return pl.BlockSpec((1, size, columns), lambda u: (u, 0, 0))

    return pl.pallas_call(
        feed_kernel,
        grid=(count,),
        in_specs=[
            rows(width),
            rows(width),
            rows(width),
            whole(weights.shape),
            whole(gain.shape),
            whole(shift.shape),
            whole(proj_bias.shape),
            whole(hidden_bias.shape),
            whole(output_bias.shape),
        ],
        out_specs=[
            rows(width),
            rows(width),
            rows(width),
            rows(width),
            rows(inner),
            rows(inner),
            rows(width),
            pl.BlockSpec((8, width), lambda u: (0, 0)),
            pl.BlockSpec((8, inner), lambda u: (0, 0)),
        ],
        out_shape=[
            shaped((count, size, width), BF16),
            shaped((count, size, width), F32),
            shaped((count, size, width), BF16),
            shaped((count, size, width), BF16),
            shaped((count, size, inner), BF16),
            shaped((count, size, inner), BF16),
            shaped((count, size, width), BF16),
            shaped((8, width), F32),
            shaped((8, inner), F32),
        ],
        compiler_params=params(1),
        cost_estimate=pl.CostEstimate(
            flops=2 * count * size * width * (4 * inner + 2 * width),
            bytes_accessed=count * size * (width * 20 + inner * 4),
            transcendentals=2 * count * size * inner,
        ),
        name="feed",
    )(units, mixed, cotangent, weights, gain, shift, proj_bias, hidden_bias, output_bias)


def weight_kernel(parts, shards, normed_ref, dh_ref, act_ref, dz_ref, o_ref, dp_ref, out_ref, left, right):
    step = pl.program_id(0)
    width = normed_ref.shape[-1]
    rows = width // shards
    per_part = shards // parts

    @pl.when(step == 0)
    def turn():
        left[...] = normed_ref[...].T
        right[...] = dz_ref[...].T

    for part in range(parts):

        @pl.when(step == part)
        def first():
            grad = mul(left[...], dh_ref[...])
            out_ref[:, part * rows : (part + 1) * rows, :] = grad.astype(BF16).reshape(
                shards, rows, width
            )

        @pl.when(step == parts + part)
        def second():
            grad = mul(right[...], act_ref[...]).T
            out_ref[
                part * per_part : (part + 1) * per_part, parts * rows : 2 * parts * rows, :
            ] = grad.astype(BF16).reshape(per_part, parts * rows, width)

    @pl.when(step == 2 * parts)
    def third():
        grad = mul(o_ref[...].T, dp_ref[...])
        out_ref[:, 2 * parts * rows :, :] = grad.astype(BF16).reshape(shards, rows, width)


def weight_grads(normed, grad_hidden, active, grad_branch, mixed, grad_attended, shards):
    count, width = normed.shape
    inner = active.shape[-1]
    parts = inner // width
    shard_rows = (2 * parts + 1) * (width // shards)
    return pl.pallas_call(
        functools.partial(weight_kernel, parts, shards),
        grid=(2 * parts + 1,),
        in_specs=[
            whole(normed.shape),
            pl.BlockSpec((count, width), lambda s: (0, jnp.minimum(s, parts - 1))),
            pl.BlockSpec((count, width), lambda s: (0, jnp.clip(s - parts, 0, parts - 1))),
            whole(grad_branch.shape),
            whole(mixed.shape),
            whole(grad_attended.shape),
        ],
        out_specs=whole((shards, shard_rows, width)),
        out_shape=shaped((shards, shard_rows, width), BF16),
        scratch_shapes=[pltpu.VMEM((width, count), BF16)] * 2,
        compiler_params=params(1),
        cost_estimate=pl.CostEstimate(
            flops=2 * count * width * (2 * inner + width),
            bytes_accessed=count * (8 * width + 4 * inner),
            transcendentals=0,
        ),
        name="weight_grads",
    )(normed, grad_hidden, active, grad_branch, mixed, grad_attended)


def halving_orders(shards):
    reaches = [1 << bit for bit in range(shards.bit_length() - 1)]
    return reaches, reaches[:1] + reaches[2:] + reaches[1:2]


def slot_of(shard, order):
    slot = 0
    for reach in order:
        slot = 2 * slot + (shard // reach) % 2
    return slot


def qkv_weight_kernel(shards, normed_ref, dq_ref, dkv_ref, low_ref, high_ref, left):
    step = pl.program_id(0)
    width = normed_ref.shape[-1]
    rows = width // shards
    half = width // 2
    low_order, high_order = halving_orders(shards)

    def keep(ref, order, start, grad):
        for shard in range(shards):
            ref[slot_of(shard, order), :, start : start + grad.shape[1]] = grad[
                shard * rows : (shard + 1) * rows
            ]

    @pl.when(step == 0)
    def query_part():
        left[...] = normed_ref[...].T
        keep(low_ref, low_order, 0, mul(left[...], dq_ref[...]).astype(BF16))

    @pl.when(step == 1)
    def key_part():
        grad = mul(left[...], dkv_ref[0]).astype(BF16)
        keep(low_ref, low_order, width, grad[:, :half])
        keep(high_ref, high_order, 0, grad[:, half:])

    @pl.when(step == 2)
    def value_part():
        keep(high_ref, high_order, half, mul(left[...], dkv_ref[0]).astype(BF16))


def qkv_weight_grad(normed, dq, dkv, shards):
    count, width = normed.shape
    half = (shards, width // shards, 3 * width // 2)
    return pl.pallas_call(
        functools.partial(qkv_weight_kernel, shards),
        grid=(3,),
        in_specs=[
            whole(normed.shape),
            whole(dq.shape),
            pl.BlockSpec((1, count, width), lambda s: (jnp.maximum(s - 1, 0), 0, 0)),
        ],
        out_specs=[whole(half), whole(half)],
        out_shape=[shaped(half, BF16), shaped(half, BF16)],
        scratch_shapes=[pltpu.VMEM((width, count), BF16)],
        compiler_params=params(1),
        cost_estimate=LATE,
        name="qkv_weight_grad",
    )(normed, dq, dkv)


def input_kernel(x_ref, dx_ref, dq_ref, dkv_ref, weight_ref, gain_ref, shift_ref, out_ref, sums_ref):
    step = pl.program_id(0)
    width = x_ref.shape[-1]

    @pl.when(step == 0)
    def clear():
        sums_ref[...] = jnp.zeros_like(sums_ref)

    gain = gain_ref[...]
    unused, unit, scale = normalize(x_ref[0].astype(F32), gain, shift_ref[...])
    grad = mul_nt(dq_ref[0], qkv_part(weight_ref, 0))
    grad = grad + mul_nt(dkv_ref[0, 0], qkv_part(weight_ref, 1))
    grad = grad + mul_nt(dkv_ref[1, 0], qkv_part(weight_ref, 2))
    out_ref[0] = (dx_ref[0] + norm_back(grad, unit, scale, gain)).astype(BF16)
    sums_ref[0:1] += column(grad * unit)
    sums_ref[1:2] += column(grad)
    sums_ref[2:3] += column(dq_ref[0].astype(F32))
    sums_ref[3:4] += column(dkv_ref[1, 0].astype(F32))


def input_grads(units, grad_middle, dq, dkv, weight, gain, shift):
    count, size, width = units.shape
    rows = pl.BlockSpec((1, size, width), lambda u: (u, 0, 0))
    return pl.pallas_call(
        input_kernel,
        grid=(count,),
        in_specs=[
            rows,
            rows,
            rows,
            pl.BlockSpec((2, 1, size, width), lambda u: (0, u, 0, 0)),
            whole(weight.shape),
            whole(gain.shape),
            whole(shift.shape),
        ],
        out_specs=[rows, pl.BlockSpec((8, width), lambda u: (0, 0))],
        out_shape=[shaped((count, size, width), BF16), shaped((8, width), F32)],
        compiler_params=params(1),
        cost_estimate=LATE,
        name="input_grads",
    )(units, grad_middle, dq, dkv, weight, gain, shift)


def tree_sum(value, axes):
    for axis, size in axes:
        reach = 1
        while reach < size:
            pairs = [(index, index ^ reach) for index in range(size)]
            value = value + lax.ppermute(value, axis, pairs)
            reach *= 2
    return value


def halving_sum(value, axis, size, place, order):
    for reach in order:
        pairs = [(index, index ^ reach) for index in range(size)]
        halves = value.reshape((2, value.shape[0] // 2) + value.shape[1:])
        bit = (place // reach) % 2
        got = lax.ppermute(lax.dynamic_index_in_dim(halves, 1 - bit, 0, False), axis, pairs)
        kept = lax.dynamic_index_in_dim(halves, bit, 0, False)
        value = (kept.astype(F32) + got.astype(F32)).astype(BF16)
    return value


def fast_body(fsdp_size, *args):
    (
        inputs,
        cotangent,
        first_gain,
        first_shift,
        qkv_weight,
        query_bias,
        value_bias,
        proj_weight,
        proj_bias,
        second_gain,
        second_shift,
        hidden_weight,
        hidden_bias,
        output_weight,
        output_bias,
    ) = args
    images, size, width = inputs.shape
    row_count = images * size
    side = lax.axis_index("seq")
    place = lax.axis_index("fsdp")
    swap_sides = [(0, 1), (1, 0)]
    swap_cores = [(index, index ^ 1) for index in range(fsdp_size)]
    swap_middle = []
    for index in range(0, fsdp_size, 2):
        swap_middle += [(fsdp_size + index, index + 1), (index + 1, fsdp_size + index)]
    stays = side == place % 2

    def middle_swap(value):
        return jnp.where(stays, value, lax.ppermute(value, ("seq", "fsdp"), swap_middle))

    def gather_units(values):
        got = lax.ppermute(
            lax.dynamic_index_in_dim(values, 2 * (1 - side), 0, False), "seq", swap_sides
        )
        kept = lax.dynamic_index_in_dim(values, 2 * side, 0, False)
        return jnp.stack([kept, got, middle_swap(values[1])])

    def return_units(values, after=None):
        got = lax.ppermute(values[1], "seq", swap_sides)
        centre = lax.ppermute(values[2], ("seq", "fsdp"), swap_middle)
        if after is not None:
            got, centre, after = lax.optimization_barrier((got, centre, after))
        centre = jnp.where(stays, values[2], centre)
        first = jnp.where(side == 0, values[0], got)
        last = jnp.where(side == 0, got, values[0])
        value = jnp.stack([first, centre, last])
        return value if after is None else (value, after)

    def both(value):
        return value.astype(F32) + lax.ppermute(value, "seq", swap_sides).astype(F32)

    parts = hidden_weight.shape[1] // width
    rows = hidden_weight.shape[0]
    small = [
        first_gain,
        first_shift,
        query_bias,
        value_bias,
        proj_bias,
        second_gain,
        second_shift,
        output_bias,
        hidden_bias,
    ]
    sizes = [value.shape[0] for value in small]
    starts = [sum(sizes[:index]) for index in range(len(sizes))]
    lines = [jnp.pad(value[None], ((0, 0), (0, 3 * width - value.shape[0]))) for value in small]
    lines.append(jnp.zeros((16 - len(small), 3 * width), BF16))
    full_head = lax.all_gather(jnp.concatenate([qkv_weight] + lines, 0), "fsdp", axis=0)
    units = gather_units(inputs)
    hidden_weight, output_weight, proj_weight, units = lax.optimization_barrier(
        (hidden_weight, output_weight, proj_weight, units)
    )
    pack = jnp.concatenate(
        [hidden_weight[:, part * width : (part + 1) * width] for part in range(parts)]
        + [output_weight, proj_weight],
        0,
    )
    full_pack = lax.all_gather(pack, "fsdp", axis=0)
    all_small = full_head[:, rows:].astype(F32)
    (
        gain_one,
        shift_one,
        bias_query,
        bias_value,
        bias_proj,
        gain_two,
        shift_two,
        bias_output,
        bias_hidden,
    ) = [
        all_small[:, index, :count].reshape(1, fsdp_size * count)
        for index, count in enumerate(sizes)
    ]

    bias_qkv = jnp.concatenate([bias_query, jnp.zeros_like(bias_query), bias_value], 0)
    qkv, normed = project(units, full_head, gain_one, shift_one, bias_qkv)
    to_other, cotangent = lax.optimization_barrier((qkv[1:, 2], cotangent))
    other = lax.ppermute(to_other, "fsdp", swap_cores)[:, None]
    grads_up = gather_units(cotangent)
    places_pair = [(qkv, 1, 0), (qkv, 2, 0), (qkv, 1, 1), (qkv, 2, 1)]
    places_one = [(qkv, 1, 2), (qkv, 2, 2), (other, 0, 0), (other, 1, 0)]
    mixed_pair, lse_pair = mix(qkv, 0, 2, places_pair)
    mixed, lse_one = mix(qkv, 2, 1, places_one, mixed_pair)
    (
        out,
        grad_middle,
        grad_mixed,
        normed_two,
        active,
        grad_hidden,
        grad_attended,
        sums_two,
        sum_hidden,
    ) = feed(
        units,
        mixed,
        grads_up,
        full_pack,
        gain_two,
        shift_two,
        bias_proj,
        bias_hidden,
        bias_output,
    )
    block_out = return_units(out)

    def flat(value):
        return value.reshape(row_count, value.shape[-1])

    grad_pack = weight_grads(
        flat(normed_two),
        flat(grad_hidden),
        flat(active),
        flat(grads_up),
        flat(mixed),
        flat(grad_attended),
        fsdp_size,
    )
    grad_mixed, grad_pack = lax.optimization_barrier((grad_mixed, grad_pack))
    shard_pack = lax.psum_scatter(grad_pack, "fsdp", scatter_dimension=0, tiled=False)
    dq_one, dkv_one = mix_back(qkv, 2, 1, places_one, mixed, grad_mixed, lse_one)
    dkv_got = lax.ppermute(dkv_one[:, 1], "fsdp", swap_cores)
    dq, dkv = mix_back(qkv, 0, 2, places_pair, mixed, grad_mixed, lse_pair, dq_one)
    dkv = dkv.at[:, 2].set((dkv_one[:, 0].astype(F32) + dkv_got.astype(F32)).astype(BF16))
    sides = qkv_weight_grad(flat(normed), flat(dq), dkv.reshape(2, row_count, width), fsdp_size)
    orders = halving_orders(fsdp_size)
    sides = [
        halving_sum(value, "fsdp", fsdp_size, place, order[:1])
        for value, order in zip(sides, orders)
    ]
    sides, shard_pack, dq, dkv = lax.optimization_barrier((sides, shard_pack, dq, dkv))
    shard_pack = both(shard_pack)
    sides = [
        halving_sum(value, "fsdp", fsdp_size, place, order[1:2])
        for value, order in zip(sides, orders)
    ]
    grad_units, sums_one = input_grads(units, grad_middle, dq, dkv, full_head, gain_one, shift_one)
    sides, grad_units, sums_one = lax.optimization_barrier((sides, grad_units, sums_one))
    shard_sides = [
        halving_sum(value, "fsdp", fsdp_size, place, order[2:])[0]
        for value, order in zip(sides, orders)
    ]
    input_grad, shard_sides = return_units(grad_units, shard_sides)

    small_grads = [
        sums_one[0],
        sums_one[1],
        sums_one[2],
        sums_one[3],
        sums_two[3],
        sums_two[1],
        sums_two[2],
        sums_two[0],
        sum_hidden[0],
    ]
    packed = jnp.concatenate([value.reshape(fsdp_size, -1) for value in small_grads], 1)
    packed = tree_sum(packed, [("seq", 2), ("fsdp", fsdp_size)])
    mine = lax.dynamic_index_in_dim(packed, place, 0, False)
    (
        grad_gain_one,
        grad_shift_one,
        grad_query_b,
        grad_value_b,
        grad_proj_b,
        grad_gain_two,
        grad_shift_two,
        grad_output_b,
        grad_hidden_b,
    ) = [mine[start : start + count] for start, count in zip(starts, sizes)]

    grad_hidden_w = jnp.concatenate(
        [shard_pack[part * rows : (part + 1) * rows] for part in range(parts)], 1
    )
    grad_output_w = shard_pack[parts * rows : 2 * parts * rows]
    grad_proj_w = shard_pack[2 * parts * rows :]
    grad_qkv_w = jnp.concatenate([both(value) for value in shard_sides], 1)
    return (
        block_out,
        input_grad,
        grad_gain_one,
        grad_shift_one,
        grad_qkv_w,
        grad_query_b,
        grad_value_b,
        grad_proj_w,
        grad_proj_b,
        grad_gain_two,
        grad_shift_two,
        grad_hidden_w,
        grad_hidden_b,
        grad_output_w,
        grad_output_b,
    )


def pick_body(seq_size, fsdp_size):
    def body(*args):
        images, size, width = args[0].shape
        inner = args[11].shape[1]
        fits = (
            seq_size == 2
            and images == 3
            and fsdp_size > 1
            and fsdp_size & (fsdp_size - 1) == 0
            and size % 8 == 0
            and width % 128 == 0
            and (width // fsdp_size) % 16 == 0
            and inner % width == 0
            and fsdp_size % (inner // width) == 0
        )
        if fits:
            return fast_body(fsdp_size, *args)
        return general_body(*args)

    return body


def solution(mesh):
    shape = mesh.shape
    body = pick_body(shape["seq"], shape["fsdp"])
    return jax.shard_map(
        body,
        mesh=mesh,
        in_specs=(
            P("fsdp", "seq", None),
            P("fsdp", "seq", None),
            P("fsdp"),
            P("fsdp"),
            P("fsdp", None),
            P("fsdp"),
            P("fsdp"),
            P("fsdp", None),
            P("fsdp"),
            P("fsdp"),
            P("fsdp"),
            P("fsdp", None),
            P("fsdp"),
            P("fsdp", None),
            P("fsdp"),
        ),
        out_specs=(
            P("fsdp", "seq", None),
            P("fsdp", "seq", None),
            P("fsdp"),
            P("fsdp"),
            P("fsdp", None),
            P("fsdp"),
            P("fsdp"),
            P("fsdp", None),
            P("fsdp"),
            P("fsdp"),
            P("fsdp"),
            P("fsdp", None),
            P("fsdp"),
            P("fsdp", None),
            P("fsdp"),
        ),
        check_vma=False,
    )
```

```python
import functools

import jax
import jax.numpy as jnp
from jax import lax
from jax.experimental import pallas as pl
from jax.experimental.pallas import tpu as pltpu
from jax.sharding import PartitionSpec as P

HEADS = 12
HEAD_DIM = 64


EPS = 1e-06


def normalize(rows, gain, shift):
    row_mean = jnp.mean(rows, -1, keepdims=True)
    centred = rows - row_mean
    variance = jnp.mean(centred * centred, -1, keepdims=True)
    scaled = lax.rsqrt(variance + EPS)
    unit = centred * scaled
    return (unit * gain + shift, unit, scaled)


def norm_back(grad_out, unit, scaled, gain):
    grad_unit = grad_out * gain
    first_mean = jnp.mean(grad_unit, -1, keepdims=True)
    second_mean = jnp.mean(grad_unit * unit, -1, keepdims=True)
    return scaled * (grad_unit - first_mean - unit * second_mean)


def gelu_exact(value):
    return jax.nn.gelu(value, approximate=False)


def column_sum(values):
    return jnp.sum(values.astype(jnp.float32), 0)


def general_body(
    inputs,
    cotangent,
    first_gain,
    first_shift,
    qkv_weight,
    query_bias,
    value_bias,
    proj_weight,
    proj_bias,
    second_gain,
    second_shift,
    hidden_weight,
    hidden_bias,
    output_weight,
    output_bias,
):
    images, local_len, width = inputs.shape
    row_count = images * local_len
    factor = HEAD_DIM ** (-0.5)
    (
        gain_one,
        shift_one,
        full_qkv,
        bias_query,
        bias_value,
        full_proj,
        bias_proj,
        gain_two,
        shift_two,
        full_hidden,
        bias_hidden,
        full_output,
        bias_output,
    ) = (
        lax.all_gather(first_gain, "fsdp", axis=0, tiled=True),
        lax.all_gather(first_shift, "fsdp", axis=0, tiled=True),
        lax.all_gather(qkv_weight, "fsdp", axis=0, tiled=True),
        lax.all_gather(query_bias, "fsdp", axis=0, tiled=True),
        lax.all_gather(value_bias, "fsdp", axis=0, tiled=True),
        lax.all_gather(proj_weight, "fsdp", axis=0, tiled=True),
        lax.all_gather(proj_bias, "fsdp", axis=0, tiled=True),
        lax.all_gather(second_gain, "fsdp", axis=0, tiled=True),
        lax.all_gather(second_shift, "fsdp", axis=0, tiled=True),
        lax.all_gather(hidden_weight, "fsdp", axis=0, tiled=True),
        lax.all_gather(hidden_bias, "fsdp", axis=0, tiled=True),
        lax.all_gather(output_weight, "fsdp", axis=0, tiled=True),
        lax.all_gather(output_bias, "fsdp", axis=0, tiled=True),
    )
    rows = inputs.reshape(row_count, width).astype(jnp.float32)
    normed, unit_one, scale_one = normalize(
        rows, gain_one.astype(jnp.float32), shift_one.astype(jnp.float32)
    )
    normed_low = normed.astype(jnp.bfloat16)
    projected = jnp.dot(normed_low, full_qkv, preferred_element_type=jnp.float32)
    head_shape = (images, local_len, HEADS, HEAD_DIM)
    query = (
        (projected[:, :width] + bias_query.astype(jnp.float32))
        .astype(jnp.bfloat16)
        .reshape(head_shape)
    )
    keys = projected[:, width : 2 * width].astype(jnp.bfloat16).reshape(head_shape)
    values = (
        (projected[:, 2 * width :] + bias_value.astype(jnp.float32))
        .astype(jnp.bfloat16)
        .reshape(head_shape)
    )
    all_keys, all_values = (
        lax.all_gather(keys, "seq", axis=1, tiled=True),
        lax.all_gather(values, "seq", axis=1, tiled=True),
    )

    def attend(items):
        query_one, key_one, value_one = items
        scores = (
            jnp.einsum("qhd,khd->hqk", query_one, key_one, preferred_element_type=jnp.float32)
            * factor
        )
        row_max = jnp.max(scores, -1, keepdims=True)
        exponent = jnp.exp(scores - row_max)
        row_total = jnp.sum(exponent, -1, keepdims=True)
        weights = (exponent / row_total).astype(jnp.bfloat16)
        mixed_one = jnp.einsum(
            "hqk,khd->qhd", weights, value_one, preferred_element_type=jnp.float32
        )
        return (mixed_one, (row_max + jnp.log(row_total))[..., 0])

    mixed, log_total = lax.map(attend, (query, all_keys, all_values))
    mixed_low = mixed.reshape(row_count, width).astype(jnp.bfloat16)
    attended = jnp.dot(mixed_low, full_proj, preferred_element_type=jnp.float32) + bias_proj.astype(
        jnp.float32
    )
    middle = rows + attended
    normed_two, unit_two, scale_two = normalize(
        middle, gain_two.astype(jnp.float32), shift_two.astype(jnp.float32)
    )
    normed_two_low = normed_two.astype(jnp.bfloat16)
    hidden_pre = jnp.dot(
        normed_two_low, full_hidden, preferred_element_type=jnp.float32
    ) + bias_hidden.astype(jnp.float32)
    activated = gelu_exact(hidden_pre).astype(jnp.bfloat16)
    branch = jnp.dot(
        activated, full_output, preferred_element_type=jnp.float32
    ) + bias_output.astype(jnp.float32)
    block_out = (middle + branch).astype(jnp.bfloat16).reshape(inputs.shape)
    upstream = cotangent.reshape(row_count, width).astype(jnp.float32)
    grad_branch = upstream.astype(jnp.bfloat16)
    grad_output_w = jnp.einsum(
        "rf,rd->fd", activated, grad_branch, preferred_element_type=jnp.float32
    )
    grad_output_b = column_sum(grad_branch)
    grad_act = jnp.einsum("rd,fd->rf", grad_branch, full_output, preferred_element_type=jnp.float32)
    unused_value, pull_gelu = jax.vjp(gelu_exact, hidden_pre)
    grad_hidden = pull_gelu(grad_act)[0].astype(jnp.bfloat16)
    grad_hidden_w = jnp.einsum(
        "rd,rf->df", normed_two_low, grad_hidden, preferred_element_type=jnp.float32
    )
    grad_hidden_b = column_sum(grad_hidden)
    grad_normed_two = jnp.einsum(
        "rf,df->rd", grad_hidden, full_hidden, preferred_element_type=jnp.float32
    )
    grad_gain_two = jnp.sum(grad_normed_two * unit_two, 0)
    grad_shift_two = jnp.sum(grad_normed_two, 0)
    grad_middle = upstream + norm_back(
        grad_normed_two, unit_two, scale_two, gain_two.astype(jnp.float32)
    )
    grad_attended = grad_middle.astype(jnp.bfloat16)
    grad_proj_w = jnp.einsum(
        "re,rd->ed", mixed_low, grad_attended, preferred_element_type=jnp.float32
    )
    grad_proj_b = column_sum(grad_attended)
    grad_mixed = jnp.einsum(
        "rd,ed->re", grad_attended, full_proj, preferred_element_type=jnp.float32
    )
    grad_mixed = grad_mixed.astype(jnp.bfloat16).reshape(head_shape)

    def attend_back(items):
        query_one, key_one, value_one, grad_one, log_one = items
        scores = (
            jnp.einsum("qhd,khd->hqk", query_one, key_one, preferred_element_type=jnp.float32)
            * factor
        )
        probs = jnp.exp(scores - log_one[..., None])
        grad_value = jnp.einsum(
            "hqk,qhd->khd", probs.astype(jnp.bfloat16), grad_one, preferred_element_type=jnp.float32
        )
        grad_probs = jnp.einsum(
            "qhd,khd->hqk", grad_one, value_one, preferred_element_type=jnp.float32
        )
        inner = jnp.sum(probs * grad_probs, -1, keepdims=True)
        grad_scores = (probs * (grad_probs - inner)).astype(jnp.bfloat16)
        grad_query = (
            jnp.einsum("hqk,khd->qhd", grad_scores, key_one, preferred_element_type=jnp.float32)
            * factor
        )
        grad_key = (
            jnp.einsum("hqk,qhd->khd", grad_scores, query_one, preferred_element_type=jnp.float32)
            * factor
        )
        return (grad_query, grad_key, grad_value)

    grad_query, grad_keys, grad_values = lax.map(
        attend_back, (query, all_keys, all_values, grad_mixed, log_total)
    )
    grad_keys, grad_values = (
        lax.psum_scatter(
            grad_keys.astype(jnp.bfloat16), "seq", scatter_dimension=1, tiled=True
        ).astype(jnp.float32),
        lax.psum_scatter(
            grad_values.astype(jnp.bfloat16), "seq", scatter_dimension=1, tiled=True
        ).astype(jnp.float32),
    )
    grad_qkv = jnp.concatenate(
        [
            grad_query.reshape(row_count, width),
            grad_keys.reshape(row_count, width),
            grad_values.reshape(row_count, width),
        ],
        -1,
    ).astype(jnp.bfloat16)
    grad_qkv_w = jnp.einsum("rd,rc->dc", normed_low, grad_qkv, preferred_element_type=jnp.float32)
    grad_query_b = column_sum(grad_qkv[:, :width])
    grad_value_b = column_sum(grad_qkv[:, 2 * width :])
    grad_normed = jnp.einsum("rc,dc->rd", grad_qkv, full_qkv, preferred_element_type=jnp.float32)
    grad_gain_one = jnp.sum(grad_normed * unit_one, 0)
    grad_shift_one = jnp.sum(grad_normed, 0)
    grad_rows = grad_middle + norm_back(
        grad_normed, unit_one, scale_one, gain_one.astype(jnp.float32)
    )
    input_grad = grad_rows.astype(jnp.bfloat16).reshape(inputs.shape)
    parts = (
        lax.psum_scatter(
            grad_gain_one.astype(jnp.bfloat16), "fsdp", scatter_dimension=0, tiled=True
        ).astype(jnp.float32),
        lax.psum_scatter(
            grad_shift_one.astype(jnp.bfloat16), "fsdp", scatter_dimension=0, tiled=True
        ).astype(jnp.float32),
        lax.psum_scatter(
            grad_qkv_w.astype(jnp.bfloat16), "fsdp", scatter_dimension=0, tiled=True
        ).astype(jnp.float32),
        lax.psum_scatter(
            grad_query_b.astype(jnp.bfloat16), "fsdp", scatter_dimension=0, tiled=True
        ).astype(jnp.float32),
        lax.psum_scatter(
            grad_value_b.astype(jnp.bfloat16), "fsdp", scatter_dimension=0, tiled=True
        ).astype(jnp.float32),
        lax.psum_scatter(
            grad_proj_w.astype(jnp.bfloat16), "fsdp", scatter_dimension=0, tiled=True
        ).astype(jnp.float32),
        lax.psum_scatter(
            grad_proj_b.astype(jnp.bfloat16), "fsdp", scatter_dimension=0, tiled=True
        ).astype(jnp.float32),
        lax.psum_scatter(
            grad_gain_two.astype(jnp.bfloat16), "fsdp", scatter_dimension=0, tiled=True
        ).astype(jnp.float32),
        lax.psum_scatter(
            grad_shift_two.astype(jnp.bfloat16), "fsdp", scatter_dimension=0, tiled=True
        ).astype(jnp.float32),
        lax.psum_scatter(
            grad_hidden_w.astype(jnp.bfloat16), "fsdp", scatter_dimension=0, tiled=True
        ).astype(jnp.float32),
        lax.psum_scatter(
            grad_hidden_b.astype(jnp.bfloat16), "fsdp", scatter_dimension=0, tiled=True
        ).astype(jnp.float32),
        lax.psum_scatter(
            grad_output_w.astype(jnp.bfloat16), "fsdp", scatter_dimension=0, tiled=True
        ).astype(jnp.float32),
        lax.psum_scatter(
            grad_output_b.astype(jnp.bfloat16), "fsdp", scatter_dimension=0, tiled=True
        ).astype(jnp.float32),
    )
    shares = (
        lax.psum(parts[0].astype(jnp.bfloat16), "seq").astype(jnp.float32),
        lax.psum(parts[1].astype(jnp.bfloat16), "seq").astype(jnp.float32),
        lax.psum(parts[2].astype(jnp.bfloat16), "seq").astype(jnp.float32),
        lax.psum(parts[3].astype(jnp.bfloat16), "seq").astype(jnp.float32),
        lax.psum(parts[4].astype(jnp.bfloat16), "seq").astype(jnp.float32),
        lax.psum(parts[5].astype(jnp.bfloat16), "seq").astype(jnp.float32),
        lax.psum(parts[6].astype(jnp.bfloat16), "seq").astype(jnp.float32),
        lax.psum(parts[7].astype(jnp.bfloat16), "seq").astype(jnp.float32),
        lax.psum(parts[8].astype(jnp.bfloat16), "seq").astype(jnp.float32),
        lax.psum(parts[9].astype(jnp.bfloat16), "seq").astype(jnp.float32),
        lax.psum(parts[10].astype(jnp.bfloat16), "seq").astype(jnp.float32),
        lax.psum(parts[11].astype(jnp.bfloat16), "seq").astype(jnp.float32),
        lax.psum(parts[12].astype(jnp.bfloat16), "seq").astype(jnp.float32),
    )
    return (
        block_out,
        input_grad,
        shares[0],
        shares[1],
        shares[2],
        shares[3],
        shares[4],
        shares[5],
        shares[6],
        shares[7],
        shares[8],
        shares[9],
        shares[10],
        shares[11],
        shares[12],
    )


F32 = jnp.float32
BF16 = jnp.bfloat16
VMEM_BYTES = 60 * 1024 * 1024
NT = (((1,), (1,)), ((), ()))
LATE = pl.CostEstimate(flops=1000, bytes_accessed=1000, transcendentals=0)


def mul(left, right):
    return jnp.dot(left, right, preferred_element_type=F32)


def mul_nt(left, right):
    return lax.dot_general(left, right, NT, preferred_element_type=F32)


def params(count):
    return pltpu.CompilerParams(
        dimension_semantics=("arbitrary",) * count, vmem_limit_bytes=VMEM_BYTES
    )


def whole(shape):
    return pl.BlockSpec(shape, lambda *ids: (0,) * len(shape), pipeline_mode=pl.Buffered(1))


def shaped(shape, dtype):
    return jax.ShapeDtypeStruct(shape, dtype)


def qkv_part(weight_ref, part):
    width = weight_ref.shape[-1] // 3
    rows = width // weight_ref.shape[0]
    return weight_ref[:, :rows, part * width : (part + 1) * width].reshape(width, width)


def project_kernel(x_ref, weight_ref, vectors_ref, qkv_ref, normed_ref, other_ref):
    step = pl.program_id(0)
    normed, unused_unit, unused_scale = normalize(
        x_ref[0].astype(F32), vectors_ref[0:1], vectors_ref[1:2]
    )
    low = normed.astype(BF16)
    normed_ref[0] = low
    for part in range(3):
        value = mul(low, qkv_part(weight_ref, part))
        if part == 0:
            value = (value + vectors_ref[2:3]) * HEAD_DIM ** (-0.5)
        elif part == 2:
            value = value + vectors_ref[3:4]
        qkv_ref[part, 0] = value.astype(BF16)

    @pl.when(step == pl.num_programs(0) - 1)
    def last():
        other_ref[...] = qkv_ref[1:, 0]


def project(units, weight, vectors):
    count, size, width = units.shape
    return pl.pallas_call(
        project_kernel,
        grid=(count,),
        in_specs=[
            pl.BlockSpec((1, size, width), lambda u: (u, 0, 0)),
            whole(weight.shape),
            whole(vectors.shape),
        ],
        out_specs=[
            pl.BlockSpec((3, 1, size, width), lambda u: (0, u, 0, 0)),
            pl.BlockSpec((1, size, width), lambda u: (u, 0, 0)),
            whole((2, size, width)),
        ],
        out_shape=[
            shaped((3, count, size, width), BF16),
            shaped((count, size, width), BF16),
            shaped((2, size, width), BF16),
        ],
        compiler_params=params(1),
        cost_estimate=pl.CostEstimate(
            flops=2 * count * size * width * 3 * width,
            bytes_accessed=count * size * width * 10 + 6 * width * width,
            transcendentals=0,
        ),
        name="project",
    )(units, weight, vectors)


def head_kernel(weight_ref, hidden_ref, *rest):
    out_ref = rest[-1]
    short = jnp.concatenate([ref[...].astype(F32) for ref in rest[:-1]], 0)
    count, length = short.shape
    columns = weight_ref.shape[1]
    hidden = hidden_ref[...].astype(F32)
    wide = hidden.shape[1]
    hidden = jnp.concatenate([hidden, jnp.zeros((count - 1, wide), F32)], 0)
    lines = jnp.concatenate(
        [
            short,
            jnp.zeros((count, 128 - length), F32),
            hidden,
            jnp.zeros((count, columns - 128 - wide), F32),
        ],
        1,
    )
    out_ref[...] = jnp.concatenate([weight_ref[...].astype(F32), lines], 0).astype(BF16)


def head_pack(weight, hidden, short):
    rows, columns = weight.shape
    return pl.pallas_call(
        head_kernel,
        out_shape=shaped((rows + len(short), columns), BF16),
        name="head_pack",
    )(weight, hidden[None], *[value[None] for value in short])


def head_mask(size):
    return lax.broadcasted_iota(jnp.int32, (size, 2 * HEAD_DIM), 1) // HEAD_DIM


def mix_kernel(q_ref, ka_ref, va_ref, kb_ref, vb_ref, *rest):
    o_ref, lse_ref = rest[-2:]
    query = q_ref[0, 0]
    lanes = head_mask(query.shape[0])
    keys = (ka_ref[0, 0], kb_ref[0, 0])
    turned = (va_ref[0, 0].T, vb_ref[0, 0].T)
    outs = []
    for head in range(2):
        one = jnp.where(lanes == head, query, jnp.zeros_like(query))
        scores = [mul_nt(key, one) for key in keys]
        top = jnp.maximum(
            jnp.max(scores[0], 0, keepdims=True), jnp.max(scores[1], 0, keepdims=True)
        )
        grown = [jnp.exp(score - top) for score in scores]
        total = jnp.sum(grown[0], 0, keepdims=True) + jnp.sum(grown[1], 0, keepdims=True)
        span = slice(head * HEAD_DIM, (head + 1) * HEAD_DIM)
        mixed = mul(turned[0][span], grown[0].astype(BF16)) + mul(
            turned[1][span], grown[1].astype(BF16)
        )
        outs.append(mixed / total)
        lse_ref[0, 0, head : head + 1] = top + jnp.log(total)
    o_ref[0] = jnp.concatenate(outs, 0).T.astype(BF16)


def attend_specs(size, key_places):
    lanes = 2 * HEAD_DIM
    specs = []
    for source, part, unit in key_places:
        specs.append(
            pl.BlockSpec((1, 1, size, lanes), lambda h, u, part=part, unit=unit: (part, unit, 0, h))
        )
    return specs


def mix(qkv, first_unit, unit_count, key_places, earlier=None):
    size, width = qkv.shape[2:]
    lanes = 2 * HEAD_DIM
    pairs = width // lanes
    flops = 4 * unit_count * size * 2 * size * width
    return pl.pallas_call(
        mix_kernel,
        grid=(pairs, unit_count),
        in_specs=[pl.BlockSpec((1, 1, size, lanes), lambda h, u: (0, first_unit + u, 0, h))]
        + attend_specs(size, key_places)
        + [pl.BlockSpec(memory_space=pl.ANY)] * (earlier is not None),
        out_specs=[
            pl.BlockSpec((1, size, lanes), lambda h, u: (first_unit + u, 0, h)),
            pl.BlockSpec((1, 1, 8, size), lambda h, u: (u, h, 0, 0)),
        ],
        out_shape=[
            shaped((qkv.shape[1], size, width), BF16),
            shaped((unit_count, pairs, 8, size), F32),
        ],
        input_output_aliases={} if earlier is None else {5: 0},
        compiler_params=params(2),
        cost_estimate=pl.CostEstimate(
            flops=4 * flops,
            bytes_accessed=unit_count * size * width * 8,
            transcendentals=unit_count * size * 2 * size * width // HEAD_DIM,
        ),
        name="mix",
    )(qkv, *[place[0] for place in key_places], *([] if earlier is None else [earlier]))


def mix_back_kernel(
    unit_count,
    q_ref,
    ka_ref,
    va_ref,
    kb_ref,
    vb_ref,
    o_ref,
    do_ref,
    lse_ref,
    *rest,
):
    dq_ref, dkv_ref, last_ref, dk_acc, dv_acc = rest[-5:]
    step = pl.program_id(1)
    query = q_ref[0, 0]
    grad = do_ref[0]
    size = query.shape[0]
    lanes = head_mask(size)
    keys = (ka_ref[0, 0], kb_ref[0, 0])
    values = (va_ref[0, 0], vb_ref[0, 0])
    turned = (keys[0].T, keys[1].T)
    product = grad.astype(F32) * o_ref[0].astype(F32)
    high = product.astype(BF16)
    rest = (product - high.astype(F32)).astype(BF16)
    chosen = (
        lax.broadcasted_iota(jnp.int32, (8, 2 * HEAD_DIM), 1) // HEAD_DIM
        == lax.broadcasted_iota(jnp.int32, (8, 2 * HEAD_DIM), 0)
    ).astype(BF16)
    inner = mul_nt(chosen, high) + mul_nt(chosen, rest)
    dks, dvs, dqs = [None, None], [None, None], []
    for head in range(2):
        mine = lanes == head
        one_query = jnp.where(mine, query, jnp.zeros_like(query))
        one_grad = jnp.where(mine, grad, jnp.zeros_like(grad))
        span = slice(head * HEAD_DIM, (head + 1) * HEAD_DIM)
        log_row = lse_ref[0, 0, head : head + 1]
        inner_row = inner[head : head + 1]
        dq = None
        for side in range(2):
            probs = jnp.exp(mul_nt(keys[side], one_query) - log_row)
            dv = mul(probs.astype(BF16), one_grad)
            change = mul_nt(values[side], one_grad)
            scored = (probs * (change - inner_row)).astype(BF16)
            dk = mul(scored, one_query)
            part = mul(turned[side][span], scored)
            dq = part if dq is None else dq + part
            dks[side] = dk if head == 0 else dks[side] + dk
            dvs[side] = dv if head == 0 else dvs[side] + dv
        dqs.append(dq)
    dq_ref[0] = (jnp.concatenate(dqs, 0).T * HEAD_DIM ** (-0.5)).astype(BF16)
    if unit_count == 1:
        for side, ref in enumerate((dkv_ref, last_ref)):
            ref[0, 0] = dks[side].astype(BF16)
            ref[1, 0] = dvs[side].astype(BF16)
        return

    last_ref[...] = jnp.zeros_like(last_ref)

    @pl.when(step == 0)
    def first():
        for side in range(2):
            dk_acc[side] = dks[side]
            dv_acc[side] = dvs[side]

    @pl.when(jnp.logical_and(step > 0, step < unit_count - 1))
    def between():
        for side in range(2):
            dk_acc[side] += dks[side]
            dv_acc[side] += dvs[side]

    @pl.when(step == unit_count - 1)
    def last():
        for side in range(2):
            dkv_ref[0, side] = (dk_acc[side] + dks[side]).astype(BF16)
            dkv_ref[1, side] = (dv_acc[side] + dvs[side]).astype(BF16)


def mix_back(qkv, first_unit, unit_count, key_places, mixed, grad_mixed, lse, earlier=None):
    size, width = qkv.shape[2:]
    lanes = 2 * HEAD_DIM
    pairs = width // lanes
    units = qkv.shape[1]
    if unit_count == 1:
        key_outs = [pl.BlockSpec((2, 1, size, lanes), lambda h, u: (0, 0, 0, h))] * 2
        key_shapes = [shaped((2, 1, size, width), BF16)] * 2
    else:
        key_outs = [
            pl.BlockSpec((2, 2, size, lanes), lambda h, u: (0, 0, 0, h)),
            pl.BlockSpec((8, lanes), lambda h, u: (0, 0)),
        ]
        key_shapes = [shaped((2, units, size, width), BF16), shaped((8, lanes), F32)]
    return pl.pallas_call(
        functools.partial(mix_back_kernel, unit_count),
        grid=(pairs, unit_count),
        in_specs=[pl.BlockSpec((1, 1, size, lanes), lambda h, u: (0, first_unit + u, 0, h))]
        + attend_specs(size, key_places)
        + [
            pl.BlockSpec((1, size, lanes), lambda h, u: (first_unit + u, 0, h)),
            pl.BlockSpec((1, size, lanes), lambda h, u: (first_unit + u, 0, h)),
            pl.BlockSpec((1, 1, 8, size), lambda h, u: (u, h, 0, 0)),
        ]
        + [pl.BlockSpec(memory_space=pl.ANY)] * (earlier is not None),
        out_specs=[
            pl.BlockSpec((1, size, lanes), lambda h, u: (first_unit + u, 0, h)),
            *key_outs,
        ],
        out_shape=[shaped((units, size, width), BF16), *key_shapes],
        input_output_aliases={} if earlier is None else {8: 0},
        scratch_shapes=[pltpu.VMEM((2, size, lanes), F32)] * 2,
        compiler_params=params(2),
        cost_estimate=LATE,
        name="mix_back",
    )(
        qkv,
        *[place[0] for place in key_places],
        mixed,
        grad_mixed,
        lse,
        *([] if earlier is None else [earlier]),
    )


def gelu_pair(value):
    share = 0.5 + 0.5 * lax.erf(value * 0.5**0.5)
    density = jnp.exp(value * value * -0.5) * 0.3989422804014327
    return value * share, share + value * density


def column(values):
    return jnp.sum(values, 0, keepdims=True)


def feed_kernel(
    x_ref,
    o_ref,
    cot_ref,
    weights_ref,
    vectors_ref,
    hidden_bias_ref,
    out_ref,
    do_ref,
    normed_ref,
    act_ref,
    dh_ref,
    dp_ref,
    sums_ref,
    hidden_sum_ref,
):
    step = pl.program_id(0)
    width = x_ref.shape[-1]
    shards, shard_rows = weights_ref.shape[:2]
    rows = width // shards
    parts = hidden_bias_ref.shape[-1] // width
    per_part = shards // parts

    @pl.when(step == 0)
    def clear():
        sums_ref[...] = jnp.zeros_like(sums_ref)
        hidden_sum_ref[...] = jnp.zeros_like(hidden_sum_ref)

    proj = weights_ref[:, 2 * parts * rows :, :].reshape(width, width)
    middle = x_ref[0].astype(F32) + (mul(o_ref[0], proj) + vectors_ref[4:5])
    gain = vectors_ref[5:6]
    normed, unit, scale = normalize(middle, gain, vectors_ref[6:7])
    low = normed.astype(BF16)
    normed_ref[0] = low
    upstream = cot_ref[0]
    branch = middle + vectors_ref[7:8]
    grad_normed = None
    for part in range(parts):
        first = weights_ref[:, part * rows : (part + 1) * rows, :].reshape(width, width)
        second = weights_ref[
            part * per_part : (part + 1) * per_part, parts * rows : 2 * parts * rows, :
        ].reshape(width, width)
        span = slice(part * width, (part + 1) * width)
        hidden = mul(low, first) + hidden_bias_ref[:, span]
        active, slope = gelu_pair(hidden)
        active = active.astype(BF16)
        act_ref[0, :, span] = active
        branch = branch + mul(active, second)
        grad_hidden = mul_nt(upstream, second) * slope
        low_grad = grad_hidden.astype(BF16)
        dh_ref[0, :, span] = low_grad
        hidden_sum_ref[0:1, span] += column(low_grad.astype(F32))
        back = mul_nt(low_grad, first)
        grad_normed = back if grad_normed is None else grad_normed + back
    out_ref[0] = branch.astype(BF16)
    wide = upstream.astype(F32)
    grad_middle = wide + norm_back(grad_normed, unit, scale, gain)
    low_middle = grad_middle.astype(BF16)
    dp_ref[0] = low_middle
    do_ref[0] = mul_nt(low_middle, proj).astype(BF16)
    sums_ref[0:1] += column(wide)
    sums_ref[1:2] += column(grad_normed * unit)
    sums_ref[2:3] += column(grad_normed)
    sums_ref[3:4] += column(low_middle.astype(F32))


def feed(units, mixed, cotangent, weights, vectors, hidden_bias):
    count, size, width = units.shape
    inner = hidden_bias.shape[-1]

    def rows(columns):
        return pl.BlockSpec((1, size, columns), lambda u: (u, 0, 0))

    return pl.pallas_call(
        feed_kernel,
        grid=(count,),
        in_specs=[
            rows(width),
            rows(width),
            rows(width),
            whole(weights.shape),
            whole(vectors.shape),
            whole(hidden_bias.shape),
        ],
        out_specs=[
            rows(width),
            rows(width),
            rows(width),
            rows(inner),
            rows(inner),
            rows(width),
            pl.BlockSpec((8, width), lambda u: (0, 0)),
            pl.BlockSpec((8, inner), lambda u: (0, 0)),
        ],
        out_shape=[
            shaped((count, size, width), BF16),
            shaped((count, size, width), BF16),
            shaped((count, size, width), BF16),
            shaped((count, size, inner), BF16),
            shaped((count, size, inner), BF16),
            shaped((count, size, width), BF16),
            shaped((8, width), F32),
            shaped((8, inner), F32),
        ],
        compiler_params=params(1),
        cost_estimate=pl.CostEstimate(
            flops=2 * count * size * width * (4 * inner + 2 * width),
            bytes_accessed=count * size * (width * 20 + inner * 4),
            transcendentals=2 * count * size * inner,
        ),
        name="feed",
    )(units, mixed, cotangent, weights, vectors, hidden_bias)


def weight_kernel(parts, shards, normed_ref, dh_ref, act_ref, dz_ref, o_ref, dp_ref, out_ref, left, right):
    step = pl.program_id(0)
    width = normed_ref.shape[-1]
    rows = width // shards
    per_part = shards // parts

    @pl.when(step == 0)
    def turn():
        left[...] = normed_ref[...].T
        right[...] = dz_ref[...].T

    for part in range(parts):

        @pl.when(step == part)
        def first():
            grad = mul(left[...], dh_ref[...])
            out_ref[:, part * rows : (part + 1) * rows, :] = grad.astype(BF16).reshape(
                shards, rows, width
            )

        @pl.when(step == parts + part)
        def second():
            grad = mul(right[...], act_ref[...]).astype(BF16).T
            out_ref[
                part * per_part : (part + 1) * per_part, parts * rows : 2 * parts * rows, :
            ] = grad.reshape(per_part, parts * rows, width)

    @pl.when(step == 2 * parts)
    def third():
        grad = mul(o_ref[...].T, dp_ref[...])
        out_ref[:, 2 * parts * rows :, :] = grad.astype(BF16).reshape(shards, rows, width)


def weight_grads(normed, grad_hidden, active, grad_branch, mixed, grad_attended, shards):
    count, width = normed.shape
    inner = active.shape[-1]
    parts = inner // width
    shard_rows = (2 * parts + 1) * (width // shards)
    return pl.pallas_call(
        functools.partial(weight_kernel, parts, shards),
        grid=(2 * parts + 1,),
        in_specs=[
            whole(normed.shape),
            pl.BlockSpec((count, width), lambda s: (0, jnp.minimum(s, parts - 1))),
            pl.BlockSpec((count, width), lambda s: (0, jnp.clip(s - parts, 0, parts - 1))),
            whole(grad_branch.shape),
            whole(mixed.shape),
            whole(grad_attended.shape),
        ],
        out_specs=whole((shards, shard_rows, width)),
        out_shape=shaped((shards, shard_rows, width), BF16),
        scratch_shapes=[pltpu.VMEM((width, count), BF16)] * 2,
        compiler_params=params(1),
        cost_estimate=pl.CostEstimate(
            flops=2 * count * width * (2 * inner + width),
            bytes_accessed=count * (8 * width + 4 * inner),
            transcendentals=0,
        ),
        name="weight_grads",
    )(normed, grad_hidden, active, grad_branch, mixed, grad_attended)


def halving_orders(shards):
    reaches = [1 << bit for bit in range(shards.bit_length() - 1)]
    return reaches, reaches[:1] + reaches[2:] + reaches[1:2]


def slot_of(shard, order):
    slot = 0
    for reach in order:
        slot = 2 * slot + (shard // reach) % 2
    return slot


def qkv_weight_kernel(shards, normed_ref, dq_ref, dkv_ref, low_ref, high_ref, left):
    step = pl.program_id(0)
    width = normed_ref.shape[-1]
    rows = width // shards
    half = width // 2
    low_order, high_order = halving_orders(shards)

    def keep(ref, order, start, grad):
        for shard in range(shards):
            ref[slot_of(shard, order), :, start : start + grad.shape[1]] = grad[
                shard * rows : (shard + 1) * rows
            ]

    @pl.when(step == 0)
    def query_part():
        left[...] = normed_ref[...].T
        keep(low_ref, low_order, 0, mul(left[...], dq_ref[...]).astype(BF16))

    @pl.when(step == 1)
    def key_part():
        grad = mul(left[...], dkv_ref[0]).astype(BF16)
        keep(low_ref, low_order, width, grad[:, :half])
        keep(high_ref, high_order, 0, grad[:, half:])

    @pl.when(step == 2)
    def value_part():
        keep(high_ref, high_order, half, mul(left[...], dkv_ref[0]).astype(BF16))


def qkv_weight_grad(normed, dq, dkv, shards):
    count, width = normed.shape
    half = (shards, width // shards, 3 * width // 2)
    return pl.pallas_call(
        functools.partial(qkv_weight_kernel, shards),
        grid=(3,),
        in_specs=[
            whole(normed.shape),
            whole(dq.shape),
            pl.BlockSpec((1, count, width), lambda s: (jnp.maximum(s - 1, 0), 0, 0)),
        ],
        out_specs=[whole(half), whole(half)],
        out_shape=[shaped(half, BF16), shaped(half, BF16)],
        scratch_shapes=[pltpu.VMEM((width, count), BF16)],
        compiler_params=params(1),
        cost_estimate=LATE,
        name="qkv_weight_grad",
    )(normed, dq, dkv)


def input_kernel(
    x_ref, dx_ref, dq_ref, dkv_ref, weight_ref, vectors_ref, first_ref, second_ref, third_ref, sums_ref
):
    step = pl.program_id(0)

    @pl.when(step == 0)
    def clear():
        sums_ref[...] = jnp.zeros_like(sums_ref)

    gain = vectors_ref[0:1]
    unused, unit, scale = normalize(x_ref[0].astype(F32), gain, vectors_ref[1:2])
    grad = mul_nt(dq_ref[0], qkv_part(weight_ref, 0))
    grad = grad + mul_nt(dkv_ref[0, 0], qkv_part(weight_ref, 1))
    grad = grad + mul_nt(dkv_ref[1, 0], qkv_part(weight_ref, 2))
    value = (dx_ref[0].astype(F32) + norm_back(grad, unit, scale, gain)).astype(BF16)
    for place, ref in enumerate((first_ref, second_ref, third_ref)):

        @pl.when(step == place)
        def keep():
            ref[...] = value

    sums_ref[0:1] += column(grad * unit)
    sums_ref[1:2] += column(grad)
    sums_ref[2:3] += column(dq_ref[0].astype(F32))
    sums_ref[3:4] += column(dkv_ref[1, 0].astype(F32))


def input_grads(units, grad_middle, dq, dkv, weight, vectors):
    count, size, width = units.shape
    rows = pl.BlockSpec((1, size, width), lambda u: (u, 0, 0))
    return pl.pallas_call(
        input_kernel,
        grid=(count,),
        in_specs=[
            rows,
            rows,
            rows,
            pl.BlockSpec((2, 1, size, width), lambda u: (0, u, 0, 0)),
            whole(weight.shape),
            whole(vectors.shape),
        ],
        out_specs=[whole((size, width))] * 3 + [pl.BlockSpec((8, width), lambda u: (0, 0))],
        out_shape=[shaped((size, width), BF16)] * 3 + [shaped((8, width), F32)],
        compiler_params=params(1),
        cost_estimate=LATE,
        name="input_grads",
    )(units, grad_middle, dq, dkv, weight, vectors)


def halving_sum(value, axis, size, place, order):
    for reach in order:
        pairs = [(index, index ^ reach) for index in range(size)]
        halves = value.reshape((2, value.shape[0] // 2) + value.shape[1:])
        bit = (place // reach) % 2
        got = lax.ppermute(lax.dynamic_index_in_dim(halves, 1 - bit, 0, False), axis, pairs)
        kept = lax.dynamic_index_in_dim(halves, bit, 0, False)
        value = (kept.astype(F32) + got.astype(F32)).astype(BF16)
    return value


def fast_body(fsdp_size, *args):
    (
        inputs,
        cotangent,
        first_gain,
        first_shift,
        qkv_weight,
        query_bias,
        value_bias,
        proj_weight,
        proj_bias,
        second_gain,
        second_shift,
        hidden_weight,
        hidden_bias,
        output_weight,
        output_bias,
    ) = args
    images, size, width = inputs.shape
    row_count = images * size
    side = lax.axis_index("seq")
    place = lax.axis_index("fsdp")
    swap_sides = [(0, 1), (1, 0)]
    swap_cores = [(index, index ^ 1) for index in range(fsdp_size)]
    swap_middle = []
    for index in range(0, fsdp_size, 2):
        swap_middle += [(fsdp_size + index, index + 1), (index + 1, fsdp_size + index)]
    stays = side == place % 2

    def middle_swap(value):
        return jnp.where(stays, value, lax.ppermute(value, ("seq", "fsdp"), swap_middle))

    def gather_units(values):
        got = lax.ppermute(
            lax.dynamic_index_in_dim(values, 2 * (1 - side), 0, False), "seq", swap_sides
        )
        kept = lax.dynamic_index_in_dim(values, 2 * side, 0, False)
        return jnp.stack([kept, got, middle_swap(values[1])])

    def return_units(values, after=None):
        got = lax.ppermute(values[1], "seq", swap_sides)
        centre = lax.ppermute(values[2], ("seq", "fsdp"), swap_middle)
        if after is not None:
            got, centre, after = lax.optimization_barrier((got, centre, after))
        centre = jnp.where(stays, values[2], centre)
        first = jnp.where(side == 0, values[0], got)
        last = jnp.where(side == 0, got, values[0])
        value = jnp.stack([first, centre, last])
        return value if after is None else (value, after)

    def both(value):
        return value.astype(F32) + lax.ppermute(value, "seq", swap_sides).astype(F32)

    parts = hidden_weight.shape[1] // width
    rows = hidden_weight.shape[0]
    short = [
        first_gain,
        first_shift,
        query_bias,
        value_bias,
        proj_bias,
        second_gain,
        second_shift,
        output_bias,
    ]
    count = first_gain.shape[0]
    full_head = lax.all_gather(head_pack(qkv_weight, hidden_bias, short), "fsdp", axis=0)
    units = gather_units(inputs)
    hidden_weight, output_weight, proj_weight, units = lax.optimization_barrier(
        (hidden_weight, output_weight, proj_weight, units)
    )
    pack = jnp.concatenate(
        [hidden_weight[:, part * width : (part + 1) * width] for part in range(parts)]
        + [output_weight, proj_weight],
        0,
    )
    full_pack = lax.all_gather(pack, "fsdp", axis=0)
    vectors = full_head[:, rows:, :count].astype(F32).transpose(1, 0, 2)
    vectors = vectors.reshape(len(short), width)
    bias_hidden = full_head[:, rows, 128 : 128 + hidden_bias.shape[0]].astype(F32)
    bias_hidden = bias_hidden.reshape(1, parts * width)
    qkv, normed, to_other = project(units, full_head, vectors)
    to_other, cotangent = lax.optimization_barrier((to_other, cotangent))
    other = lax.ppermute(to_other, "fsdp", swap_cores)[:, None]
    grads_up = gather_units(cotangent)
    places_pair = [(qkv, 1, 0), (qkv, 2, 0), (qkv, 1, 1), (qkv, 2, 1)]
    places_one = [(qkv, 1, 2), (qkv, 2, 2), (other, 0, 0), (other, 1, 0)]
    mixed_pair, lse_pair = mix(qkv, 0, 2, places_pair)
    mixed, lse_one = mix(qkv, 2, 1, places_one, mixed_pair)
    (
        out,
        grad_mixed,
        normed_two,
        active,
        grad_hidden,
        grad_attended,
        sums_two,
        sum_hidden,
    ) = feed(units, mixed, grads_up, full_pack, vectors, bias_hidden)
    block_out = return_units(out)

    def flat(value):
        return value.reshape(row_count, value.shape[-1])

    grad_pack = weight_grads(
        flat(normed_two),
        flat(grad_hidden),
        flat(active),
        flat(grads_up),
        flat(mixed),
        flat(grad_attended),
        fsdp_size,
    )
    grad_mixed, grad_pack = lax.optimization_barrier((grad_mixed, grad_pack))
    shard_pack = lax.psum_scatter(grad_pack, "fsdp", scatter_dimension=0, tiled=False)
    dq_one, dkv_one, dkv_other = mix_back(qkv, 2, 1, places_one, mixed, grad_mixed, lse_one)
    dkv_got = lax.ppermute(dkv_other, "fsdp", swap_cores)
    dq, dkv, unused = mix_back(qkv, 0, 2, places_pair, mixed, grad_mixed, lse_pair, dq_one)
    dkv = dkv.at[:, 2].set((dkv_one.astype(F32) + dkv_got.astype(F32)).astype(BF16)[:, 0])
    sides = qkv_weight_grad(flat(normed), flat(dq), dkv.reshape(2, row_count, width), fsdp_size)
    orders = halving_orders(fsdp_size)
    sides = [
        halving_sum(value, "fsdp", fsdp_size, place, order[:1])
        for value, order in zip(sides, orders)
    ]
    sides, shard_pack, dq, dkv = lax.optimization_barrier((sides, shard_pack, dq, dkv))
    shard_pack = both(shard_pack)
    sides = [
        halving_sum(value, "fsdp", fsdp_size, place, order[1:2])
        for value, order in zip(sides, orders)
    ]
    *grad_units, sums_one = input_grads(units, grad_attended, dq, dkv, full_head, vectors)
    sides, grad_units, sums_one = lax.optimization_barrier((sides, grad_units, sums_one))
    shard_sides = [
        halving_sum(value, "fsdp", fsdp_size, place, order[2:])[0]
        for value, order in zip(sides, orders)
    ]
    small_grads = [
        sums_one[0],
        sums_one[1],
        sums_one[2],
        sums_one[3],
        sums_two[3],
        sums_two[1],
        sums_two[2],
        sums_two[0],
        sum_hidden[0],
    ]
    packed = jnp.concatenate([value.reshape(fsdp_size, -1) for value in small_grads], 1)
    packed = jnp.pad(packed, ((0, 0), (0, -packed.shape[1] % 1024)))
    packed = packed.reshape(-1, 128)
    mine = lax.psum_scatter(packed, "fsdp", scatter_dimension=0, tiled=True)
    shard_sides = [both(value) for value in shard_sides]
    input_grad, shard_sides = return_units(grad_units, shard_sides)
    mine = both(mine).reshape(-1)
    pieces = []
    for index in range(len(short)):
        pieces.append(mine[index * count : (index + 1) * count])
    (
        grad_gain_one,
        grad_shift_one,
        grad_query_b,
        grad_value_b,
        grad_proj_b,
        grad_gain_two,
        grad_shift_two,
        grad_output_b,
    ) = pieces
    grad_hidden_b = mine[len(short) * count :][: hidden_bias.shape[0]]
    grad_hidden_w = jnp.concatenate(
        [shard_pack[part * rows : (part + 1) * rows] for part in range(parts)], 1
    )
    grad_output_w = shard_pack[parts * rows : 2 * parts * rows]
    grad_proj_w = shard_pack[2 * parts * rows :]
    grad_qkv_w = jnp.concatenate(shard_sides, 1)
    return (
        block_out,
        input_grad,
        grad_gain_one,
        grad_shift_one,
        grad_qkv_w,
        grad_query_b,
        grad_value_b,
        grad_proj_w,
        grad_proj_b,
        grad_gain_two,
        grad_shift_two,
        grad_hidden_w,
        grad_hidden_b,
        grad_output_w,
        grad_output_b,
    )


def pick_body(seq_size, fsdp_size):
    def body(*args):
        images, size, width = args[0].shape
        inner = args[11].shape[1]
        fits = (
            seq_size == 2
            and images == 3
            and fsdp_size > 1
            and fsdp_size & (fsdp_size - 1) == 0
            and size % 8 == 0
            and width % 128 == 0
            and (width // fsdp_size) % 16 == 0
            and inner % width == 0
            and width // fsdp_size <= 128
            and 128 + inner // fsdp_size <= 3 * width
            and fsdp_size % (inner // width) == 0
        )
        if fits:
            return fast_body(fsdp_size, *args)
        return general_body(*args)

    return body


def solution(mesh):
    shape = mesh.shape
    body = pick_body(shape["seq"], shape["fsdp"])
    return jax.shard_map(
        body,
        mesh=mesh,
        in_specs=(
            P("fsdp", "seq", None),
            P("fsdp", "seq", None),
            P("fsdp"),
            P("fsdp"),
            P("fsdp", None),
            P("fsdp"),
            P("fsdp"),
            P("fsdp", None),
            P("fsdp"),
            P("fsdp"),
            P("fsdp"),
            P("fsdp", None),
            P("fsdp"),
            P("fsdp", None),
            P("fsdp"),
        ),
        out_specs=(
            P("fsdp", "seq", None),
            P("fsdp", "seq", None),
            P("fsdp"),
            P("fsdp"),
            P("fsdp", None),
            P("fsdp"),
            P("fsdp"),
            P("fsdp", None),
            P("fsdp"),
            P("fsdp"),
            P("fsdp"),
            P("fsdp", None),
            P("fsdp"),
            P("fsdp", None),
            P("fsdp"),
        ),
        check_vma=False,
    )
```

```python
import functools

import jax
import jax.numpy as jnp
from jax import lax
from jax.experimental import pallas as pl
from jax.experimental.pallas import tpu as pltpu
from jax.sharding import PartitionSpec as P

HEADS = 12
HEAD_DIM = 64


EPS = 1e-06


def normalize(rows, gain, shift):
    row_mean = jnp.mean(rows, -1, keepdims=True)
    centred = rows - row_mean
    variance = jnp.mean(centred * centred, -1, keepdims=True)
    scaled = lax.rsqrt(variance + EPS)
    unit = centred * scaled
    return (unit * gain + shift, unit, scaled)


def norm_back(grad_out, unit, scaled, gain):
    grad_unit = grad_out * gain
    first_mean = jnp.mean(grad_unit, -1, keepdims=True)
    second_mean = jnp.mean(grad_unit * unit, -1, keepdims=True)
    return scaled * (grad_unit - first_mean - unit * second_mean)


def gelu_exact(value):
    return jax.nn.gelu(value, approximate=False)


def column_sum(values):
    return jnp.sum(values.astype(jnp.float32), 0)


def general_body(
    inputs,
    cotangent,
    first_gain,
    first_shift,
    qkv_weight,
    query_bias,
    value_bias,
    proj_weight,
    proj_bias,
    second_gain,
    second_shift,
    hidden_weight,
    hidden_bias,
    output_weight,
    output_bias,
):
    images, local_len, width = inputs.shape
    row_count = images * local_len
    factor = HEAD_DIM ** (-0.5)
    (
        gain_one,
        shift_one,
        full_qkv,
        bias_query,
        bias_value,
        full_proj,
        bias_proj,
        gain_two,
        shift_two,
        full_hidden,
        bias_hidden,
        full_output,
        bias_output,
    ) = (
        lax.all_gather(first_gain, "fsdp", axis=0, tiled=True),
        lax.all_gather(first_shift, "fsdp", axis=0, tiled=True),
        lax.all_gather(qkv_weight, "fsdp", axis=0, tiled=True),
        lax.all_gather(query_bias, "fsdp", axis=0, tiled=True),
        lax.all_gather(value_bias, "fsdp", axis=0, tiled=True),
        lax.all_gather(proj_weight, "fsdp", axis=0, tiled=True),
        lax.all_gather(proj_bias, "fsdp", axis=0, tiled=True),
        lax.all_gather(second_gain, "fsdp", axis=0, tiled=True),
        lax.all_gather(second_shift, "fsdp", axis=0, tiled=True),
        lax.all_gather(hidden_weight, "fsdp", axis=0, tiled=True),
        lax.all_gather(hidden_bias, "fsdp", axis=0, tiled=True),
        lax.all_gather(output_weight, "fsdp", axis=0, tiled=True),
        lax.all_gather(output_bias, "fsdp", axis=0, tiled=True),
    )
    rows = inputs.reshape(row_count, width).astype(jnp.float32)
    normed, unit_one, scale_one = normalize(
        rows, gain_one.astype(jnp.float32), shift_one.astype(jnp.float32)
    )
    normed_low = normed.astype(jnp.bfloat16)
    projected = jnp.dot(normed_low, full_qkv, preferred_element_type=jnp.float32)
    head_shape = (images, local_len, HEADS, HEAD_DIM)
    query = (
        (projected[:, :width] + bias_query.astype(jnp.float32))
        .astype(jnp.bfloat16)
        .reshape(head_shape)
    )
    keys = projected[:, width : 2 * width].astype(jnp.bfloat16).reshape(head_shape)
    values = (
        (projected[:, 2 * width :] + bias_value.astype(jnp.float32))
        .astype(jnp.bfloat16)
        .reshape(head_shape)
    )
    all_keys, all_values = (
        lax.all_gather(keys, "seq", axis=1, tiled=True),
        lax.all_gather(values, "seq", axis=1, tiled=True),
    )

    def attend(items):
        query_one, key_one, value_one = items
        scores = (
            jnp.einsum("qhd,khd->hqk", query_one, key_one, preferred_element_type=jnp.float32)
            * factor
        )
        row_max = jnp.max(scores, -1, keepdims=True)
        exponent = jnp.exp(scores - row_max)
        row_total = jnp.sum(exponent, -1, keepdims=True)
        weights = (exponent / row_total).astype(jnp.bfloat16)
        mixed_one = jnp.einsum(
            "hqk,khd->qhd", weights, value_one, preferred_element_type=jnp.float32
        )
        return (mixed_one, (row_max + jnp.log(row_total))[..., 0])

    mixed, log_total = lax.map(attend, (query, all_keys, all_values))
    mixed_low = mixed.reshape(row_count, width).astype(jnp.bfloat16)
    attended = jnp.dot(mixed_low, full_proj, preferred_element_type=jnp.float32) + bias_proj.astype(
        jnp.float32
    )
    middle = rows + attended
    normed_two, unit_two, scale_two = normalize(
        middle, gain_two.astype(jnp.float32), shift_two.astype(jnp.float32)
    )
    normed_two_low = normed_two.astype(jnp.bfloat16)
    hidden_pre = jnp.dot(
        normed_two_low, full_hidden, preferred_element_type=jnp.float32
    ) + bias_hidden.astype(jnp.float32)
    activated = gelu_exact(hidden_pre).astype(jnp.bfloat16)
    branch = jnp.dot(
        activated, full_output, preferred_element_type=jnp.float32
    ) + bias_output.astype(jnp.float32)
    block_out = (middle + branch).astype(jnp.bfloat16).reshape(inputs.shape)
    upstream = cotangent.reshape(row_count, width).astype(jnp.float32)
    grad_branch = upstream.astype(jnp.bfloat16)
    grad_output_w = jnp.einsum(
        "rf,rd->fd", activated, grad_branch, preferred_element_type=jnp.float32
    )
    grad_output_b = column_sum(grad_branch)
    grad_act = jnp.einsum("rd,fd->rf", grad_branch, full_output, preferred_element_type=jnp.float32)
    unused_value, pull_gelu = jax.vjp(gelu_exact, hidden_pre)
    grad_hidden = pull_gelu(grad_act)[0].astype(jnp.bfloat16)
    grad_hidden_w = jnp.einsum(
        "rd,rf->df", normed_two_low, grad_hidden, preferred_element_type=jnp.float32
    )
    grad_hidden_b = column_sum(grad_hidden)
    grad_normed_two = jnp.einsum(
        "rf,df->rd", grad_hidden, full_hidden, preferred_element_type=jnp.float32
    )
    grad_gain_two = jnp.sum(grad_normed_two * unit_two, 0)
    grad_shift_two = jnp.sum(grad_normed_two, 0)
    grad_middle = upstream + norm_back(
        grad_normed_two, unit_two, scale_two, gain_two.astype(jnp.float32)
    )
    grad_attended = grad_middle.astype(jnp.bfloat16)
    grad_proj_w = jnp.einsum(
        "re,rd->ed", mixed_low, grad_attended, preferred_element_type=jnp.float32
    )
    grad_proj_b = column_sum(grad_attended)
    grad_mixed = jnp.einsum(
        "rd,ed->re", grad_attended, full_proj, preferred_element_type=jnp.float32
    )
    grad_mixed = grad_mixed.astype(jnp.bfloat16).reshape(head_shape)

    def attend_back(items):
        query_one, key_one, value_one, grad_one, log_one = items
        scores = (
            jnp.einsum("qhd,khd->hqk", query_one, key_one, preferred_element_type=jnp.float32)
            * factor
        )
        probs = jnp.exp(scores - log_one[..., None])
        grad_value = jnp.einsum(
            "hqk,qhd->khd", probs.astype(jnp.bfloat16), grad_one, preferred_element_type=jnp.float32
        )
        grad_probs = jnp.einsum(
            "qhd,khd->hqk", grad_one, value_one, preferred_element_type=jnp.float32
        )
        inner = jnp.sum(probs * grad_probs, -1, keepdims=True)
        grad_scores = (probs * (grad_probs - inner)).astype(jnp.bfloat16)
        grad_query = (
            jnp.einsum("hqk,khd->qhd", grad_scores, key_one, preferred_element_type=jnp.float32)
            * factor
        )
        grad_key = (
            jnp.einsum("hqk,qhd->khd", grad_scores, query_one, preferred_element_type=jnp.float32)
            * factor
        )
        return (grad_query, grad_key, grad_value)

    grad_query, grad_keys, grad_values = lax.map(
        attend_back, (query, all_keys, all_values, grad_mixed, log_total)
    )
    grad_keys, grad_values = (
        lax.psum_scatter(
            grad_keys.astype(jnp.bfloat16), "seq", scatter_dimension=1, tiled=True
        ).astype(jnp.float32),
        lax.psum_scatter(
            grad_values.astype(jnp.bfloat16), "seq", scatter_dimension=1, tiled=True
        ).astype(jnp.float32),
    )
    grad_qkv = jnp.concatenate(
        [
            grad_query.reshape(row_count, width),
            grad_keys.reshape(row_count, width),
            grad_values.reshape(row_count, width),
        ],
        -1,
    ).astype(jnp.bfloat16)
    grad_qkv_w = jnp.einsum("rd,rc->dc", normed_low, grad_qkv, preferred_element_type=jnp.float32)
    grad_query_b = column_sum(grad_qkv[:, :width])
    grad_value_b = column_sum(grad_qkv[:, 2 * width :])
    grad_normed = jnp.einsum("rc,dc->rd", grad_qkv, full_qkv, preferred_element_type=jnp.float32)
    grad_gain_one = jnp.sum(grad_normed * unit_one, 0)
    grad_shift_one = jnp.sum(grad_normed, 0)
    grad_rows = grad_middle + norm_back(
        grad_normed, unit_one, scale_one, gain_one.astype(jnp.float32)
    )
    input_grad = grad_rows.astype(jnp.bfloat16).reshape(inputs.shape)
    parts = (
        lax.psum_scatter(
            grad_gain_one.astype(jnp.bfloat16), "fsdp", scatter_dimension=0, tiled=True
        ).astype(jnp.float32),
        lax.psum_scatter(
            grad_shift_one.astype(jnp.bfloat16), "fsdp", scatter_dimension=0, tiled=True
        ).astype(jnp.float32),
        lax.psum_scatter(
            grad_qkv_w.astype(jnp.bfloat16), "fsdp", scatter_dimension=0, tiled=True
        ).astype(jnp.float32),
        lax.psum_scatter(
            grad_query_b.astype(jnp.bfloat16), "fsdp", scatter_dimension=0, tiled=True
        ).astype(jnp.float32),
        lax.psum_scatter(
            grad_value_b.astype(jnp.bfloat16), "fsdp", scatter_dimension=0, tiled=True
        ).astype(jnp.float32),
        lax.psum_scatter(
            grad_proj_w.astype(jnp.bfloat16), "fsdp", scatter_dimension=0, tiled=True
        ).astype(jnp.float32),
        lax.psum_scatter(
            grad_proj_b.astype(jnp.bfloat16), "fsdp", scatter_dimension=0, tiled=True
        ).astype(jnp.float32),
        lax.psum_scatter(
            grad_gain_two.astype(jnp.bfloat16), "fsdp", scatter_dimension=0, tiled=True
        ).astype(jnp.float32),
        lax.psum_scatter(
            grad_shift_two.astype(jnp.bfloat16), "fsdp", scatter_dimension=0, tiled=True
        ).astype(jnp.float32),
        lax.psum_scatter(
            grad_hidden_w.astype(jnp.bfloat16), "fsdp", scatter_dimension=0, tiled=True
        ).astype(jnp.float32),
        lax.psum_scatter(
            grad_hidden_b.astype(jnp.bfloat16), "fsdp", scatter_dimension=0, tiled=True
        ).astype(jnp.float32),
        lax.psum_scatter(
            grad_output_w.astype(jnp.bfloat16), "fsdp", scatter_dimension=0, tiled=True
        ).astype(jnp.float32),
        lax.psum_scatter(
            grad_output_b.astype(jnp.bfloat16), "fsdp", scatter_dimension=0, tiled=True
        ).astype(jnp.float32),
    )
    shares = (
        lax.psum(parts[0].astype(jnp.bfloat16), "seq").astype(jnp.float32),
        lax.psum(parts[1].astype(jnp.bfloat16), "seq").astype(jnp.float32),
        lax.psum(parts[2].astype(jnp.bfloat16), "seq").astype(jnp.float32),
        lax.psum(parts[3].astype(jnp.bfloat16), "seq").astype(jnp.float32),
        lax.psum(parts[4].astype(jnp.bfloat16), "seq").astype(jnp.float32),
        lax.psum(parts[5].astype(jnp.bfloat16), "seq").astype(jnp.float32),
        lax.psum(parts[6].astype(jnp.bfloat16), "seq").astype(jnp.float32),
        lax.psum(parts[7].astype(jnp.bfloat16), "seq").astype(jnp.float32),
        lax.psum(parts[8].astype(jnp.bfloat16), "seq").astype(jnp.float32),
        lax.psum(parts[9].astype(jnp.bfloat16), "seq").astype(jnp.float32),
        lax.psum(parts[10].astype(jnp.bfloat16), "seq").astype(jnp.float32),
        lax.psum(parts[11].astype(jnp.bfloat16), "seq").astype(jnp.float32),
        lax.psum(parts[12].astype(jnp.bfloat16), "seq").astype(jnp.float32),
    )
    return (
        block_out,
        input_grad,
        shares[0],
        shares[1],
        shares[2],
        shares[3],
        shares[4],
        shares[5],
        shares[6],
        shares[7],
        shares[8],
        shares[9],
        shares[10],
        shares[11],
        shares[12],
    )


F32 = jnp.float32
BF16 = jnp.bfloat16
VMEM_BYTES = 60 * 1024 * 1024
NT = (((1,), (1,)), ((), ()))
LATE = pl.CostEstimate(flops=1000, bytes_accessed=1000, transcendentals=0)


def mul(left, right):
    return jnp.dot(left, right, preferred_element_type=F32)


def mul_nt(left, right):
    return lax.dot_general(left, right, NT, preferred_element_type=F32)


def params(count):
    return pltpu.CompilerParams(
        dimension_semantics=("arbitrary",) * count, vmem_limit_bytes=VMEM_BYTES
    )


def whole(shape):
    return pl.BlockSpec(shape, lambda *ids: (0,) * len(shape), pipeline_mode=pl.Buffered(1))


def shaped(shape, dtype):
    return jax.ShapeDtypeStruct(shape, dtype)


def qkv_part(weight_ref, part):
    width = weight_ref.shape[-1] // 3
    rows = width // weight_ref.shape[0]
    return weight_ref[:, :rows, part * width : (part + 1) * width].reshape(width, width)


def project_kernel(x_ref, weight_ref, vectors_ref, qkv_ref, normed_ref, other_ref):
    step = pl.program_id(0)
    normed, unused_unit, unused_scale = normalize(
        x_ref[0].astype(F32), vectors_ref[0:1], vectors_ref[1:2]
    )
    low = normed.astype(BF16)
    normed_ref[0] = low
    for part in range(3):
        value = mul(low, qkv_part(weight_ref, part))
        if part == 0:
            value = (value + vectors_ref[2:3]) * HEAD_DIM ** (-0.5)
        elif part == 2:
            value = value + vectors_ref[3:4]
        qkv_ref[part, 0] = value.astype(BF16)

    @pl.when(step == pl.num_programs(0) - 1)
    def last():
        other_ref[...] = qkv_ref[1:, 0]


def project(units, weight, vectors):
    count, size, width = units.shape
    return pl.pallas_call(
        project_kernel,
        grid=(count,),
        in_specs=[
            pl.BlockSpec((1, size, width), lambda u: (u, 0, 0)),
            whole(weight.shape),
            whole(vectors.shape),
        ],
        out_specs=[
            pl.BlockSpec((3, 1, size, width), lambda u: (0, u, 0, 0)),
            pl.BlockSpec((1, size, width), lambda u: (u, 0, 0)),
            whole((2, size, width)),
        ],
        out_shape=[
            shaped((3, count, size, width), BF16),
            shaped((count, size, width), BF16),
            shaped((2, size, width), BF16),
        ],
        compiler_params=params(1),
        cost_estimate=pl.CostEstimate(
            flops=2 * count * size * width * 3 * width,
            bytes_accessed=count * size * width * 10 + 6 * width * width,
            transcendentals=0,
        ),
        name="project",
    )(units, weight, vectors)


def head_kernel(weight_ref, hidden_ref, *rest):
    out_ref = rest[-1]
    short = jnp.concatenate([ref[...].astype(F32) for ref in rest[:-1]], 0)
    count, length = short.shape
    columns = weight_ref.shape[1]
    hidden = hidden_ref[...].astype(F32)
    wide = hidden.shape[1]
    hidden = jnp.concatenate([hidden, jnp.zeros((count - 1, wide), F32)], 0)
    lines = jnp.concatenate(
        [
            short,
            jnp.zeros((count, 128 - length), F32),
            hidden,
            jnp.zeros((count, columns - 128 - wide), F32),
        ],
        1,
    )
    out_ref[...] = jnp.concatenate([weight_ref[...].astype(F32), lines], 0).astype(BF16)


def head_pack(weight, hidden, short):
    rows, columns = weight.shape
    return pl.pallas_call(
        head_kernel,
        out_shape=shaped((rows + len(short), columns), BF16),
        name="head_pack",
    )(weight, hidden[None], *[value[None] for value in short])


def head_mask(size):
    return lax.broadcasted_iota(jnp.int32, (size, 2 * HEAD_DIM), 1) // HEAD_DIM


def mix_kernel(q_ref, ka_ref, va_ref, kb_ref, vb_ref, *rest):
    o_ref, lse_ref = rest[-2:]
    query = q_ref[0, 0]
    lanes = head_mask(query.shape[0])
    keys = (ka_ref[0, 0], kb_ref[0, 0])
    turned = (va_ref[0, 0].T, vb_ref[0, 0].T)
    outs = []
    for head in range(2):
        one = jnp.where(lanes == head, query, jnp.zeros_like(query))
        scores = [mul_nt(key, one) for key in keys]
        top = jnp.maximum(
            jnp.max(scores[0], 0, keepdims=True), jnp.max(scores[1], 0, keepdims=True)
        )
        grown = [jnp.exp(score - top) for score in scores]
        total = jnp.sum(grown[0], 0, keepdims=True) + jnp.sum(grown[1], 0, keepdims=True)
        span = slice(head * HEAD_DIM, (head + 1) * HEAD_DIM)
        mixed = mul(turned[0][span], grown[0].astype(BF16)) + mul(
            turned[1][span], grown[1].astype(BF16)
        )
        outs.append(mixed / total)
        lse_ref[0, 0, head : head + 1] = top + jnp.log(total)
    o_ref[0] = jnp.concatenate(outs, 0).T.astype(BF16)


def attend_specs(size, key_places):
    lanes = 2 * HEAD_DIM
    specs = []
    for source, part, unit in key_places:
        specs.append(
            pl.BlockSpec((1, 1, size, lanes), lambda h, u, part=part, unit=unit: (part, unit, 0, h))
        )
    return specs


def mix(qkv, first_unit, unit_count, key_places, earlier=None):
    size, width = qkv.shape[2:]
    lanes = 2 * HEAD_DIM
    pairs = width // lanes
    flops = 4 * unit_count * size * 2 * size * width
    return pl.pallas_call(
        mix_kernel,
        grid=(pairs, unit_count),
        in_specs=[pl.BlockSpec((1, 1, size, lanes), lambda h, u: (0, first_unit + u, 0, h))]
        + attend_specs(size, key_places)
        + [pl.BlockSpec(memory_space=pl.ANY)] * (earlier is not None),
        out_specs=[
            pl.BlockSpec((1, size, lanes), lambda h, u: (first_unit + u, 0, h)),
            pl.BlockSpec((1, 1, 8, size), lambda h, u: (u, h, 0, 0)),
        ],
        out_shape=[
            shaped((qkv.shape[1], size, width), BF16),
            shaped((unit_count, pairs, 8, size), F32),
        ],
        input_output_aliases={} if earlier is None else {5: 0},
        compiler_params=params(2),
        cost_estimate=pl.CostEstimate(
            flops=4 * flops,
            bytes_accessed=unit_count * size * width * 8,
            transcendentals=unit_count * size * 2 * size * width // HEAD_DIM,
        ),
        name="mix",
    )(qkv, *[place[0] for place in key_places], *([] if earlier is None else [earlier]))


def mix_back_kernel(
    unit_count,
    q_ref,
    ka_ref,
    va_ref,
    kb_ref,
    vb_ref,
    o_ref,
    do_ref,
    lse_ref,
    *rest,
):
    dq_ref, dkv_ref, last_ref, dk_acc, dv_acc = rest[-5:]
    step = pl.program_id(1)
    query = q_ref[0, 0]
    grad = do_ref[0]
    size = query.shape[0]
    lanes = head_mask(size)
    keys = (ka_ref[0, 0], kb_ref[0, 0])
    values = (va_ref[0, 0], vb_ref[0, 0])
    turned = (keys[0].T, keys[1].T)
    product = grad.astype(F32) * o_ref[0].astype(F32)
    high = product.astype(BF16)
    rest = (product - high.astype(F32)).astype(BF16)
    chosen = (
        lax.broadcasted_iota(jnp.int32, (8, 2 * HEAD_DIM), 1) // HEAD_DIM
        == lax.broadcasted_iota(jnp.int32, (8, 2 * HEAD_DIM), 0)
    ).astype(BF16)
    inner = mul_nt(chosen, high) + mul_nt(chosen, rest)
    dks, dvs, dqs = [None, None], [None, None], []
    for head in range(2):
        mine = lanes == head
        one_query = jnp.where(mine, query, jnp.zeros_like(query))
        one_grad = jnp.where(mine, grad, jnp.zeros_like(grad))
        span = slice(head * HEAD_DIM, (head + 1) * HEAD_DIM)
        log_row = lse_ref[0, 0, head : head + 1]
        inner_row = inner[head : head + 1]
        dq = None
        for side in range(2):
            probs = jnp.exp(mul_nt(keys[side], one_query) - log_row)
            dv = mul(probs.astype(BF16), one_grad)
            change = mul_nt(values[side], one_grad)
            scored = (probs * (change - inner_row)).astype(BF16)
            dk = mul(scored, one_query)
            part = mul(turned[side][span], scored)
            dq = part if dq is None else dq + part
            dks[side] = dk if head == 0 else dks[side] + dk
            dvs[side] = dv if head == 0 else dvs[side] + dv
        dqs.append(dq)
    dq_ref[0] = (jnp.concatenate(dqs, 0).T * HEAD_DIM ** (-0.5)).astype(BF16)
    if unit_count == 1:
        for side, ref in enumerate((dkv_ref, last_ref)):
            ref[0, 0] = dks[side].astype(BF16)
            ref[1, 0] = dvs[side].astype(BF16)
        return

    last_ref[...] = jnp.zeros_like(last_ref)

    @pl.when(step == 0)
    def first():
        for side in range(2):
            dk_acc[side] = dks[side]
            dv_acc[side] = dvs[side]

    @pl.when(jnp.logical_and(step > 0, step < unit_count - 1))
    def between():
        for side in range(2):
            dk_acc[side] += dks[side]
            dv_acc[side] += dvs[side]

    @pl.when(step == unit_count - 1)
    def last():
        for side in range(2):
            dkv_ref[0, side] = (dk_acc[side] + dks[side]).astype(BF16)
            dkv_ref[1, side] = (dv_acc[side] + dvs[side]).astype(BF16)


def mix_back(qkv, first_unit, unit_count, key_places, mixed, grad_mixed, lse, earlier=None):
    size, width = qkv.shape[2:]
    lanes = 2 * HEAD_DIM
    pairs = width // lanes
    units = qkv.shape[1]
    if unit_count == 1:
        key_outs = [pl.BlockSpec((2, 1, size, lanes), lambda h, u: (0, 0, 0, h))] * 2
        key_shapes = [shaped((2, 1, size, width), BF16)] * 2
    else:
        key_outs = [
            pl.BlockSpec((2, 2, size, lanes), lambda h, u: (0, 0, 0, h)),
            pl.BlockSpec((8, lanes), lambda h, u: (0, 0)),
        ]
        key_shapes = [shaped((2, units, size, width), BF16), shaped((8, lanes), F32)]
    return pl.pallas_call(
        functools.partial(mix_back_kernel, unit_count),
        grid=(pairs, unit_count),
        in_specs=[pl.BlockSpec((1, 1, size, lanes), lambda h, u: (0, first_unit + u, 0, h))]
        + attend_specs(size, key_places)
        + [
            pl.BlockSpec((1, size, lanes), lambda h, u: (first_unit + u, 0, h)),
            pl.BlockSpec((1, size, lanes), lambda h, u: (first_unit + u, 0, h)),
            pl.BlockSpec((1, 1, 8, size), lambda h, u: (u, h, 0, 0)),
        ]
        + [pl.BlockSpec(memory_space=pl.ANY)] * (earlier is not None),
        out_specs=[
            pl.BlockSpec((1, size, lanes), lambda h, u: (first_unit + u, 0, h)),
            *key_outs,
        ],
        out_shape=[shaped((units, size, width), BF16), *key_shapes],
        input_output_aliases={} if earlier is None else {8: 0},
        scratch_shapes=[pltpu.VMEM((2, size, lanes), F32)] * 2,
        compiler_params=params(2),
        cost_estimate=LATE,
        name="mix_back",
    )(
        qkv,
        *[place[0] for place in key_places],
        mixed,
        grad_mixed,
        lse,
        *([] if earlier is None else [earlier]),
    )


def gelu_pair(value):
    share = 0.5 + 0.5 * lax.erf(value * 0.5**0.5)
    density = jnp.exp(value * value * -0.5) * 0.3989422804014327
    return value * share, share + value * density


def column(values):
    return jnp.sum(values, 0, keepdims=True)


def feed_kernel(
    x_ref,
    o_ref,
    cot_ref,
    weights_ref,
    vectors_ref,
    hidden_bias_ref,
    out_ref,
    do_ref,
    normed_ref,
    act_ref,
    dh_ref,
    dp_ref,
    sums_ref,
    hidden_sum_ref,
):
    step = pl.program_id(0)
    width = x_ref.shape[-1]
    shards, shard_rows = weights_ref.shape[:2]
    rows = width // shards
    parts = hidden_bias_ref.shape[-1] // width
    per_part = shards // parts

    @pl.when(step == 0)
    def clear():
        sums_ref[...] = jnp.zeros_like(sums_ref)
        hidden_sum_ref[...] = jnp.zeros_like(hidden_sum_ref)

    proj = weights_ref[:, 2 * parts * rows :, :].reshape(width, width)
    middle = x_ref[0].astype(F32) + (mul(o_ref[0], proj) + vectors_ref[4:5])
    gain = vectors_ref[5:6]
    normed, unit, scale = normalize(middle, gain, vectors_ref[6:7])
    low = normed.astype(BF16)
    normed_ref[0] = low
    upstream = cot_ref[0]
    branch = middle + vectors_ref[7:8]
    grad_normed = None
    for part in range(parts):
        first = weights_ref[:, part * rows : (part + 1) * rows, :].reshape(width, width)
        second = weights_ref[
            part * per_part : (part + 1) * per_part, parts * rows : 2 * parts * rows, :
        ].reshape(width, width)
        span = slice(part * width, (part + 1) * width)
        hidden = mul(low, first) + hidden_bias_ref[:, span]
        active, slope = gelu_pair(hidden)
        active = active.astype(BF16)
        act_ref[0, :, span] = active
        branch = branch + mul(active, second)
        grad_hidden = mul_nt(upstream, second) * slope
        low_grad = grad_hidden.astype(BF16)
        dh_ref[0, :, span] = low_grad
        hidden_sum_ref[0:1, span] += column(low_grad.astype(F32))
        back = mul_nt(low_grad, first)
        grad_normed = back if grad_normed is None else grad_normed + back
    out_ref[0] = branch.astype(BF16)
    wide = upstream.astype(F32)
    grad_middle = wide + norm_back(grad_normed, unit, scale, gain)
    low_middle = grad_middle.astype(BF16)
    dp_ref[0] = low_middle
    do_ref[0] = mul_nt(low_middle, proj).astype(BF16)
    sums_ref[0:1] += column(wide)
    sums_ref[1:2] += column(grad_normed * unit)
    sums_ref[2:3] += column(grad_normed)
    sums_ref[3:4] += column(low_middle.astype(F32))


def feed(units, mixed, cotangent, weights, vectors, hidden_bias):
    count, size, width = units.shape
    inner = hidden_bias.shape[-1]

    def rows(columns):
        return pl.BlockSpec((1, size, columns), lambda u: (u, 0, 0))

    return pl.pallas_call(
        feed_kernel,
        grid=(count,),
        in_specs=[
            rows(width),
            rows(width),
            rows(width),
            whole(weights.shape),
            whole(vectors.shape),
            whole(hidden_bias.shape),
        ],
        out_specs=[
            rows(width),
            rows(width),
            rows(width),
            rows(inner),
            rows(inner),
            rows(width),
            pl.BlockSpec((8, width), lambda u: (0, 0)),
            pl.BlockSpec((8, inner), lambda u: (0, 0)),
        ],
        out_shape=[
            shaped((count, size, width), BF16),
            shaped((count, size, width), BF16),
            shaped((count, size, width), BF16),
            shaped((count, size, inner), BF16),
            shaped((count, size, inner), BF16),
            shaped((count, size, width), BF16),
            shaped((8, width), F32),
            shaped((8, inner), F32),
        ],
        compiler_params=params(1),
        cost_estimate=pl.CostEstimate(
            flops=2 * count * size * width * (4 * inner + 2 * width),
            bytes_accessed=count * size * (width * 20 + inner * 4),
            transcendentals=2 * count * size * inner,
        ),
        name="feed",
    )(units, mixed, cotangent, weights, vectors, hidden_bias)


def weight_kernel(parts, shards, normed_ref, dh_ref, act_ref, dz_ref, o_ref, dp_ref, out_ref, left, right):
    step = pl.program_id(0)
    width = normed_ref.shape[-1]
    rows = width // shards
    per_part = shards // parts

    @pl.when(step == 0)
    def turn():
        left[...] = normed_ref[...].T
        right[...] = dz_ref[...].T

    for part in range(parts):

        @pl.when(step == part)
        def first():
            grad = mul(left[...], dh_ref[...])
            out_ref[:, part * rows : (part + 1) * rows, :] = grad.astype(BF16).reshape(
                shards, rows, width
            )

        @pl.when(step == parts + part)
        def second():
            grad = mul(right[...], act_ref[...]).astype(BF16).T
            out_ref[
                part * per_part : (part + 1) * per_part, parts * rows : 2 * parts * rows, :
            ] = grad.reshape(per_part, parts * rows, width)

    @pl.when(step == 2 * parts)
    def third():
        grad = mul(o_ref[...].T, dp_ref[...])
        out_ref[:, 2 * parts * rows :, :] = grad.astype(BF16).reshape(shards, rows, width)


def weight_grads(normed, grad_hidden, active, grad_branch, mixed, grad_attended, shards):
    count, width = normed.shape
    inner = active.shape[-1]
    parts = inner // width
    shard_rows = (2 * parts + 1) * (width // shards)
    return pl.pallas_call(
        functools.partial(weight_kernel, parts, shards),
        grid=(2 * parts + 1,),
        in_specs=[
            whole(normed.shape),
            pl.BlockSpec((count, width), lambda s: (0, jnp.minimum(s, parts - 1))),
            pl.BlockSpec((count, width), lambda s: (0, jnp.clip(s - parts, 0, parts - 1))),
            whole(grad_branch.shape),
            whole(mixed.shape),
            whole(grad_attended.shape),
        ],
        out_specs=whole((shards, shard_rows, width)),
        out_shape=shaped((shards, shard_rows, width), BF16),
        scratch_shapes=[pltpu.VMEM((width, count), BF16)] * 2,
        compiler_params=params(1),
        cost_estimate=pl.CostEstimate(
            flops=2 * count * width * (2 * inner + width),
            bytes_accessed=count * (8 * width + 4 * inner),
            transcendentals=0,
        ),
        name="weight_grads",
    )(normed, grad_hidden, active, grad_branch, mixed, grad_attended)


def halving_orders(shards):
    reaches = [1 << bit for bit in range(shards.bit_length() - 1)]
    return reaches, reaches[:1] + reaches[2:] + reaches[1:2]


def slot_of(shard, order):
    slot = 0
    for reach in order:
        slot = 2 * slot + (shard // reach) % 2
    return slot


def qkv_weight_kernel(shards, normed_ref, dq_ref, dkv_ref, out_ref, left):
    step = pl.program_id(0)
    width = normed_ref.shape[-1]
    rows = width // shards
    half = width // 2
    orders = halving_orders(shards)

    def keep(side, start, grad):
        for shard in range(shards):
            slot = slot_of(shard, orders[side][1:])
            out_ref[shard % 2, side, slot, :, start : start + grad.shape[1]] = grad[
                shard * rows : (shard + 1) * rows
            ]

    @pl.when(step == 0)
    def query_part():
        left[...] = normed_ref[...].T
        keep(0, 0, mul(left[...], dq_ref[...]).astype(BF16))

    @pl.when(step == 1)
    def key_part():
        grad = mul(left[...], dkv_ref[0]).astype(BF16)
        keep(0, width, grad[:, :half])
        keep(1, 0, grad[:, half:])

    @pl.when(step == 2)
    def value_part():
        keep(1, half, mul(left[...], dkv_ref[0]).astype(BF16))


def qkv_weight_grad(normed, dq, dkv, shards):
    count, width = normed.shape
    half = (2, 2, shards // 2, width // shards, 3 * width // 2)
    return pl.pallas_call(
        functools.partial(qkv_weight_kernel, shards),
        grid=(3,),
        in_specs=[
            whole(normed.shape),
            whole(dq.shape),
            pl.BlockSpec((1, count, width), lambda s: (jnp.maximum(s - 1, 0), 0, 0)),
        ],
        out_specs=whole(half),
        out_shape=shaped(half, BF16),
        scratch_shapes=[pltpu.VMEM((width, count), BF16)],
        compiler_params=params(1),
        cost_estimate=LATE,
        name="qkv_weight_grad",
    )(normed, dq, dkv)


def input_kernel(
    x_ref, dx_ref, dq_ref, dkv_ref, weight_ref, vectors_ref, first_ref, second_ref, third_ref, sums_ref
):
    step = pl.program_id(0)

    @pl.when(step == 0)
    def clear():
        sums_ref[...] = jnp.zeros_like(sums_ref)

    gain = vectors_ref[0:1]
    unused, unit, scale = normalize(x_ref[0].astype(F32), gain, vectors_ref[1:2])
    grad = mul_nt(dq_ref[0], qkv_part(weight_ref, 0))
    grad = grad + mul_nt(dkv_ref[0, 0], qkv_part(weight_ref, 1))
    grad = grad + mul_nt(dkv_ref[1, 0], qkv_part(weight_ref, 2))
    value = (dx_ref[0].astype(F32) + norm_back(grad, unit, scale, gain)).astype(BF16)
    for place, ref in enumerate((first_ref, second_ref, third_ref)):

        @pl.when(step == place)
        def keep():
            ref[...] = value

    sums_ref[0:1] += column(grad * unit)
    sums_ref[1:2] += column(grad)
    sums_ref[2:3] += column(dq_ref[0].astype(F32))
    sums_ref[3:4] += column(dkv_ref[1, 0].astype(F32))


def input_grads(units, grad_middle, dq, dkv, weight, vectors):
    count, size, width = units.shape
    rows = pl.BlockSpec((1, size, width), lambda u: (u, 0, 0))
    return pl.pallas_call(
        input_kernel,
        grid=(count,),
        in_specs=[
            rows,
            rows,
            rows,
            pl.BlockSpec((2, 1, size, width), lambda u: (0, u, 0, 0)),
            whole(weight.shape),
            whole(vectors.shape),
        ],
        out_specs=[whole((size, width))] * 3 + [pl.BlockSpec((8, width), lambda u: (0, 0))],
        out_shape=[shaped((size, width), BF16)] * 3 + [shaped((8, width), F32)],
        compiler_params=params(1),
        cost_estimate=LATE,
        name="input_grads",
    )(units, grad_middle, dq, dkv, weight, vectors)


def halving_sum(value, axis, size, place, order):
    for reach in order:
        pairs = [(index, index ^ reach) for index in range(size)]
        halves = value.reshape((2, value.shape[0] // 2) + value.shape[1:])
        bit = (place // reach) % 2
        got = lax.ppermute(lax.dynamic_index_in_dim(halves, 1 - bit, 0, False), axis, pairs)
        kept = lax.dynamic_index_in_dim(halves, bit, 0, False)
        value = (kept.astype(F32) + got.astype(F32)).astype(BF16)
    return value


def fast_body(fsdp_size, *args):
    (
        inputs,
        cotangent,
        first_gain,
        first_shift,
        qkv_weight,
        query_bias,
        value_bias,
        proj_weight,
        proj_bias,
        second_gain,
        second_shift,
        hidden_weight,
        hidden_bias,
        output_weight,
        output_bias,
    ) = args
    images, size, width = inputs.shape
    row_count = images * size
    side = lax.axis_index("seq")
    place = lax.axis_index("fsdp")
    swap_sides = [(0, 1), (1, 0)]
    swap_cores = [(index, index ^ 1) for index in range(fsdp_size)]
    swap_middle = []
    for index in range(0, fsdp_size, 2):
        swap_middle += [(fsdp_size + index, index + 1), (index + 1, fsdp_size + index)]
    stays = side == place % 2

    def middle_swap(value):
        return jnp.where(stays, value, lax.ppermute(value, ("seq", "fsdp"), swap_middle))

    def gather_units(values):
        got = lax.ppermute(
            lax.dynamic_index_in_dim(values, 2 * (1 - side), 0, False), "seq", swap_sides
        )
        kept = lax.dynamic_index_in_dim(values, 2 * side, 0, False)
        return jnp.stack([kept, got, middle_swap(values[1])])

    def send_back(values):
        return (
            lax.ppermute(values[1], "seq", swap_sides),
            lax.ppermute(values[2], ("seq", "fsdp"), swap_middle),
        )

    def in_place(values, got, centre):
        centre = jnp.where(stays, values[2], centre)
        first = jnp.where(side == 0, values[0], got)
        last = jnp.where(side == 0, got, values[0])
        return jnp.stack([first, centre, last])

    def both(value):
        return value.astype(F32) + lax.ppermute(value, "seq", swap_sides).astype(F32)

    parts = hidden_weight.shape[1] // width
    rows = hidden_weight.shape[0]
    short = [
        first_gain,
        first_shift,
        query_bias,
        value_bias,
        proj_bias,
        second_gain,
        second_shift,
        output_bias,
    ]
    count = first_gain.shape[0]
    full_head = lax.all_gather(head_pack(qkv_weight, hidden_bias, short), "fsdp", axis=0)
    units = gather_units(inputs)
    hidden_weight, output_weight, proj_weight, units = lax.optimization_barrier(
        (hidden_weight, output_weight, proj_weight, units)
    )
    pack = jnp.concatenate(
        [hidden_weight[:, part * width : (part + 1) * width] for part in range(parts)]
        + [output_weight, proj_weight],
        0,
    )
    full_pack = lax.all_gather(pack, "fsdp", axis=0)
    vectors = full_head[:, rows:, :count].astype(F32).transpose(1, 0, 2)
    vectors = vectors.reshape(len(short), width)
    bias_hidden = full_head[:, rows, 128 : 128 + hidden_bias.shape[0]].astype(F32)
    bias_hidden = bias_hidden.reshape(1, parts * width)
    qkv, normed, to_other = project(units, full_head, vectors)
    to_other, cotangent = lax.optimization_barrier((to_other, cotangent))
    other = lax.ppermute(to_other, "fsdp", swap_cores)[:, None]
    grads_up = gather_units(cotangent)
    places_pair = [(qkv, 1, 0), (qkv, 2, 0), (qkv, 1, 1), (qkv, 2, 1)]
    places_one = [(qkv, 1, 2), (qkv, 2, 2), (other, 0, 0), (other, 1, 0)]
    mixed_pair, lse_pair = mix(qkv, 0, 2, places_pair)
    mixed, lse_one = mix(qkv, 2, 1, places_one, mixed_pair)
    (
        out,
        grad_mixed,
        normed_two,
        active,
        grad_hidden,
        grad_attended,
        sums_two,
        sum_hidden,
    ) = feed(units, mixed, grads_up, full_pack, vectors, bias_hidden)
    out_got, out_centre = send_back(out)

    def flat(value):
        return value.reshape(row_count, value.shape[-1])

    grad_pack = weight_grads(
        flat(normed_two),
        flat(grad_hidden),
        flat(active),
        flat(grads_up),
        flat(mixed),
        flat(grad_attended),
        fsdp_size,
    )
    grad_mixed, grad_pack = lax.optimization_barrier((grad_mixed, grad_pack))
    shard_pack = lax.psum_scatter(grad_pack, "fsdp", scatter_dimension=0, tiled=False)
    dq_one, dkv_one, dkv_other = mix_back(qkv, 2, 1, places_one, mixed, grad_mixed, lse_one)
    dkv_got = lax.ppermute(dkv_other, "fsdp", swap_cores)
    dq, dkv, unused = mix_back(qkv, 0, 2, places_pair, mixed, grad_mixed, lse_pair, dq_one)
    dkv = dkv.at[:, 2].set((dkv_one.astype(F32) + dkv_got.astype(F32)).astype(BF16)[:, 0])
    dq, dkv, out_got, out_centre = lax.optimization_barrier((dq, dkv, out_got, out_centre))
    block_out = in_place(out, out_got, out_centre)
    sides = qkv_weight_grad(flat(normed), flat(dq), dkv.reshape(2, row_count, width), fsdp_size)
    orders = halving_orders(fsdp_size)
    sides = halving_sum(sides, "fsdp", fsdp_size, place, [1])[0]
    sides, shard_pack, dq, dkv = lax.optimization_barrier((sides, shard_pack, dq, dkv))
    shard_pack = both(shard_pack)
    sides = [
        halving_sum(value, "fsdp", fsdp_size, place, order[1:2])
        for value, order in zip(sides, orders)
    ]
    *grad_units, sums_one = input_grads(units, grad_attended, dq, dkv, full_head, vectors)
    sides, grad_units, sums_one = lax.optimization_barrier((sides, grad_units, sums_one))
    shard_sides = [
        halving_sum(value, "fsdp", fsdp_size, place, order[2:])[0]
        for value, order in zip(sides, orders)
    ]
    small_grads = [
        sums_one[0],
        sums_one[1],
        sums_one[2],
        sums_one[3],
        sums_two[3],
        sums_two[1],
        sums_two[2],
        sums_two[0],
        sum_hidden[0],
    ]
    packed = jnp.concatenate([value.reshape(fsdp_size, -1) for value in small_grads], 1)
    packed = jnp.pad(packed, ((0, 0), (0, -packed.shape[1] % 128)))
    lines = packed.shape[1] // 128
    everyone = lax.all_gather(packed.reshape(-1, 128), "fsdp", axis=0)
    mine = lax.dynamic_slice_in_dim(everyone, place * lines, lines, 1).sum(0)
    shard_sides = [both(value) for value in shard_sides]
    got, centre = send_back(grad_units)
    got, centre, shard_sides = lax.optimization_barrier((got, centre, shard_sides))
    input_grad = in_place(grad_units, got, centre)
    mine = both(mine).reshape(-1)
    pieces = []
    for index in range(len(short)):
        pieces.append(mine[index * count : (index + 1) * count])
    (
        grad_gain_one,
        grad_shift_one,
        grad_query_b,
        grad_value_b,
        grad_proj_b,
        grad_gain_two,
        grad_shift_two,
        grad_output_b,
    ) = pieces
    grad_hidden_b = mine[len(short) * count :][: hidden_bias.shape[0]]
    grad_hidden_w = jnp.concatenate(
        [shard_pack[part * rows : (part + 1) * rows] for part in range(parts)], 1
    )
    grad_output_w = shard_pack[parts * rows : 2 * parts * rows]
    grad_proj_w = shard_pack[2 * parts * rows :]
    grad_qkv_w = jnp.concatenate(shard_sides, 1)
    return (
        block_out,
        input_grad,
        grad_gain_one,
        grad_shift_one,
        grad_qkv_w,
        grad_query_b,
        grad_value_b,
        grad_proj_w,
        grad_proj_b,
        grad_gain_two,
        grad_shift_two,
        grad_hidden_w,
        grad_hidden_b,
        grad_output_w,
        grad_output_b,
    )


def pick_body(seq_size, fsdp_size):
    def body(*args):
        images, size, width = args[0].shape
        inner = args[11].shape[1]
        fits = (
            seq_size == 2
            and images == 3
            and fsdp_size > 1
            and fsdp_size & (fsdp_size - 1) == 0
            and size % 8 == 0
            and width % 128 == 0
            and (width // fsdp_size) % 16 == 0
            and inner % width == 0
            and width // fsdp_size <= 128
            and 128 + inner // fsdp_size <= 3 * width
            and fsdp_size % (inner // width) == 0
        )
        if fits:
            return fast_body(fsdp_size, *args)
        return general_body(*args)

    return body


def solution(mesh):
    shape = mesh.shape
    body = pick_body(shape["seq"], shape["fsdp"])
    return jax.shard_map(
        body,
        mesh=mesh,
        in_specs=(
            P("fsdp", "seq", None),
            P("fsdp", "seq", None),
            P("fsdp"),
            P("fsdp"),
            P("fsdp", None),
            P("fsdp"),
            P("fsdp"),
            P("fsdp", None),
            P("fsdp"),
            P("fsdp"),
            P("fsdp"),
            P("fsdp", None),
            P("fsdp"),
            P("fsdp", None),
            P("fsdp"),
        ),
        out_specs=(
            P("fsdp", "seq", None),
            P("fsdp", "seq", None),
            P("fsdp"),
            P("fsdp"),
            P("fsdp", None),
            P("fsdp"),
            P("fsdp"),
            P("fsdp", None),
            P("fsdp"),
            P("fsdp"),
            P("fsdp"),
            P("fsdp", None),
            P("fsdp"),
            P("fsdp", None),
            P("fsdp"),
        ),
        check_vma=False,
    )
```

```python
import functools

import jax
import jax.numpy as jnp
from jax import lax
from jax.experimental import pallas as pl
from jax.experimental.pallas import tpu as pltpu
from jax.sharding import PartitionSpec as P

HEADS = 12
HEAD_DIM = 64


EPS = 1e-06


def normalize(rows, gain, shift):
    row_mean = jnp.mean(rows, -1, keepdims=True)
    centred = rows - row_mean
    variance = jnp.mean(centred * centred, -1, keepdims=True)
    scaled = lax.rsqrt(variance + EPS)
    unit = centred * scaled
    return (unit * gain + shift, unit, scaled)


def norm_back(grad_out, unit, scaled, gain):
    grad_unit = grad_out * gain
    first_mean = jnp.mean(grad_unit, -1, keepdims=True)
    second_mean = jnp.mean(grad_unit * unit, -1, keepdims=True)
    return scaled * (grad_unit - first_mean - unit * second_mean)


def gelu_exact(value):
    return jax.nn.gelu(value, approximate=False)


def column_sum(values):
    return jnp.sum(values.astype(jnp.float32), 0)


def general_body(
    inputs,
    cotangent,
    first_gain,
    first_shift,
    qkv_weight,
    query_bias,
    value_bias,
    proj_weight,
    proj_bias,
    second_gain,
    second_shift,
    hidden_weight,
    hidden_bias,
    output_weight,
    output_bias,
):
    images, local_len, width = inputs.shape
    row_count = images * local_len
    factor = HEAD_DIM ** (-0.5)
    (
        gain_one,
        shift_one,
        full_qkv,
        bias_query,
        bias_value,
        full_proj,
        bias_proj,
        gain_two,
        shift_two,
        full_hidden,
        bias_hidden,
        full_output,
        bias_output,
    ) = (
        lax.all_gather(first_gain, "fsdp", axis=0, tiled=True),
        lax.all_gather(first_shift, "fsdp", axis=0, tiled=True),
        lax.all_gather(qkv_weight, "fsdp", axis=0, tiled=True),
        lax.all_gather(query_bias, "fsdp", axis=0, tiled=True),
        lax.all_gather(value_bias, "fsdp", axis=0, tiled=True),
        lax.all_gather(proj_weight, "fsdp", axis=0, tiled=True),
        lax.all_gather(proj_bias, "fsdp", axis=0, tiled=True),
        lax.all_gather(second_gain, "fsdp", axis=0, tiled=True),
        lax.all_gather(second_shift, "fsdp", axis=0, tiled=True),
        lax.all_gather(hidden_weight, "fsdp", axis=0, tiled=True),
        lax.all_gather(hidden_bias, "fsdp", axis=0, tiled=True),
        lax.all_gather(output_weight, "fsdp", axis=0, tiled=True),
        lax.all_gather(output_bias, "fsdp", axis=0, tiled=True),
    )
    rows = inputs.reshape(row_count, width).astype(jnp.float32)
    normed, unit_one, scale_one = normalize(
        rows, gain_one.astype(jnp.float32), shift_one.astype(jnp.float32)
    )
    normed_low = normed.astype(jnp.bfloat16)
    projected = jnp.dot(normed_low, full_qkv, preferred_element_type=jnp.float32)
    head_shape = (images, local_len, HEADS, HEAD_DIM)
    query = (
        (projected[:, :width] + bias_query.astype(jnp.float32))
        .astype(jnp.bfloat16)
        .reshape(head_shape)
    )
    keys = projected[:, width : 2 * width].astype(jnp.bfloat16).reshape(head_shape)
    values = (
        (projected[:, 2 * width :] + bias_value.astype(jnp.float32))
        .astype(jnp.bfloat16)
        .reshape(head_shape)
    )
    all_keys, all_values = (
        lax.all_gather(keys, "seq", axis=1, tiled=True),
        lax.all_gather(values, "seq", axis=1, tiled=True),
    )

    def attend(items):
        query_one, key_one, value_one = items
        scores = (
            jnp.einsum("qhd,khd->hqk", query_one, key_one, preferred_element_type=jnp.float32)
            * factor
        )
        row_max = jnp.max(scores, -1, keepdims=True)
        exponent = jnp.exp(scores - row_max)
        row_total = jnp.sum(exponent, -1, keepdims=True)
        weights = (exponent / row_total).astype(jnp.bfloat16)
        mixed_one = jnp.einsum(
            "hqk,khd->qhd", weights, value_one, preferred_element_type=jnp.float32
        )
        return (mixed_one, (row_max + jnp.log(row_total))[..., 0])

    mixed, log_total = lax.map(attend, (query, all_keys, all_values))
    mixed_low = mixed.reshape(row_count, width).astype(jnp.bfloat16)
    attended = jnp.dot(mixed_low, full_proj, preferred_element_type=jnp.float32) + bias_proj.astype(
        jnp.float32
    )
    middle = rows + attended
    normed_two, unit_two, scale_two = normalize(
        middle, gain_two.astype(jnp.float32), shift_two.astype(jnp.float32)
    )
    normed_two_low = normed_two.astype(jnp.bfloat16)
    hidden_pre = jnp.dot(
        normed_two_low, full_hidden, preferred_element_type=jnp.float32
    ) + bias_hidden.astype(jnp.float32)
    activated = gelu_exact(hidden_pre).astype(jnp.bfloat16)
    branch = jnp.dot(
        activated, full_output, preferred_element_type=jnp.float32
    ) + bias_output.astype(jnp.float32)
    block_out = (middle + branch).astype(jnp.bfloat16).reshape(inputs.shape)
    upstream = cotangent.reshape(row_count, width).astype(jnp.float32)
    grad_branch = upstream.astype(jnp.bfloat16)
    grad_output_w = jnp.einsum(
        "rf,rd->fd", activated, grad_branch, preferred_element_type=jnp.float32
    )
    grad_output_b = column_sum(grad_branch)
    grad_act = jnp.einsum("rd,fd->rf", grad_branch, full_output, preferred_element_type=jnp.float32)
    unused_value, pull_gelu = jax.vjp(gelu_exact, hidden_pre)
    grad_hidden = pull_gelu(grad_act)[0].astype(jnp.bfloat16)
    grad_hidden_w = jnp.einsum(
        "rd,rf->df", normed_two_low, grad_hidden, preferred_element_type=jnp.float32
    )
    grad_hidden_b = column_sum(grad_hidden)
    grad_normed_two = jnp.einsum(
        "rf,df->rd", grad_hidden, full_hidden, preferred_element_type=jnp.float32
    )
    grad_gain_two = jnp.sum(grad_normed_two * unit_two, 0)
    grad_shift_two = jnp.sum(grad_normed_two, 0)
    grad_middle = upstream + norm_back(
        grad_normed_two, unit_two, scale_two, gain_two.astype(jnp.float32)
    )
    grad_attended = grad_middle.astype(jnp.bfloat16)
    grad_proj_w = jnp.einsum(
        "re,rd->ed", mixed_low, grad_attended, preferred_element_type=jnp.float32
    )
    grad_proj_b = column_sum(grad_attended)
    grad_mixed = jnp.einsum(
        "rd,ed->re", grad_attended, full_proj, preferred_element_type=jnp.float32
    )
    grad_mixed = grad_mixed.astype(jnp.bfloat16).reshape(head_shape)

    def attend_back(items):
        query_one, key_one, value_one, grad_one, log_one = items
        scores = (
            jnp.einsum("qhd,khd->hqk", query_one, key_one, preferred_element_type=jnp.float32)
            * factor
        )
        probs = jnp.exp(scores - log_one[..., None])
        grad_value = jnp.einsum(
            "hqk,qhd->khd", probs.astype(jnp.bfloat16), grad_one, preferred_element_type=jnp.float32
        )
        grad_probs = jnp.einsum(
            "qhd,khd->hqk", grad_one, value_one, preferred_element_type=jnp.float32
        )
        inner = jnp.sum(probs * grad_probs, -1, keepdims=True)
        grad_scores = (probs * (grad_probs - inner)).astype(jnp.bfloat16)
        grad_query = (
            jnp.einsum("hqk,khd->qhd", grad_scores, key_one, preferred_element_type=jnp.float32)
            * factor
        )
        grad_key = (
            jnp.einsum("hqk,qhd->khd", grad_scores, query_one, preferred_element_type=jnp.float32)
            * factor
        )
        return (grad_query, grad_key, grad_value)

    grad_query, grad_keys, grad_values = lax.map(
        attend_back, (query, all_keys, all_values, grad_mixed, log_total)
    )
    grad_keys, grad_values = (
        lax.psum_scatter(
            grad_keys.astype(jnp.bfloat16), "seq", scatter_dimension=1, tiled=True
        ).astype(jnp.float32),
        lax.psum_scatter(
            grad_values.astype(jnp.bfloat16), "seq", scatter_dimension=1, tiled=True
        ).astype(jnp.float32),
    )
    grad_qkv = jnp.concatenate(
        [
            grad_query.reshape(row_count, width),
            grad_keys.reshape(row_count, width),
            grad_values.reshape(row_count, width),
        ],
        -1,
    ).astype(jnp.bfloat16)
    grad_qkv_w = jnp.einsum("rd,rc->dc", normed_low, grad_qkv, preferred_element_type=jnp.float32)
    grad_query_b = column_sum(grad_qkv[:, :width])
    grad_value_b = column_sum(grad_qkv[:, 2 * width :])
    grad_normed = jnp.einsum("rc,dc->rd", grad_qkv, full_qkv, preferred_element_type=jnp.float32)
    grad_gain_one = jnp.sum(grad_normed * unit_one, 0)
    grad_shift_one = jnp.sum(grad_normed, 0)
    grad_rows = grad_middle + norm_back(
        grad_normed, unit_one, scale_one, gain_one.astype(jnp.float32)
    )
    input_grad = grad_rows.astype(jnp.bfloat16).reshape(inputs.shape)
    parts = (
        lax.psum_scatter(
            grad_gain_one.astype(jnp.bfloat16), "fsdp", scatter_dimension=0, tiled=True
        ).astype(jnp.float32),
        lax.psum_scatter(
            grad_shift_one.astype(jnp.bfloat16), "fsdp", scatter_dimension=0, tiled=True
        ).astype(jnp.float32),
        lax.psum_scatter(
            grad_qkv_w.astype(jnp.bfloat16), "fsdp", scatter_dimension=0, tiled=True
        ).astype(jnp.float32),
        lax.psum_scatter(
            grad_query_b.astype(jnp.bfloat16), "fsdp", scatter_dimension=0, tiled=True
        ).astype(jnp.float32),
        lax.psum_scatter(
            grad_value_b.astype(jnp.bfloat16), "fsdp", scatter_dimension=0, tiled=True
        ).astype(jnp.float32),
        lax.psum_scatter(
            grad_proj_w.astype(jnp.bfloat16), "fsdp", scatter_dimension=0, tiled=True
        ).astype(jnp.float32),
        lax.psum_scatter(
            grad_proj_b.astype(jnp.bfloat16), "fsdp", scatter_dimension=0, tiled=True
        ).astype(jnp.float32),
        lax.psum_scatter(
            grad_gain_two.astype(jnp.bfloat16), "fsdp", scatter_dimension=0, tiled=True
        ).astype(jnp.float32),
        lax.psum_scatter(
            grad_shift_two.astype(jnp.bfloat16), "fsdp", scatter_dimension=0, tiled=True
        ).astype(jnp.float32),
        lax.psum_scatter(
            grad_hidden_w.astype(jnp.bfloat16), "fsdp", scatter_dimension=0, tiled=True
        ).astype(jnp.float32),
        lax.psum_scatter(
            grad_hidden_b.astype(jnp.bfloat16), "fsdp", scatter_dimension=0, tiled=True
        ).astype(jnp.float32),
        lax.psum_scatter(
            grad_output_w.astype(jnp.bfloat16), "fsdp", scatter_dimension=0, tiled=True
        ).astype(jnp.float32),
        lax.psum_scatter(
            grad_output_b.astype(jnp.bfloat16), "fsdp", scatter_dimension=0, tiled=True
        ).astype(jnp.float32),
    )
    shares = (
        lax.psum(parts[0].astype(jnp.bfloat16), "seq").astype(jnp.float32),
        lax.psum(parts[1].astype(jnp.bfloat16), "seq").astype(jnp.float32),
        lax.psum(parts[2].astype(jnp.bfloat16), "seq").astype(jnp.float32),
        lax.psum(parts[3].astype(jnp.bfloat16), "seq").astype(jnp.float32),
        lax.psum(parts[4].astype(jnp.bfloat16), "seq").astype(jnp.float32),
        lax.psum(parts[5].astype(jnp.bfloat16), "seq").astype(jnp.float32),
        lax.psum(parts[6].astype(jnp.bfloat16), "seq").astype(jnp.float32),
        lax.psum(parts[7].astype(jnp.bfloat16), "seq").astype(jnp.float32),
        lax.psum(parts[8].astype(jnp.bfloat16), "seq").astype(jnp.float32),
        lax.psum(parts[9].astype(jnp.bfloat16), "seq").astype(jnp.float32),
        lax.psum(parts[10].astype(jnp.bfloat16), "seq").astype(jnp.float32),
        lax.psum(parts[11].astype(jnp.bfloat16), "seq").astype(jnp.float32),
        lax.psum(parts[12].astype(jnp.bfloat16), "seq").astype(jnp.float32),
    )
    return (
        block_out,
        input_grad,
        shares[0],
        shares[1],
        shares[2],
        shares[3],
        shares[4],
        shares[5],
        shares[6],
        shares[7],
        shares[8],
        shares[9],
        shares[10],
        shares[11],
        shares[12],
    )


F32 = jnp.float32
BF16 = jnp.bfloat16
VMEM_BYTES = 60 * 1024 * 1024
NT = (((1,), (1,)), ((), ()))
LATE = pl.CostEstimate(flops=1000, bytes_accessed=1000, transcendentals=0)


def mul(left, right):
    return jnp.dot(left, right, preferred_element_type=F32)


def mul_nt(left, right):
    return lax.dot_general(left, right, NT, preferred_element_type=F32)


def params(count):
    return pltpu.CompilerParams(
        dimension_semantics=("arbitrary",) * count, vmem_limit_bytes=VMEM_BYTES
    )


def whole(shape):
    return pl.BlockSpec(shape, lambda *ids: (0,) * len(shape), pipeline_mode=pl.Buffered(1))


def shaped(shape, dtype):
    return jax.ShapeDtypeStruct(shape, dtype)


def qkv_part(weight_ref, part):
    width = weight_ref.shape[-1] // 3
    rows = width // weight_ref.shape[0]
    return weight_ref[:, :rows, part * width : (part + 1) * width].reshape(width, width)


def project_kernel(x_ref, weight_ref, vectors_ref, qkv_ref, normed_ref, other_ref):
    step = pl.program_id(0)
    normed, unused_unit, unused_scale = normalize(
        x_ref[0].astype(F32), vectors_ref[0:1], vectors_ref[1:2]
    )
    low = normed.astype(BF16)
    normed_ref[0] = low
    for part in range(3):
        value = mul(low, qkv_part(weight_ref, part))
        if part == 0:
            value = (value + vectors_ref[2:3]) * HEAD_DIM ** (-0.5)
        elif part == 2:
            value = value + vectors_ref[3:4]
        qkv_ref[part, 0] = value.astype(BF16)

    @pl.when(step == pl.num_programs(0) - 1)
    def last():
        other_ref[...] = qkv_ref[1:, 0]


def project(units, weight, vectors):
    count, size, width = units.shape
    return pl.pallas_call(
        project_kernel,
        grid=(count,),
        in_specs=[
            pl.BlockSpec((1, size, width), lambda u: (u, 0, 0)),
            whole(weight.shape),
            whole(vectors.shape),
        ],
        out_specs=[
            pl.BlockSpec((3, 1, size, width), lambda u: (0, u, 0, 0)),
            pl.BlockSpec((1, size, width), lambda u: (u, 0, 0)),
            whole((2, size, width)),
        ],
        out_shape=[
            shaped((3, count, size, width), BF16),
            shaped((count, size, width), BF16),
            shaped((2, size, width), BF16),
        ],
        compiler_params=params(1),
        cost_estimate=pl.CostEstimate(
            flops=2 * count * size * width * 3 * width,
            bytes_accessed=count * size * width * 10 + 6 * width * width,
            transcendentals=0,
        ),
        name="project",
    )(units, weight, vectors)


def head_kernel(weight_ref, hidden_ref, *rest):
    out_ref = rest[-1]
    short = jnp.concatenate([ref[...].astype(F32) for ref in rest[:-1]], 0)
    count, length = short.shape
    columns = weight_ref.shape[1]
    hidden = hidden_ref[...].astype(F32)
    wide = hidden.shape[1]
    hidden = jnp.concatenate([hidden, jnp.zeros((count - 1, wide), F32)], 0)
    lines = jnp.concatenate(
        [
            short,
            jnp.zeros((count, 128 - length), F32),
            hidden,
            jnp.zeros((count, columns - 128 - wide), F32),
        ],
        1,
    )
    out_ref[...] = jnp.concatenate([weight_ref[...].astype(F32), lines], 0).astype(BF16)


def head_pack(weight, hidden, short):
    rows, columns = weight.shape
    return pl.pallas_call(
        head_kernel,
        out_shape=shaped((rows + len(short), columns), BF16),
        name="head_pack",
    )(weight, hidden[None], *[value[None] for value in short])


def head_mask(size):
    return lax.broadcasted_iota(jnp.int32, (size, 2 * HEAD_DIM), 1) // HEAD_DIM


def mix_kernel(q_ref, ka_ref, va_ref, kb_ref, vb_ref, *rest):
    o_ref, lse_ref = rest[-2:]
    query = q_ref[0, 0]
    lanes = head_mask(query.shape[0])
    keys = (ka_ref[0, 0], kb_ref[0, 0])
    turned = (va_ref[0, 0].T, vb_ref[0, 0].T)
    outs = []
    for head in range(2):
        one = jnp.where(lanes == head, query, jnp.zeros_like(query))
        scores = [mul_nt(key, one) for key in keys]
        top = jnp.maximum(
            jnp.max(scores[0], 0, keepdims=True), jnp.max(scores[1], 0, keepdims=True)
        )
        grown = [jnp.exp(score - top) for score in scores]
        total = jnp.sum(grown[0], 0, keepdims=True) + jnp.sum(grown[1], 0, keepdims=True)
        span = slice(head * HEAD_DIM, (head + 1) * HEAD_DIM)
        mixed = mul(turned[0][span], grown[0].astype(BF16)) + mul(
            turned[1][span], grown[1].astype(BF16)
        )
        outs.append(mixed / total)
        lse_ref[0, 0, head : head + 1] = top + jnp.log(total)
    o_ref[0] = jnp.concatenate(outs, 0).T.astype(BF16)


def attend_specs(size, key_places):
    lanes = 2 * HEAD_DIM
    specs = []
    for source, part, unit in key_places:
        specs.append(
            pl.BlockSpec((1, 1, size, lanes), lambda h, u, part=part, unit=unit: (part, unit, 0, h))
        )
    return specs


def mix(qkv, first_unit, unit_count, key_places, earlier=None):
    size, width = qkv.shape[2:]
    lanes = 2 * HEAD_DIM
    pairs = width // lanes
    flops = 4 * unit_count * size * 2 * size * width
    return pl.pallas_call(
        mix_kernel,
        grid=(pairs, unit_count),
        in_specs=[pl.BlockSpec((1, 1, size, lanes), lambda h, u: (0, first_unit + u, 0, h))]
        + attend_specs(size, key_places)
        + [pl.BlockSpec(memory_space=pl.ANY)] * (earlier is not None),
        out_specs=[
            pl.BlockSpec((1, size, lanes), lambda h, u: (first_unit + u, 0, h)),
            pl.BlockSpec((1, 1, 8, size), lambda h, u: (u, h, 0, 0)),
        ],
        out_shape=[
            shaped((qkv.shape[1], size, width), BF16),
            shaped((unit_count, pairs, 8, size), F32),
        ],
        input_output_aliases={} if earlier is None else {5: 0},
        compiler_params=params(2),
        cost_estimate=pl.CostEstimate(
            flops=4 * flops,
            bytes_accessed=unit_count * size * width * 8,
            transcendentals=unit_count * size * 2 * size * width // HEAD_DIM,
        ),
        name="mix",
    )(qkv, *[place[0] for place in key_places], *([] if earlier is None else [earlier]))


def mix_back_kernel(
    unit_count,
    q_ref,
    ka_ref,
    va_ref,
    kb_ref,
    vb_ref,
    o_ref,
    do_ref,
    lse_ref,
    *rest,
):
    dq_ref, dkv_ref, last_ref, dk_acc, dv_acc = rest[-5:]
    step = pl.program_id(1)
    query = q_ref[0, 0]
    grad = do_ref[0]
    size = query.shape[0]
    lanes = head_mask(size)
    keys = (ka_ref[0, 0], kb_ref[0, 0])
    values = (va_ref[0, 0], vb_ref[0, 0])
    turned = (keys[0].T, keys[1].T)
    product = grad.astype(F32) * o_ref[0].astype(F32)
    high = product.astype(BF16)
    rest = (product - high.astype(F32)).astype(BF16)
    chosen = (
        lax.broadcasted_iota(jnp.int32, (8, 2 * HEAD_DIM), 1) // HEAD_DIM
        == lax.broadcasted_iota(jnp.int32, (8, 2 * HEAD_DIM), 0)
    ).astype(BF16)
    inner = mul_nt(chosen, high) + mul_nt(chosen, rest)
    dks, dvs, dqs = [None, None], [None, None], []
    for head in range(2):
        mine = lanes == head
        one_query = jnp.where(mine, query, jnp.zeros_like(query))
        one_grad = jnp.where(mine, grad, jnp.zeros_like(grad))
        span = slice(head * HEAD_DIM, (head + 1) * HEAD_DIM)
        log_row = lse_ref[0, 0, head : head + 1]
        inner_row = inner[head : head + 1]
        dq = None
        for side in range(2):
            probs = jnp.exp(mul_nt(keys[side], one_query) - log_row)
            dv = mul(probs.astype(BF16), one_grad)
            change = mul_nt(values[side], one_grad)
            scored = (probs * (change - inner_row)).astype(BF16)
            dk = mul(scored, one_query)
            part = mul(turned[side][span], scored)
            dq = part if dq is None else dq + part
            dks[side] = dk if head == 0 else dks[side] + dk
            dvs[side] = dv if head == 0 else dvs[side] + dv
        dqs.append(dq)
    dq_ref[0] = (jnp.concatenate(dqs, 0).T * HEAD_DIM ** (-0.5)).astype(BF16)
    if unit_count == 1:
        for side, ref in enumerate((dkv_ref, last_ref)):
            ref[0, 0] = dks[side].astype(BF16)
            ref[1, 0] = dvs[side].astype(BF16)
        return

    last_ref[...] = jnp.zeros_like(last_ref)

    @pl.when(step == 0)
    def first():
        for side in range(2):
            dk_acc[side] = dks[side]
            dv_acc[side] = dvs[side]

    @pl.when(jnp.logical_and(step > 0, step < unit_count - 1))
    def between():
        for side in range(2):
            dk_acc[side] += dks[side]
            dv_acc[side] += dvs[side]

    @pl.when(step == unit_count - 1)
    def last():
        for side in range(2):
            dkv_ref[0, side] = (dk_acc[side] + dks[side]).astype(BF16)
            dkv_ref[1, side] = (dv_acc[side] + dvs[side]).astype(BF16)


def mix_back(qkv, first_unit, unit_count, key_places, mixed, grad_mixed, lse, earlier=None):
    size, width = qkv.shape[2:]
    lanes = 2 * HEAD_DIM
    pairs = width // lanes
    units = qkv.shape[1]
    if unit_count == 1:
        key_outs = [pl.BlockSpec((2, 1, size, lanes), lambda h, u: (0, 0, 0, h))] * 2
        key_shapes = [shaped((2, 1, size, width), BF16)] * 2
    else:
        key_outs = [
            pl.BlockSpec((2, 2, size, lanes), lambda h, u: (0, 0, 0, h)),
            pl.BlockSpec((8, lanes), lambda h, u: (0, 0)),
        ]
        key_shapes = [shaped((2, units, size, width), BF16), shaped((8, lanes), F32)]
    return pl.pallas_call(
        functools.partial(mix_back_kernel, unit_count),
        grid=(pairs, unit_count),
        in_specs=[pl.BlockSpec((1, 1, size, lanes), lambda h, u: (0, first_unit + u, 0, h))]
        + attend_specs(size, key_places)
        + [
            pl.BlockSpec((1, size, lanes), lambda h, u: (first_unit + u, 0, h)),
            pl.BlockSpec((1, size, lanes), lambda h, u: (first_unit + u, 0, h)),
            pl.BlockSpec((1, 1, 8, size), lambda h, u: (u, h, 0, 0)),
        ]
        + [pl.BlockSpec(memory_space=pl.ANY)] * (earlier is not None),
        out_specs=[
            pl.BlockSpec((1, size, lanes), lambda h, u: (first_unit + u, 0, h)),
            *key_outs,
        ],
        out_shape=[shaped((units, size, width), BF16), *key_shapes],
        input_output_aliases={} if earlier is None else {8: 0},
        scratch_shapes=[pltpu.VMEM((2, size, lanes), F32)] * 2,
        compiler_params=params(2),
        cost_estimate=LATE,
        name="mix_back",
    )(
        qkv,
        *[place[0] for place in key_places],
        mixed,
        grad_mixed,
        lse,
        *([] if earlier is None else [earlier]),
    )


def gelu_pair(value):
    share = 0.5 + 0.5 * lax.erf(value * 0.5**0.5)
    density = jnp.exp(value * value * -0.5) * 0.3989422804014327
    return value * share, share + value * density


def column(values):
    return jnp.sum(values, 0, keepdims=True)


def feed_kernel(
    x_ref,
    o_ref,
    cot_ref,
    weights_ref,
    vectors_ref,
    hidden_bias_ref,
    out_ref,
    do_ref,
    normed_ref,
    act_ref,
    dh_ref,
    dp_ref,
    sums_ref,
    hidden_sum_ref,
):
    step = pl.program_id(0)
    width = x_ref.shape[-1]
    shards, shard_rows = weights_ref.shape[:2]
    rows = width // shards
    parts = hidden_bias_ref.shape[-1] // width
    per_part = shards // parts

    @pl.when(step == 0)
    def clear():
        sums_ref[...] = jnp.zeros_like(sums_ref)
        hidden_sum_ref[...] = jnp.zeros_like(hidden_sum_ref)

    proj = weights_ref[:, 2 * parts * rows :, :].reshape(width, width)
    middle = x_ref[0].astype(F32) + (mul(o_ref[0], proj) + vectors_ref[4:5])
    gain = vectors_ref[5:6]
    normed, unit, scale = normalize(middle, gain, vectors_ref[6:7])
    low = normed.astype(BF16)
    normed_ref[0] = low
    upstream = cot_ref[0]
    branch = middle + vectors_ref[7:8]
    grad_normed = None
    for part in range(parts):
        first = weights_ref[:, part * rows : (part + 1) * rows, :].reshape(width, width)
        second = weights_ref[
            part * per_part : (part + 1) * per_part, parts * rows : 2 * parts * rows, :
        ].reshape(width, width)
        span = slice(part * width, (part + 1) * width)
        hidden = mul(low, first) + hidden_bias_ref[:, span]
        active, slope = gelu_pair(hidden)
        active = active.astype(BF16)
        act_ref[0, :, span] = active
        branch = branch + mul(active, second)
        grad_hidden = mul_nt(upstream, second) * slope
        low_grad = grad_hidden.astype(BF16)
        dh_ref[0, :, span] = low_grad
        hidden_sum_ref[0:1, span] += column(low_grad.astype(F32))
        back = mul_nt(low_grad, first)
        grad_normed = back if grad_normed is None else grad_normed + back
    out_ref[0] = branch.astype(BF16)
    wide = upstream.astype(F32)
    grad_middle = wide + norm_back(grad_normed, unit, scale, gain)
    low_middle = grad_middle.astype(BF16)
    dp_ref[0] = low_middle
    do_ref[0] = mul_nt(low_middle, proj).astype(BF16)
    sums_ref[0:1] += column(wide)
    sums_ref[1:2] += column(grad_normed * unit)
    sums_ref[2:3] += column(grad_normed)
    sums_ref[3:4] += column(low_middle.astype(F32))


def feed(units, mixed, cotangent, weights, vectors, hidden_bias):
    count, size, width = units.shape
    inner = hidden_bias.shape[-1]

    def rows(columns):
        return pl.BlockSpec((1, size, columns), lambda u: (u, 0, 0))

    return pl.pallas_call(
        feed_kernel,
        grid=(count,),
        in_specs=[
            rows(width),
            rows(width),
            rows(width),
            whole(weights.shape),
            whole(vectors.shape),
            whole(hidden_bias.shape),
        ],
        out_specs=[
            rows(width),
            rows(width),
            rows(width),
            rows(inner),
            rows(inner),
            rows(width),
            pl.BlockSpec((8, width), lambda u: (0, 0)),
            pl.BlockSpec((8, inner), lambda u: (0, 0)),
        ],
        out_shape=[
            shaped((count, size, width), BF16),
            shaped((count, size, width), BF16),
            shaped((count, size, width), BF16),
            shaped((count, size, inner), BF16),
            shaped((count, size, inner), BF16),
            shaped((count, size, width), BF16),
            shaped((8, width), F32),
            shaped((8, inner), F32),
        ],
        compiler_params=params(1),
        cost_estimate=pl.CostEstimate(
            flops=2 * count * size * width * (4 * inner + 2 * width),
            bytes_accessed=count * size * (width * 20 + inner * 4),
            transcendentals=2 * count * size * inner,
        ),
        name="feed",
    )(units, mixed, cotangent, weights, vectors, hidden_bias)


def weight_kernel(parts, shards, normed_ref, dh_ref, act_ref, dz_ref, o_ref, dp_ref, out_ref, left, right):
    step = pl.program_id(0)
    width = normed_ref.shape[-1]
    rows = width // shards
    per_part = shards // parts

    @pl.when(step == 0)
    def turn():
        left[...] = normed_ref[...].T
        right[...] = dz_ref[...].T

    for part in range(parts):

        @pl.when(step == part)
        def first():
            grad = mul(left[...], dh_ref[...])
            out_ref[:, part * rows : (part + 1) * rows, :] = grad.astype(BF16).reshape(
                shards, rows, width
            )

        @pl.when(step == parts + part)
        def second():
            grad = mul(right[...], act_ref[...]).astype(BF16).T
            out_ref[
                part * per_part : (part + 1) * per_part, parts * rows : 2 * parts * rows, :
            ] = grad.reshape(per_part, parts * rows, width)

    @pl.when(step == 2 * parts)
    def third():
        grad = mul(o_ref[...].T, dp_ref[...])
        out_ref[:, 2 * parts * rows :, :] = grad.astype(BF16).reshape(shards, rows, width)


def weight_grads(normed, grad_hidden, active, grad_branch, mixed, grad_attended, shards):
    count, width = normed.shape
    inner = active.shape[-1]
    parts = inner // width
    shard_rows = (2 * parts + 1) * (width // shards)
    return pl.pallas_call(
        functools.partial(weight_kernel, parts, shards),
        grid=(2 * parts + 1,),
        in_specs=[
            whole(normed.shape),
            pl.BlockSpec((count, width), lambda s: (0, jnp.minimum(s, parts - 1))),
            pl.BlockSpec((count, width), lambda s: (0, jnp.clip(s - parts, 0, parts - 1))),
            whole(grad_branch.shape),
            whole(mixed.shape),
            whole(grad_attended.shape),
        ],
        out_specs=whole((shards, shard_rows, width)),
        out_shape=shaped((shards, shard_rows, width), BF16),
        scratch_shapes=[pltpu.VMEM((width, count), BF16)] * 2,
        compiler_params=params(1),
        cost_estimate=pl.CostEstimate(
            flops=2 * count * width * (2 * inner + width),
            bytes_accessed=count * (8 * width + 4 * inner),
            transcendentals=0,
        ),
        name="weight_grads",
    )(normed, grad_hidden, active, grad_branch, mixed, grad_attended)


def halving_orders(shards):
    reaches = [1 << bit for bit in range(shards.bit_length() - 1)]
    return reaches, reaches[:1] + reaches[2:] + reaches[1:2]


def slot_of(shard, order):
    slot = 0
    for reach in order:
        slot = 2 * slot + (shard // reach) % 2
    return slot


def qkv_weight_kernel(shards, normed_ref, dq_ref, dkv_ref, out_ref, left):
    step = pl.program_id(0)
    width = normed_ref.shape[-1]
    rows = width // shards
    half = width // 2
    orders = halving_orders(shards)

    def keep(side, start, grad):
        for shard in range(shards):
            slot = slot_of(shard, orders[side][1:])
            out_ref[shard % 2, side, slot, :, start : start + grad.shape[1]] = grad[
                shard * rows : (shard + 1) * rows
            ]

    @pl.when(step == 0)
    def query_part():
        left[...] = normed_ref[...].T
        keep(0, 0, mul(left[...], dq_ref[...]).astype(BF16))

    @pl.when(step == 1)
    def key_part():
        grad = mul(left[...], dkv_ref[0]).astype(BF16)
        keep(0, width, grad[:, :half])
        keep(1, 0, grad[:, half:])

    @pl.when(step == 2)
    def value_part():
        keep(1, half, mul(left[...], dkv_ref[0]).astype(BF16))


def qkv_weight_grad(normed, dq, dkv, shards):
    count, width = normed.shape
    half = (2, 2, shards // 2, width // shards, 3 * width // 2)
    return pl.pallas_call(
        functools.partial(qkv_weight_kernel, shards),
        grid=(3,),
        in_specs=[
            whole(normed.shape),
            whole(dq.shape),
            pl.BlockSpec((1, count, width), lambda s: (jnp.maximum(s - 1, 0), 0, 0)),
        ],
        out_specs=whole(half),
        out_shape=shaped(half, BF16),
        scratch_shapes=[pltpu.VMEM((width, count), BF16)],
        compiler_params=params(1),
        cost_estimate=LATE,
        name="qkv_weight_grad",
    )(normed, dq, dkv)


def input_kernel(
    x_ref, dx_ref, dq_ref, dkv_ref, weight_ref, vectors_ref, first_ref, second_ref, third_ref, sums_ref
):
    step = pl.program_id(0)

    @pl.when(step == 0)
    def clear():
        sums_ref[...] = jnp.zeros_like(sums_ref)

    gain = vectors_ref[0:1]
    unused, unit, scale = normalize(x_ref[0].astype(F32), gain, vectors_ref[1:2])
    grad = mul_nt(dq_ref[0], qkv_part(weight_ref, 0))
    grad = grad + mul_nt(dkv_ref[0, 0], qkv_part(weight_ref, 1))
    grad = grad + mul_nt(dkv_ref[1, 0], qkv_part(weight_ref, 2))
    value = (dx_ref[0].astype(F32) + norm_back(grad, unit, scale, gain)).astype(BF16)
    for place, ref in enumerate((first_ref, second_ref, third_ref)):

        @pl.when(step == place)
        def keep():
            ref[...] = value

    sums_ref[0:1] += column(grad * unit)
    sums_ref[1:2] += column(grad)
    sums_ref[2:3] += column(dq_ref[0].astype(F32))
    sums_ref[3:4] += column(dkv_ref[1, 0].astype(F32))


def input_grads(units, grad_middle, dq, dkv, weight, vectors):
    count, size, width = units.shape
    rows = pl.BlockSpec((1, size, width), lambda u: (u, 0, 0))
    return pl.pallas_call(
        input_kernel,
        grid=(count,),
        in_specs=[
            rows,
            rows,
            rows,
            pl.BlockSpec((2, 1, size, width), lambda u: (0, u, 0, 0)),
            whole(weight.shape),
            whole(vectors.shape),
        ],
        out_specs=[whole((size, width))] * 3 + [pl.BlockSpec((8, width), lambda u: (0, 0))],
        out_shape=[shaped((size, width), BF16)] * 3 + [shaped((8, width), F32)],
        compiler_params=params(1),
        cost_estimate=LATE,
        name="input_grads",
    )(units, grad_middle, dq, dkv, weight, vectors)


def halving_sum(value, axis, size, place, order):
    for reach in order:
        pairs = [(index, index ^ reach) for index in range(size)]
        halves = value.reshape((2, value.shape[0] // 2) + value.shape[1:])
        bit = (place // reach) % 2
        got = lax.ppermute(lax.dynamic_index_in_dim(halves, 1 - bit, 0, False), axis, pairs)
        kept = lax.dynamic_index_in_dim(halves, bit, 0, False)
        value = (kept.astype(F32) + got.astype(F32)).astype(BF16)
    return value


def fast_body(fsdp_size, *args):
    (
        inputs,
        cotangent,
        first_gain,
        first_shift,
        qkv_weight,
        query_bias,
        value_bias,
        proj_weight,
        proj_bias,
        second_gain,
        second_shift,
        hidden_weight,
        hidden_bias,
        output_weight,
        output_bias,
    ) = args
    images, size, width = inputs.shape
    row_count = images * size
    side = lax.axis_index("seq")
    place = lax.axis_index("fsdp")
    swap_sides = [(0, 1), (1, 0)]
    swap_cores = [(index, index ^ 1) for index in range(fsdp_size)]
    swap_middle = []
    for index in range(0, fsdp_size, 2):
        swap_middle += [(fsdp_size + index, index + 1), (index + 1, fsdp_size + index)]
    stays = side == place % 2

    def middle_swap(value):
        return jnp.where(stays, value, lax.ppermute(value, ("seq", "fsdp"), swap_middle))

    def gather_units(values):
        got = lax.ppermute(
            lax.dynamic_index_in_dim(values, 2 * (1 - side), 0, False), "seq", swap_sides
        )
        kept = lax.dynamic_index_in_dim(values, 2 * side, 0, False)
        return jnp.stack([kept, got, middle_swap(values[1])])

    def send_back(values):
        return (
            lax.ppermute(values[1], "seq", swap_sides),
            lax.ppermute(values[2], ("seq", "fsdp"), swap_middle),
        )

    def in_place(values, got, centre):
        centre = jnp.where(stays, values[2], centre)
        first = jnp.where(side == 0, values[0], got)
        last = jnp.where(side == 0, got, values[0])
        return jnp.stack([first, centre, last])

    def both(value):
        return value.astype(F32) + lax.ppermute(value, "seq", swap_sides).astype(F32)

    parts = hidden_weight.shape[1] // width
    rows = hidden_weight.shape[0]
    short = [
        first_gain,
        first_shift,
        query_bias,
        value_bias,
        proj_bias,
        second_gain,
        second_shift,
        output_bias,
    ]
    count = first_gain.shape[0]
    full_head = lax.all_gather(head_pack(qkv_weight, hidden_bias, short), "fsdp", axis=0)
    units = gather_units(inputs)
    hidden_weight, output_weight, proj_weight, units = lax.optimization_barrier(
        (hidden_weight, output_weight, proj_weight, units)
    )
    pack = jnp.concatenate(
        [hidden_weight[:, part * width : (part + 1) * width] for part in range(parts)]
        + [output_weight, proj_weight],
        0,
    )
    full_pack = lax.all_gather(pack, "fsdp", axis=0)
    vectors = full_head[:, rows:, :count].astype(F32).transpose(1, 0, 2)
    vectors = vectors.reshape(len(short), width)
    bias_hidden = full_head[:, rows, 128 : 128 + hidden_bias.shape[0]].astype(F32)
    bias_hidden = bias_hidden.reshape(1, parts * width)
    qkv, normed, to_other = project(units, full_head, vectors)
    to_other, cotangent = lax.optimization_barrier((to_other, cotangent))
    other = lax.ppermute(to_other, "fsdp", swap_cores)[:, None]
    grads_up = gather_units(cotangent)
    places_pair = [(qkv, 1, 0), (qkv, 2, 0), (qkv, 1, 1), (qkv, 2, 1)]
    places_one = [(qkv, 1, 2), (qkv, 2, 2), (other, 0, 0), (other, 1, 0)]
    mixed_pair, lse_pair = mix(qkv, 0, 2, places_pair)
    mixed, lse_one = mix(qkv, 2, 1, places_one, mixed_pair)
    (
        out,
        grad_mixed,
        normed_two,
        active,
        grad_hidden,
        grad_attended,
        sums_two,
        sum_hidden,
    ) = feed(units, mixed, grads_up, full_pack, vectors, bias_hidden)
    out_got, out_centre = send_back(out)

    def flat(value):
        return value.reshape(row_count, value.shape[-1])

    grad_pack = weight_grads(
        flat(normed_two),
        flat(grad_hidden),
        flat(active),
        flat(grads_up),
        flat(mixed),
        flat(grad_attended),
        fsdp_size,
    )
    grad_mixed, grad_pack = lax.optimization_barrier((grad_mixed, grad_pack))
    shard_pack = lax.psum_scatter(grad_pack, "fsdp", scatter_dimension=0, tiled=False)
    dq_one, dkv_one, dkv_other = mix_back(qkv, 2, 1, places_one, mixed, grad_mixed, lse_one)
    dkv_got = lax.ppermute(dkv_other, "fsdp", swap_cores)
    dq, dkv, unused = mix_back(qkv, 0, 2, places_pair, mixed, grad_mixed, lse_pair, dq_one)
    dkv = dkv.at[:, 2].set((dkv_one.astype(F32) + dkv_got.astype(F32)).astype(BF16)[:, 0])
    dq, dkv, out_got, out_centre = lax.optimization_barrier((dq, dkv, out_got, out_centre))
    block_out = in_place(out, out_got, out_centre)
    *grad_units, sums_one = input_grads(units, grad_attended, dq, dkv, full_head, vectors)
    got, centre = send_back(grad_units)
    dq, dkv, sums_one = lax.optimization_barrier((dq, dkv, sums_one))
    sides = qkv_weight_grad(flat(normed), flat(dq), dkv.reshape(2, row_count, width), fsdp_size)
    orders = halving_orders(fsdp_size)
    sides = halving_sum(sides, "fsdp", fsdp_size, place, [1])[0]
    sides, shard_pack = lax.optimization_barrier((sides, shard_pack))
    shard_pack = both(shard_pack)
    shard_sides = [
        halving_sum(value, "fsdp", fsdp_size, place, order[1:])[0]
        for value, order in zip(sides, orders)
    ]
    small_grads = [
        sums_one[0],
        sums_one[1],
        sums_one[2],
        sums_one[3],
        sums_two[3],
        sums_two[1],
        sums_two[2],
        sums_two[0],
        sum_hidden[0],
    ]
    packed = jnp.concatenate([value.reshape(fsdp_size, -1) for value in small_grads], 1)
    packed = jnp.pad(packed, ((0, 0), (0, -packed.shape[1] % 1280)))
    lines = packed.shape[1] // 128
    everyone = lax.all_gather(packed.reshape(-1, 128), "fsdp", axis=0)
    shard_sides = [both(value) for value in shard_sides]
    got, centre, shard_sides, everyone = lax.optimization_barrier(
        (got, centre, shard_sides, everyone)
    )
    mine = lax.dynamic_slice_in_dim(everyone, place * lines, lines, 1).sum(0)
    input_grad = in_place(grad_units, got, centre)
    mine = both(mine).reshape(-1)
    pieces = []
    for index in range(len(short)):
        pieces.append(mine[index * count : (index + 1) * count])
    (
        grad_gain_one,
        grad_shift_one,
        grad_query_b,
        grad_value_b,
        grad_proj_b,
        grad_gain_two,
        grad_shift_two,
        grad_output_b,
    ) = pieces
    grad_hidden_b = mine[len(short) * count :][: hidden_bias.shape[0]]
    grad_hidden_w = jnp.concatenate(
        [shard_pack[part * rows : (part + 1) * rows] for part in range(parts)], 1
    )
    grad_output_w = shard_pack[parts * rows : 2 * parts * rows]
    grad_proj_w = shard_pack[2 * parts * rows :]
    grad_qkv_w = jnp.concatenate(shard_sides, 1)
    return (
        block_out,
        input_grad,
        grad_gain_one,
        grad_shift_one,
        grad_qkv_w,
        grad_query_b,
        grad_value_b,
        grad_proj_w,
        grad_proj_b,
        grad_gain_two,
        grad_shift_two,
        grad_hidden_w,
        grad_hidden_b,
        grad_output_w,
        grad_output_b,
    )


def pick_body(seq_size, fsdp_size):
    def body(*args):
        images, size, width = args[0].shape
        inner = args[11].shape[1]
        fits = (
            seq_size == 2
            and images == 3
            and fsdp_size > 1
            and fsdp_size & (fsdp_size - 1) == 0
            and size % 8 == 0
            and width % 128 == 0
            and (width // fsdp_size) % 16 == 0
            and inner % width == 0
            and width // fsdp_size <= 128
            and 128 + inner // fsdp_size <= 3 * width
            and fsdp_size % (inner // width) == 0
        )
        if fits:
            return fast_body(fsdp_size, *args)
        return general_body(*args)

    return body


def solution(mesh):
    shape = mesh.shape
    body = pick_body(shape["seq"], shape["fsdp"])
    return jax.shard_map(
        body,
        mesh=mesh,
        in_specs=(
            P("fsdp", "seq", None),
            P("fsdp", "seq", None),
            P("fsdp"),
            P("fsdp"),
            P("fsdp", None),
            P("fsdp"),
            P("fsdp"),
            P("fsdp", None),
            P("fsdp"),
            P("fsdp"),
            P("fsdp"),
            P("fsdp", None),
            P("fsdp"),
            P("fsdp", None),
            P("fsdp"),
        ),
        out_specs=(
            P("fsdp", "seq", None),
            P("fsdp", "seq", None),
            P("fsdp"),
            P("fsdp"),
            P("fsdp", None),
            P("fsdp"),
            P("fsdp"),
            P("fsdp", None),
            P("fsdp"),
            P("fsdp"),
            P("fsdp"),
            P("fsdp", None),
            P("fsdp"),
            P("fsdp", None),
            P("fsdp"),
        ),
        check_vma=False,
    )
```

```python
import functools

import jax
import jax.numpy as jnp
from jax import lax
from jax.experimental import pallas as pl
from jax.experimental.pallas import tpu as pltpu
from jax.sharding import PartitionSpec as P

HEADS = 12
HEAD_DIM = 64


EPS = 1e-06


def normalize(rows, gain, shift):
    row_mean = jnp.mean(rows, -1, keepdims=True)
    centred = rows - row_mean
    variance = jnp.mean(centred * centred, -1, keepdims=True)
    scaled = lax.rsqrt(variance + EPS)
    unit = centred * scaled
    return (unit * gain + shift, unit, scaled)


def norm_back(grad_out, unit, scaled, gain):
    grad_unit = grad_out * gain
    first_mean = jnp.mean(grad_unit, -1, keepdims=True)
    second_mean = jnp.mean(grad_unit * unit, -1, keepdims=True)
    return scaled * (grad_unit - first_mean - unit * second_mean)


def gelu_exact(value):
    return jax.nn.gelu(value, approximate=False)


def column_sum(values):
    return jnp.sum(values.astype(jnp.float32), 0)


def general_body(
    inputs,
    cotangent,
    first_gain,
    first_shift,
    qkv_weight,
    query_bias,
    value_bias,
    proj_weight,
    proj_bias,
    second_gain,
    second_shift,
    hidden_weight,
    hidden_bias,
    output_weight,
    output_bias,
):
    images, local_len, width = inputs.shape
    row_count = images * local_len
    factor = HEAD_DIM ** (-0.5)
    (
        gain_one,
        shift_one,
        full_qkv,
        bias_query,
        bias_value,
        full_proj,
        bias_proj,
        gain_two,
        shift_two,
        full_hidden,
        bias_hidden,
        full_output,
        bias_output,
    ) = (
        lax.all_gather(first_gain, "fsdp", axis=0, tiled=True),
        lax.all_gather(first_shift, "fsdp", axis=0, tiled=True),
        lax.all_gather(qkv_weight, "fsdp", axis=0, tiled=True),
        lax.all_gather(query_bias, "fsdp", axis=0, tiled=True),
        lax.all_gather(value_bias, "fsdp", axis=0, tiled=True),
        lax.all_gather(proj_weight, "fsdp", axis=0, tiled=True),
        lax.all_gather(proj_bias, "fsdp", axis=0, tiled=True),
        lax.all_gather(second_gain, "fsdp", axis=0, tiled=True),
        lax.all_gather(second_shift, "fsdp", axis=0, tiled=True),
        lax.all_gather(hidden_weight, "fsdp", axis=0, tiled=True),
        lax.all_gather(hidden_bias, "fsdp", axis=0, tiled=True),
        lax.all_gather(output_weight, "fsdp", axis=0, tiled=True),
        lax.all_gather(output_bias, "fsdp", axis=0, tiled=True),
    )
    rows = inputs.reshape(row_count, width).astype(jnp.float32)
    normed, unit_one, scale_one = normalize(
        rows, gain_one.astype(jnp.float32), shift_one.astype(jnp.float32)
    )
    normed_low = normed.astype(jnp.bfloat16)
    projected = jnp.dot(normed_low, full_qkv, preferred_element_type=jnp.float32)
    head_shape = (images, local_len, HEADS, HEAD_DIM)
    query = (
        (projected[:, :width] + bias_query.astype(jnp.float32))
        .astype(jnp.bfloat16)
        .reshape(head_shape)
    )
    keys = projected[:, width : 2 * width].astype(jnp.bfloat16).reshape(head_shape)
    values = (
        (projected[:, 2 * width :] + bias_value.astype(jnp.float32))
        .astype(jnp.bfloat16)
        .reshape(head_shape)
    )
    all_keys, all_values = (
        lax.all_gather(keys, "seq", axis=1, tiled=True),
        lax.all_gather(values, "seq", axis=1, tiled=True),
    )

    def attend(items):
        query_one, key_one, value_one = items
        scores = (
            jnp.einsum("qhd,khd->hqk", query_one, key_one, preferred_element_type=jnp.float32)
            * factor
        )
        row_max = jnp.max(scores, -1, keepdims=True)
        exponent = jnp.exp(scores - row_max)
        row_total = jnp.sum(exponent, -1, keepdims=True)
        weights = (exponent / row_total).astype(jnp.bfloat16)
        mixed_one = jnp.einsum(
            "hqk,khd->qhd", weights, value_one, preferred_element_type=jnp.float32
        )
        return (mixed_one, (row_max + jnp.log(row_total))[..., 0])

    mixed, log_total = lax.map(attend, (query, all_keys, all_values))
    mixed_low = mixed.reshape(row_count, width).astype(jnp.bfloat16)
    attended = jnp.dot(mixed_low, full_proj, preferred_element_type=jnp.float32) + bias_proj.astype(
        jnp.float32
    )
    middle = rows + attended
    normed_two, unit_two, scale_two = normalize(
        middle, gain_two.astype(jnp.float32), shift_two.astype(jnp.float32)
    )
    normed_two_low = normed_two.astype(jnp.bfloat16)
    hidden_pre = jnp.dot(
        normed_two_low, full_hidden, preferred_element_type=jnp.float32
    ) + bias_hidden.astype(jnp.float32)
    activated = gelu_exact(hidden_pre).astype(jnp.bfloat16)
    branch = jnp.dot(
        activated, full_output, preferred_element_type=jnp.float32
    ) + bias_output.astype(jnp.float32)
    block_out = (middle + branch).astype(jnp.bfloat16).reshape(inputs.shape)
    upstream = cotangent.reshape(row_count, width).astype(jnp.float32)
    grad_branch = upstream.astype(jnp.bfloat16)
    grad_output_w = jnp.einsum(
        "rf,rd->fd", activated, grad_branch, preferred_element_type=jnp.float32
    )
    grad_output_b = column_sum(grad_branch)
    grad_act = jnp.einsum("rd,fd->rf", grad_branch, full_output, preferred_element_type=jnp.float32)
    unused_value, pull_gelu = jax.vjp(gelu_exact, hidden_pre)
    grad_hidden = pull_gelu(grad_act)[0].astype(jnp.bfloat16)
    grad_hidden_w = jnp.einsum(
        "rd,rf->df", normed_two_low, grad_hidden, preferred_element_type=jnp.float32
    )
    grad_hidden_b = column_sum(grad_hidden)
    grad_normed_two = jnp.einsum(
        "rf,df->rd", grad_hidden, full_hidden, preferred_element_type=jnp.float32
    )
    grad_gain_two = jnp.sum(grad_normed_two * unit_two, 0)
    grad_shift_two = jnp.sum(grad_normed_two, 0)
    grad_middle = upstream + norm_back(
        grad_normed_two, unit_two, scale_two, gain_two.astype(jnp.float32)
    )
    grad_attended = grad_middle.astype(jnp.bfloat16)
    grad_proj_w = jnp.einsum(
        "re,rd->ed", mixed_low, grad_attended, preferred_element_type=jnp.float32
    )
    grad_proj_b = column_sum(grad_attended)
    grad_mixed = jnp.einsum(
        "rd,ed->re", grad_attended, full_proj, preferred_element_type=jnp.float32
    )
    grad_mixed = grad_mixed.astype(jnp.bfloat16).reshape(head_shape)

    def attend_back(items):
        query_one, key_one, value_one, grad_one, log_one = items
        scores = (
            jnp.einsum("qhd,khd->hqk", query_one, key_one, preferred_element_type=jnp.float32)
            * factor
        )
        probs = jnp.exp(scores - log_one[..., None])
        grad_value = jnp.einsum(
            "hqk,qhd->khd", probs.astype(jnp.bfloat16), grad_one, preferred_element_type=jnp.float32
        )
        grad_probs = jnp.einsum(
            "qhd,khd->hqk", grad_one, value_one, preferred_element_type=jnp.float32
        )
        inner = jnp.sum(probs * grad_probs, -1, keepdims=True)
        grad_scores = (probs * (grad_probs - inner)).astype(jnp.bfloat16)
        grad_query = (
            jnp.einsum("hqk,khd->qhd", grad_scores, key_one, preferred_element_type=jnp.float32)
            * factor
        )
        grad_key = (
            jnp.einsum("hqk,qhd->khd", grad_scores, query_one, preferred_element_type=jnp.float32)
            * factor
        )
        return (grad_query, grad_key, grad_value)

    grad_query, grad_keys, grad_values = lax.map(
        attend_back, (query, all_keys, all_values, grad_mixed, log_total)
    )
    grad_keys, grad_values = (
        lax.psum_scatter(
            grad_keys.astype(jnp.bfloat16), "seq", scatter_dimension=1, tiled=True
        ).astype(jnp.float32),
        lax.psum_scatter(
            grad_values.astype(jnp.bfloat16), "seq", scatter_dimension=1, tiled=True
        ).astype(jnp.float32),
    )
    grad_qkv = jnp.concatenate(
        [
            grad_query.reshape(row_count, width),
            grad_keys.reshape(row_count, width),
            grad_values.reshape(row_count, width),
        ],
        -1,
    ).astype(jnp.bfloat16)
    grad_qkv_w = jnp.einsum("rd,rc->dc", normed_low, grad_qkv, preferred_element_type=jnp.float32)
    grad_query_b = column_sum(grad_qkv[:, :width])
    grad_value_b = column_sum(grad_qkv[:, 2 * width :])
    grad_normed = jnp.einsum("rc,dc->rd", grad_qkv, full_qkv, preferred_element_type=jnp.float32)
    grad_gain_one = jnp.sum(grad_normed * unit_one, 0)
    grad_shift_one = jnp.sum(grad_normed, 0)
    grad_rows = grad_middle + norm_back(
        grad_normed, unit_one, scale_one, gain_one.astype(jnp.float32)
    )
    input_grad = grad_rows.astype(jnp.bfloat16).reshape(inputs.shape)
    parts = (
        lax.psum_scatter(
            grad_gain_one.astype(jnp.bfloat16), "fsdp", scatter_dimension=0, tiled=True
        ).astype(jnp.float32),
        lax.psum_scatter(
            grad_shift_one.astype(jnp.bfloat16), "fsdp", scatter_dimension=0, tiled=True
        ).astype(jnp.float32),
        lax.psum_scatter(
            grad_qkv_w.astype(jnp.bfloat16), "fsdp", scatter_dimension=0, tiled=True
        ).astype(jnp.float32),
        lax.psum_scatter(
            grad_query_b.astype(jnp.bfloat16), "fsdp", scatter_dimension=0, tiled=True
        ).astype(jnp.float32),
        lax.psum_scatter(
            grad_value_b.astype(jnp.bfloat16), "fsdp", scatter_dimension=0, tiled=True
        ).astype(jnp.float32),
        lax.psum_scatter(
            grad_proj_w.astype(jnp.bfloat16), "fsdp", scatter_dimension=0, tiled=True
        ).astype(jnp.float32),
        lax.psum_scatter(
            grad_proj_b.astype(jnp.bfloat16), "fsdp", scatter_dimension=0, tiled=True
        ).astype(jnp.float32),
        lax.psum_scatter(
            grad_gain_two.astype(jnp.bfloat16), "fsdp", scatter_dimension=0, tiled=True
        ).astype(jnp.float32),
        lax.psum_scatter(
            grad_shift_two.astype(jnp.bfloat16), "fsdp", scatter_dimension=0, tiled=True
        ).astype(jnp.float32),
        lax.psum_scatter(
            grad_hidden_w.astype(jnp.bfloat16), "fsdp", scatter_dimension=0, tiled=True
        ).astype(jnp.float32),
        lax.psum_scatter(
            grad_hidden_b.astype(jnp.bfloat16), "fsdp", scatter_dimension=0, tiled=True
        ).astype(jnp.float32),
        lax.psum_scatter(
            grad_output_w.astype(jnp.bfloat16), "fsdp", scatter_dimension=0, tiled=True
        ).astype(jnp.float32),
        lax.psum_scatter(
            grad_output_b.astype(jnp.bfloat16), "fsdp", scatter_dimension=0, tiled=True
        ).astype(jnp.float32),
    )
    shares = (
        lax.psum(parts[0].astype(jnp.bfloat16), "seq").astype(jnp.float32),
        lax.psum(parts[1].astype(jnp.bfloat16), "seq").astype(jnp.float32),
        lax.psum(parts[2].astype(jnp.bfloat16), "seq").astype(jnp.float32),
        lax.psum(parts[3].astype(jnp.bfloat16), "seq").astype(jnp.float32),
        lax.psum(parts[4].astype(jnp.bfloat16), "seq").astype(jnp.float32),
        lax.psum(parts[5].astype(jnp.bfloat16), "seq").astype(jnp.float32),
        lax.psum(parts[6].astype(jnp.bfloat16), "seq").astype(jnp.float32),
        lax.psum(parts[7].astype(jnp.bfloat16), "seq").astype(jnp.float32),
        lax.psum(parts[8].astype(jnp.bfloat16), "seq").astype(jnp.float32),
        lax.psum(parts[9].astype(jnp.bfloat16), "seq").astype(jnp.float32),
        lax.psum(parts[10].astype(jnp.bfloat16), "seq").astype(jnp.float32),
        lax.psum(parts[11].astype(jnp.bfloat16), "seq").astype(jnp.float32),
        lax.psum(parts[12].astype(jnp.bfloat16), "seq").astype(jnp.float32),
    )
    return (
        block_out,
        input_grad,
        shares[0],
        shares[1],
        shares[2],
        shares[3],
        shares[4],
        shares[5],
        shares[6],
        shares[7],
        shares[8],
        shares[9],
        shares[10],
        shares[11],
        shares[12],
    )


F32 = jnp.float32
BF16 = jnp.bfloat16
VMEM_BYTES = 60 * 1024 * 1024
NT = (((1,), (1,)), ((), ()))
LATE = pl.CostEstimate(flops=1000, bytes_accessed=1000, transcendentals=0)


def mul(left, right):
    return jnp.dot(left, right, preferred_element_type=F32)


def mul_nt(left, right):
    return lax.dot_general(left, right, NT, preferred_element_type=F32)


def params(count):
    return pltpu.CompilerParams(
        dimension_semantics=("arbitrary",) * count, vmem_limit_bytes=VMEM_BYTES
    )


def whole(shape):
    return pl.BlockSpec(shape, lambda *ids: (0,) * len(shape), pipeline_mode=pl.Buffered(1))


def shaped(shape, dtype):
    return jax.ShapeDtypeStruct(shape, dtype)


def qkv_part(weight_ref, part):
    width = weight_ref.shape[-1] // 3
    rows = width // weight_ref.shape[0]
    return weight_ref[:, :rows, part * width : (part + 1) * width].reshape(width, width)


def project_kernel(x_ref, weight_ref, vectors_ref, qkv_ref, normed_ref, other_ref):
    step = pl.program_id(0)
    normed, unused_unit, unused_scale = normalize(
        x_ref[0].astype(F32), vectors_ref[0:1], vectors_ref[1:2]
    )
    low = normed.astype(BF16)
    normed_ref[0] = low
    for part in range(3):
        value = mul(low, qkv_part(weight_ref, part))
        if part == 0:
            value = (value + vectors_ref[2:3]) * HEAD_DIM ** (-0.5)
        elif part == 2:
            value = value + vectors_ref[3:4]
        qkv_ref[part, 0] = value.astype(BF16)

    @pl.when(step == pl.num_programs(0) - 1)
    def last():
        other_ref[...] = qkv_ref[1:, 0]


def project(units, weight, vectors):
    count, size, width = units.shape
    return pl.pallas_call(
        project_kernel,
        grid=(count,),
        in_specs=[
            pl.BlockSpec((1, size, width), lambda u: (u, 0, 0)),
            whole(weight.shape),
            whole(vectors.shape),
        ],
        out_specs=[
            pl.BlockSpec((3, 1, size, width), lambda u: (0, u, 0, 0)),
            pl.BlockSpec((1, size, width), lambda u: (u, 0, 0)),
            whole((2, size, width)),
        ],
        out_shape=[
            shaped((3, count, size, width), BF16),
            shaped((count, size, width), BF16),
            shaped((2, size, width), BF16),
        ],
        compiler_params=params(1),
        cost_estimate=pl.CostEstimate(
            flops=2 * count * size * width * 3 * width,
            bytes_accessed=count * size * width * 10 + 6 * width * width,
            transcendentals=0,
        ),
        name="project",
    )(units, weight, vectors)


def head_kernel(weight_ref, hidden_ref, *rest):
    out_ref = rest[-1]
    short = jnp.concatenate([ref[...].astype(F32) for ref in rest[:-1]], 0)
    count, length = short.shape
    columns = weight_ref.shape[1]
    hidden = hidden_ref[...].astype(F32)
    wide = hidden.shape[1]
    hidden = jnp.concatenate([hidden, jnp.zeros((count - 1, wide), F32)], 0)
    lines = jnp.concatenate(
        [
            short,
            jnp.zeros((count, 128 - length), F32),
            hidden,
            jnp.zeros((count, columns - 128 - wide), F32),
        ],
        1,
    )
    out_ref[...] = jnp.concatenate([weight_ref[...].astype(F32), lines], 0).astype(BF16)


def head_pack(weight, hidden, short):
    rows, columns = weight.shape
    return pl.pallas_call(
        head_kernel,
        out_shape=shaped((rows + len(short), columns), BF16),
        name="head_pack",
    )(weight, hidden[None], *[value[None] for value in short])


def head_mask(size):
    return lax.broadcasted_iota(jnp.int32, (size, 2 * HEAD_DIM), 1) // HEAD_DIM


def mix_kernel(q_ref, ka_ref, va_ref, kb_ref, vb_ref, *rest):
    o_ref, lse_ref = rest[-2:]
    query = q_ref[0, 0]
    lanes = head_mask(query.shape[0])
    keys = (ka_ref[0, 0], kb_ref[0, 0])
    turned = (va_ref[0, 0].T, vb_ref[0, 0].T)
    outs = []
    for head in range(2):
        one = jnp.where(lanes == head, query, jnp.zeros_like(query))
        scores = [mul_nt(key, one) for key in keys]
        top = jnp.maximum(
            jnp.max(scores[0], 0, keepdims=True), jnp.max(scores[1], 0, keepdims=True)
        )
        grown = [jnp.exp(score - top) for score in scores]
        total = jnp.sum(grown[0], 0, keepdims=True) + jnp.sum(grown[1], 0, keepdims=True)
        span = slice(head * HEAD_DIM, (head + 1) * HEAD_DIM)
        mixed = mul(turned[0][span], grown[0].astype(BF16)) + mul(
            turned[1][span], grown[1].astype(BF16)
        )
        outs.append(mixed / total)
        lse_ref[0, 0, head : head + 1] = top + jnp.log(total)
    o_ref[0] = jnp.concatenate(outs, 0).T.astype(BF16)


def attend_specs(size, key_places):
    lanes = 2 * HEAD_DIM
    specs = []
    for source, part, unit in key_places:
        specs.append(
            pl.BlockSpec((1, 1, size, lanes), lambda h, u, part=part, unit=unit: (part, unit, 0, h))
        )
    return specs


def mix(qkv, first_unit, unit_count, key_places, earlier=None):
    size, width = qkv.shape[2:]
    lanes = 2 * HEAD_DIM
    pairs = width // lanes
    flops = 4 * unit_count * size * 2 * size * width
    return pl.pallas_call(
        mix_kernel,
        grid=(pairs, unit_count),
        in_specs=[pl.BlockSpec((1, 1, size, lanes), lambda h, u: (0, first_unit + u, 0, h))]
        + attend_specs(size, key_places)
        + [pl.BlockSpec(memory_space=pl.ANY)] * (earlier is not None),
        out_specs=[
            pl.BlockSpec((1, size, lanes), lambda h, u: (first_unit + u, 0, h)),
            pl.BlockSpec((1, 1, 8, size), lambda h, u: (u, h, 0, 0)),
        ],
        out_shape=[
            shaped((qkv.shape[1], size, width), BF16),
            shaped((unit_count, pairs, 8, size), F32),
        ],
        input_output_aliases={} if earlier is None else {5: 0},
        compiler_params=params(2),
        cost_estimate=pl.CostEstimate(
            flops=4 * flops,
            bytes_accessed=unit_count * size * width * 8,
            transcendentals=unit_count * size * 2 * size * width // HEAD_DIM,
        ),
        name="mix",
    )(qkv, *[place[0] for place in key_places], *([] if earlier is None else [earlier]))


def mix_back_kernel(
    unit_count,
    q_ref,
    ka_ref,
    va_ref,
    kb_ref,
    vb_ref,
    o_ref,
    do_ref,
    lse_ref,
    *rest,
):
    dq_ref, dkv_ref, last_ref, dk_acc, dv_acc = rest[-5:]
    step = pl.program_id(1)
    query = q_ref[0, 0]
    grad = do_ref[0]
    size = query.shape[0]
    lanes = head_mask(size)
    keys = (ka_ref[0, 0], kb_ref[0, 0])
    values = (va_ref[0, 0], vb_ref[0, 0])
    turned = (keys[0].T, keys[1].T)
    product = grad.astype(F32) * o_ref[0].astype(F32)
    high = product.astype(BF16)
    rest = (product - high.astype(F32)).astype(BF16)
    chosen = (
        lax.broadcasted_iota(jnp.int32, (8, 2 * HEAD_DIM), 1) // HEAD_DIM
        == lax.broadcasted_iota(jnp.int32, (8, 2 * HEAD_DIM), 0)
    ).astype(BF16)
    inner = mul_nt(chosen, high) + mul_nt(chosen, rest)
    dks, dvs, dqs = [None, None], [None, None], []
    for head in range(2):
        mine = lanes == head
        one_query = jnp.where(mine, query, jnp.zeros_like(query))
        one_grad = jnp.where(mine, grad, jnp.zeros_like(grad))
        span = slice(head * HEAD_DIM, (head + 1) * HEAD_DIM)
        log_row = lse_ref[0, 0, head : head + 1]
        inner_row = inner[head : head + 1]
        dq = None
        for side in range(2):
            probs = jnp.exp(mul_nt(keys[side], one_query) - log_row)
            dv = mul(probs.astype(BF16), one_grad)
            change = mul_nt(values[side], one_grad)
            scored = (probs * (change - inner_row)).astype(BF16)
            dk = mul(scored, one_query)
            part = mul(turned[side][span], scored)
            dq = part if dq is None else dq + part
            dks[side] = dk if head == 0 else dks[side] + dk
            dvs[side] = dv if head == 0 else dvs[side] + dv
        dqs.append(dq)
    dq_ref[0] = (jnp.concatenate(dqs, 0).T * HEAD_DIM ** (-0.5)).astype(BF16)
    if unit_count == 1:
        for side, ref in enumerate((dkv_ref, last_ref)):
            ref[0, 0] = dks[side].astype(BF16)
            ref[1, 0] = dvs[side].astype(BF16)
        return

    last_ref[...] = jnp.zeros_like(last_ref)

    @pl.when(step == 0)
    def first():
        for side in range(2):
            dk_acc[side] = dks[side]
            dv_acc[side] = dvs[side]

    @pl.when(jnp.logical_and(step > 0, step < unit_count - 1))
    def between():
        for side in range(2):
            dk_acc[side] += dks[side]
            dv_acc[side] += dvs[side]

    @pl.when(step == unit_count - 1)
    def last():
        for side in range(2):
            dkv_ref[0, side] = (dk_acc[side] + dks[side]).astype(BF16)
            dkv_ref[1, side] = (dv_acc[side] + dvs[side]).astype(BF16)


def mix_back(qkv, first_unit, unit_count, key_places, mixed, grad_mixed, lse, earlier=None):
    size, width = qkv.shape[2:]
    lanes = 2 * HEAD_DIM
    pairs = width // lanes
    units = qkv.shape[1]
    if unit_count == 1:
        key_outs = [pl.BlockSpec((2, 1, size, lanes), lambda h, u: (0, 0, 0, h))] * 2
        key_shapes = [shaped((2, 1, size, width), BF16)] * 2
    else:
        key_outs = [
            pl.BlockSpec((2, 2, size, lanes), lambda h, u: (0, 0, 0, h)),
            pl.BlockSpec((8, lanes), lambda h, u: (0, 0)),
        ]
        key_shapes = [shaped((2, units, size, width), BF16), shaped((8, lanes), F32)]
    return pl.pallas_call(
        functools.partial(mix_back_kernel, unit_count),
        grid=(pairs, unit_count),
        in_specs=[pl.BlockSpec((1, 1, size, lanes), lambda h, u: (0, first_unit + u, 0, h))]
        + attend_specs(size, key_places)
        + [
            pl.BlockSpec((1, size, lanes), lambda h, u: (first_unit + u, 0, h)),
            pl.BlockSpec((1, size, lanes), lambda h, u: (first_unit + u, 0, h)),
            pl.BlockSpec((1, 1, 8, size), lambda h, u: (u, h, 0, 0)),
        ]
        + [pl.BlockSpec(memory_space=pl.ANY)] * (earlier is not None),
        out_specs=[
            pl.BlockSpec((1, size, lanes), lambda h, u: (first_unit + u, 0, h)),
            *key_outs,
        ],
        out_shape=[shaped((units, size, width), BF16), *key_shapes],
        input_output_aliases={} if earlier is None else {8: 0},
        scratch_shapes=[pltpu.VMEM((2, size, lanes), F32)] * 2,
        compiler_params=params(2),
        cost_estimate=LATE,
        name="mix_back",
    )(
        qkv,
        *[place[0] for place in key_places],
        mixed,
        grad_mixed,
        lse,
        *([] if earlier is None else [earlier]),
    )


def gelu_pair(value):
    share = 0.5 + 0.5 * lax.erf(value * 0.5**0.5)
    density = jnp.exp(value * value * -0.5) * 0.3989422804014327
    return value * share, share + value * density


def column(values):
    return jnp.sum(values, 0, keepdims=True)


def feed_kernel(
    x_ref,
    o_ref,
    cot_ref,
    weights_ref,
    vectors_ref,
    hidden_bias_ref,
    out_ref,
    do_ref,
    normed_ref,
    act_ref,
    dh_ref,
    dp_ref,
    sums_ref,
    hidden_sum_ref,
):
    step = pl.program_id(0)
    width = x_ref.shape[-1]
    shards, shard_rows = weights_ref.shape[:2]
    rows = width // shards
    parts = hidden_bias_ref.shape[-1] // width
    per_part = shards // parts

    @pl.when(step == 0)
    def clear():
        sums_ref[...] = jnp.zeros_like(sums_ref)
        hidden_sum_ref[...] = jnp.zeros_like(hidden_sum_ref)

    proj = weights_ref[:, 2 * parts * rows :, :].reshape(width, width)
    middle = x_ref[0].astype(F32) + (mul(o_ref[0], proj) + vectors_ref[4:5])
    gain = vectors_ref[5:6]
    normed, unit, scale = normalize(middle, gain, vectors_ref[6:7])
    low = normed.astype(BF16)
    normed_ref[0] = low
    upstream = cot_ref[0]
    branch = middle + vectors_ref[7:8]
    grad_normed = None
    for part in range(parts):
        first = weights_ref[:, part * rows : (part + 1) * rows, :].reshape(width, width)
        second = weights_ref[
            part * per_part : (part + 1) * per_part, parts * rows : 2 * parts * rows, :
        ].reshape(width, width)
        span = slice(part * width, (part + 1) * width)
        hidden = mul(low, first) + hidden_bias_ref[:, span]
        active, slope = gelu_pair(hidden)
        active = active.astype(BF16)
        act_ref[0, :, span] = active
        branch = branch + mul(active, second)
        grad_hidden = mul_nt(upstream, second) * slope
        low_grad = grad_hidden.astype(BF16)
        dh_ref[0, :, span] = low_grad
        hidden_sum_ref[0:1, span] += column(low_grad.astype(F32))
        back = mul_nt(low_grad, first)
        grad_normed = back if grad_normed is None else grad_normed + back
    out_ref[0] = branch.astype(BF16)
    wide = upstream.astype(F32)
    grad_middle = wide + norm_back(grad_normed, unit, scale, gain)
    low_middle = grad_middle.astype(BF16)
    dp_ref[0] = low_middle
    do_ref[0] = mul_nt(low_middle, proj).astype(BF16)
    sums_ref[0:1] += column(wide)
    sums_ref[1:2] += column(grad_normed * unit)
    sums_ref[2:3] += column(grad_normed)
    sums_ref[3:4] += column(low_middle.astype(F32))


def feed(units, mixed, cotangent, weights, vectors, hidden_bias):
    count, size, width = units.shape
    inner = hidden_bias.shape[-1]

    def rows(columns):
        return pl.BlockSpec((1, size, columns), lambda u: (u, 0, 0))

    return pl.pallas_call(
        feed_kernel,
        grid=(count,),
        in_specs=[
            rows(width),
            rows(width),
            rows(width),
            whole(weights.shape),
            whole(vectors.shape),
            whole(hidden_bias.shape),
        ],
        out_specs=[
            rows(width),
            rows(width),
            rows(width),
            rows(inner),
            rows(inner),
            rows(width),
            pl.BlockSpec((8, width), lambda u: (0, 0)),
            pl.BlockSpec((8, inner), lambda u: (0, 0)),
        ],
        out_shape=[
            shaped((count, size, width), BF16),
            shaped((count, size, width), BF16),
            shaped((count, size, width), BF16),
            shaped((count, size, inner), BF16),
            shaped((count, size, inner), BF16),
            shaped((count, size, width), BF16),
            shaped((8, width), F32),
            shaped((8, inner), F32),
        ],
        compiler_params=params(1),
        cost_estimate=pl.CostEstimate(
            flops=2 * count * size * width * (4 * inner + 2 * width),
            bytes_accessed=count * size * (width * 20 + inner * 4),
            transcendentals=2 * count * size * inner,
        ),
        name="feed",
    )(units, mixed, cotangent, weights, vectors, hidden_bias)


def weight_kernel(parts, shards, normed_ref, dh_ref, act_ref, dz_ref, o_ref, dp_ref, out_ref, left, right):
    step = pl.program_id(0)
    width = normed_ref.shape[-1]
    rows = width // shards
    per_part = shards // parts

    @pl.when(step == 0)
    def turn():
        left[...] = normed_ref[...].T
        right[...] = dz_ref[...].T

    for part in range(parts):

        @pl.when(step == part)
        def first():
            grad = mul(left[...], dh_ref[...])
            out_ref[:, part * rows : (part + 1) * rows, :] = grad.astype(BF16).reshape(
                shards, rows, width
            )

        @pl.when(step == parts + part)
        def second():
            grad = mul(right[...], act_ref[...]).astype(BF16).T
            out_ref[
                part * per_part : (part + 1) * per_part, parts * rows : 2 * parts * rows, :
            ] = grad.reshape(per_part, parts * rows, width)

    @pl.when(step == 2 * parts)
    def third():
        grad = mul(o_ref[...].T, dp_ref[...])
        out_ref[:, 2 * parts * rows :, :] = grad.astype(BF16).reshape(shards, rows, width)


def weight_grads(normed, grad_hidden, active, grad_branch, mixed, grad_attended, shards):
    count, width = normed.shape
    inner = active.shape[-1]
    parts = inner // width
    shard_rows = (2 * parts + 1) * (width // shards)
    return pl.pallas_call(
        functools.partial(weight_kernel, parts, shards),
        grid=(2 * parts + 1,),
        in_specs=[
            whole(normed.shape),
            pl.BlockSpec((count, width), lambda s: (0, jnp.minimum(s, parts - 1))),
            pl.BlockSpec((count, width), lambda s: (0, jnp.clip(s - parts, 0, parts - 1))),
            whole(grad_branch.shape),
            whole(mixed.shape),
            whole(grad_attended.shape),
        ],
        out_specs=whole((shards, shard_rows, width)),
        out_shape=shaped((shards, shard_rows, width), BF16),
        scratch_shapes=[pltpu.VMEM((width, count), BF16)] * 2,
        compiler_params=params(1),
        cost_estimate=pl.CostEstimate(
            flops=2 * count * width * (2 * inner + width),
            bytes_accessed=count * (8 * width + 4 * inner),
            transcendentals=0,
        ),
        name="weight_grads",
    )(normed, grad_hidden, active, grad_branch, mixed, grad_attended)


def halving_orders(shards):
    reaches = [1 << bit for bit in range(shards.bit_length() - 1)]
    return reaches, reaches[:1] + reaches[2:] + reaches[1:2]


def slot_of(shard, order):
    slot = 0
    for reach in order:
        slot = 2 * slot + (shard // reach) % 2
    return slot


def qkv_weight_kernel(shards, normed_ref, dq_ref, dkv_ref, out_ref, left):
    step = pl.program_id(0)
    width = normed_ref.shape[-1]
    rows = width // shards
    half = width // 2
    orders = halving_orders(shards)

    def keep(side, start, grad):
        for shard in range(shards):
            slot = slot_of(shard, orders[side][1:])
            out_ref[shard % 2, side, slot, :, start : start + grad.shape[1]] = grad[
                shard * rows : (shard + 1) * rows
            ]

    @pl.when(step == 0)
    def query_part():
        left[...] = normed_ref[...].T
        keep(0, 0, mul(left[...], dq_ref[...]).astype(BF16))

    @pl.when(step == 1)
    def key_part():
        grad = mul(left[...], dkv_ref[0]).astype(BF16)
        keep(0, width, grad[:, :half])
        keep(1, 0, grad[:, half:])

    @pl.when(step == 2)
    def value_part():
        keep(1, half, mul(left[...], dkv_ref[0]).astype(BF16))


def qkv_weight_grad(normed, dq, dkv, shards):
    count, width = normed.shape
    half = (2, 2, shards // 2, width // shards, 3 * width // 2)
    return pl.pallas_call(
        functools.partial(qkv_weight_kernel, shards),
        grid=(3,),
        in_specs=[
            whole(normed.shape),
            whole(dq.shape),
            pl.BlockSpec((1, count, width), lambda s: (jnp.maximum(s - 1, 0), 0, 0)),
        ],
        out_specs=whole(half),
        out_shape=shaped(half, BF16),
        scratch_shapes=[pltpu.VMEM((width, count), BF16)],
        compiler_params=params(1),
        cost_estimate=LATE,
        name="qkv_weight_grad",
    )(normed, dq, dkv)


def input_kernel(
    x_ref,
    dx_ref,
    dq_ref,
    dkv_ref,
    weight_ref,
    vectors_ref,
    sums_two_ref,
    hidden_sum_ref,
    first_ref,
    second_ref,
    third_ref,
    sums_ref,
):
    step = pl.program_id(0)
    width = x_ref.shape[-1]

    @pl.when(step == 0)
    def clear():
        sums_ref[...] = jnp.zeros_like(sums_ref)
        sums_ref[4:8] = sums_two_ref[0:4]
        for part in range(hidden_sum_ref.shape[1] // width):
            sums_ref[8 + part : 9 + part] = hidden_sum_ref[0:1, part * width : (part + 1) * width]

    gain = vectors_ref[0:1]
    unused, unit, scale = normalize(x_ref[0].astype(F32), gain, vectors_ref[1:2])
    grad = mul_nt(dq_ref[0], qkv_part(weight_ref, 0))
    grad = grad + mul_nt(dkv_ref[0, 0], qkv_part(weight_ref, 1))
    grad = grad + mul_nt(dkv_ref[1, 0], qkv_part(weight_ref, 2))
    value = (dx_ref[0].astype(F32) + norm_back(grad, unit, scale, gain)).astype(BF16)
    for place, ref in enumerate((first_ref, second_ref, third_ref)):

        @pl.when(step == place)
        def keep():
            ref[...] = value

    sums_ref[0:1] += column(grad * unit)
    sums_ref[1:2] += column(grad)
    sums_ref[2:3] += column(dq_ref[0].astype(F32))
    sums_ref[3:4] += column(dkv_ref[1, 0].astype(F32))


def input_grads(units, grad_middle, dq, dkv, weight, vectors, sums_two, sum_hidden):
    count, size, width = units.shape
    rows = pl.BlockSpec((1, size, width), lambda u: (u, 0, 0))
    return pl.pallas_call(
        input_kernel,
        grid=(count,),
        in_specs=[
            rows,
            rows,
            rows,
            pl.BlockSpec((2, 1, size, width), lambda u: (0, u, 0, 0)),
            whole(weight.shape),
            whole(vectors.shape),
            whole(sums_two.shape),
            whole(sum_hidden.shape),
        ],
        out_specs=[whole((size, width))] * 3 + [whole((32, width))],
        out_shape=[shaped((size, width), BF16)] * 3 + [shaped((32, width), F32)],
        compiler_params=params(1),
        cost_estimate=LATE,
        name="input_grads",
    )(units, grad_middle, dq, dkv, weight, vectors, sums_two, sum_hidden)


def halving_sum(value, axis, size, place, order):
    for reach in order:
        pairs = [(index, index ^ reach) for index in range(size)]
        halves = value.reshape((2, value.shape[0] // 2) + value.shape[1:])
        bit = (place // reach) % 2
        got = lax.ppermute(lax.dynamic_index_in_dim(halves, 1 - bit, 0, False), axis, pairs)
        kept = lax.dynamic_index_in_dim(halves, bit, 0, False)
        value = (kept.astype(F32) + got.astype(F32)).astype(BF16)
    return value


def fast_body(fsdp_size, *args):
    (
        inputs,
        cotangent,
        first_gain,
        first_shift,
        qkv_weight,
        query_bias,
        value_bias,
        proj_weight,
        proj_bias,
        second_gain,
        second_shift,
        hidden_weight,
        hidden_bias,
        output_weight,
        output_bias,
    ) = args
    images, size, width = inputs.shape
    row_count = images * size
    side = lax.axis_index("seq")
    place = lax.axis_index("fsdp")
    swap_sides = [(0, 1), (1, 0)]
    swap_cores = [(index, index ^ 1) for index in range(fsdp_size)]
    swap_middle = []
    for index in range(0, fsdp_size, 2):
        swap_middle += [(fsdp_size + index, index + 1), (index + 1, fsdp_size + index)]
    stays = side == place % 2

    def middle_swap(value):
        return jnp.where(stays, value, lax.ppermute(value, ("seq", "fsdp"), swap_middle))

    def gather_units(values):
        got = lax.ppermute(
            lax.dynamic_index_in_dim(values, 2 * (1 - side), 0, False), "seq", swap_sides
        )
        kept = lax.dynamic_index_in_dim(values, 2 * side, 0, False)
        return jnp.stack([kept, got, middle_swap(values[1])])

    def send_back(values):
        return (
            lax.ppermute(values[1], "seq", swap_sides),
            lax.ppermute(values[2], ("seq", "fsdp"), swap_middle),
        )

    def in_place(values, got, centre):
        centre = jnp.where(stays, values[2], centre)
        first = jnp.where(side == 0, values[0], got)
        last = jnp.where(side == 0, got, values[0])
        return jnp.stack([first, centre, last])

    def both(value):
        return value.astype(F32) + lax.ppermute(value, "seq", swap_sides).astype(F32)

    parts = hidden_weight.shape[1] // width
    rows = hidden_weight.shape[0]
    short = [
        first_gain,
        first_shift,
        query_bias,
        value_bias,
        proj_bias,
        second_gain,
        second_shift,
        output_bias,
    ]
    count = first_gain.shape[0]
    full_head = lax.all_gather(head_pack(qkv_weight, hidden_bias, short), "fsdp", axis=0)
    units = gather_units(inputs)
    hidden_weight, output_weight, proj_weight, units = lax.optimization_barrier(
        (hidden_weight, output_weight, proj_weight, units)
    )
    pack = jnp.concatenate(
        [hidden_weight[:, part * width : (part + 1) * width] for part in range(parts)]
        + [output_weight, proj_weight],
        0,
    )
    full_pack = lax.all_gather(pack, "fsdp", axis=0)
    vectors = full_head[:, rows:, :count].astype(F32).transpose(1, 0, 2)
    vectors = vectors.reshape(len(short), width)
    bias_hidden = full_head[:, rows, 128 : 128 + hidden_bias.shape[0]].astype(F32)
    bias_hidden = bias_hidden.reshape(1, parts * width)
    qkv, normed, to_other = project(units, full_head, vectors)
    to_other, cotangent = lax.optimization_barrier((to_other, cotangent))
    other = lax.ppermute(to_other, "fsdp", swap_cores)[:, None]
    grads_up = gather_units(cotangent)
    places_pair = [(qkv, 1, 0), (qkv, 2, 0), (qkv, 1, 1), (qkv, 2, 1)]
    places_one = [(qkv, 1, 2), (qkv, 2, 2), (other, 0, 0), (other, 1, 0)]
    mixed_pair, lse_pair = mix(qkv, 0, 2, places_pair)
    mixed, lse_one = mix(qkv, 2, 1, places_one, mixed_pair)
    (
        out,
        grad_mixed,
        normed_two,
        active,
        grad_hidden,
        grad_attended,
        sums_two,
        sum_hidden,
    ) = feed(units, mixed, grads_up, full_pack, vectors, bias_hidden)
    out_got, out_centre = send_back(out)

    def flat(value):
        return value.reshape(row_count, value.shape[-1])

    grad_pack = weight_grads(
        flat(normed_two),
        flat(grad_hidden),
        flat(active),
        flat(grads_up),
        flat(mixed),
        flat(grad_attended),
        fsdp_size,
    )
    grad_mixed, grad_pack = lax.optimization_barrier((grad_mixed, grad_pack))
    shard_pack = lax.psum_scatter(grad_pack, "fsdp", scatter_dimension=0, tiled=False)
    dq_one, dkv_one, dkv_other = mix_back(qkv, 2, 1, places_one, mixed, grad_mixed, lse_one)
    dkv_got = lax.ppermute(dkv_other, "fsdp", swap_cores)
    dq, dkv, unused = mix_back(qkv, 0, 2, places_pair, mixed, grad_mixed, lse_pair, dq_one)
    dkv = dkv.at[:, 2].set((dkv_one.astype(F32) + dkv_got.astype(F32)).astype(BF16)[:, 0])
    dq, dkv, out_got, out_centre = lax.optimization_barrier((dq, dkv, out_got, out_centre))
    block_out = in_place(out, out_got, out_centre)
    *grad_units, sums = input_grads(
        units, grad_attended, dq, dkv, full_head, vectors, sums_two, sum_hidden
    )
    got, centre = send_back(grad_units)
    everyone = lax.all_gather(sums, "fsdp", axis=0)
    dq, dkv, sums = lax.optimization_barrier((dq, dkv, sums))
    sides = qkv_weight_grad(flat(normed), flat(dq), dkv.reshape(2, row_count, width), fsdp_size)
    orders = halving_orders(fsdp_size)
    sides = halving_sum(sides, "fsdp", fsdp_size, place, [1])[0]
    sides, shard_pack = lax.optimization_barrier((sides, shard_pack))
    shard_pack = both(shard_pack)
    shard_sides = [
        halving_sum(value, "fsdp", fsdp_size, place, order[1:])[0]
        for value, order in zip(sides, orders)
    ]
    shard_sides = [both(value) for value in shard_sides]
    got, centre, shard_sides, everyone = lax.optimization_barrier(
        (got, centre, shard_sides, everyone)
    )
    input_grad = in_place(grad_units, got, centre)
    totals = both(everyone[:, : 8 + parts].sum(0))
    mine = lax.dynamic_slice_in_dim(totals[:8], place * count, count, 1)
    (
        grad_gain_one,
        grad_shift_one,
        grad_query_b,
        grad_value_b,
        grad_output_b,
        grad_gain_two,
        grad_shift_two,
        grad_proj_b,
    ) = [mine[index] for index in range(8)]
    inner_count = hidden_bias.shape[0]
    grad_hidden_b = lax.dynamic_slice_in_dim(
        totals[8:].reshape(-1), place * inner_count, inner_count, 0
    )
    grad_hidden_w = jnp.concatenate(
        [shard_pack[part * rows : (part + 1) * rows] for part in range(parts)], 1
    )
    grad_output_w = shard_pack[parts * rows : 2 * parts * rows]
    grad_proj_w = shard_pack[2 * parts * rows :]
    grad_qkv_w = jnp.concatenate(shard_sides, 1)
    return (
        block_out,
        input_grad,
        grad_gain_one,
        grad_shift_one,
        grad_qkv_w,
        grad_query_b,
        grad_value_b,
        grad_proj_w,
        grad_proj_b,
        grad_gain_two,
        grad_shift_two,
        grad_hidden_w,
        grad_hidden_b,
        grad_output_w,
        grad_output_b,
    )


def pick_body(seq_size, fsdp_size):
    def body(*args):
        images, size, width = args[0].shape
        inner = args[11].shape[1]
        fits = (
            seq_size == 2
            and images == 3
            and fsdp_size > 1
            and fsdp_size & (fsdp_size - 1) == 0
            and size % 8 == 0
            and width % 128 == 0
            and (width // fsdp_size) % 16 == 0
            and inner % width == 0
            and inner // width <= 24
            and width // fsdp_size <= 128
            and 128 + inner // fsdp_size <= 3 * width
            and fsdp_size % (inner // width) == 0
        )
        if fits:
            return fast_body(fsdp_size, *args)
        return general_body(*args)

    return body


def solution(mesh):
    shape = mesh.shape
    body = pick_body(shape["seq"], shape["fsdp"])
    return jax.shard_map(
        body,
        mesh=mesh,
        in_specs=(
            P("fsdp", "seq", None),
            P("fsdp", "seq", None),
            P("fsdp"),
            P("fsdp"),
            P("fsdp", None),
            P("fsdp"),
            P("fsdp"),
            P("fsdp", None),
            P("fsdp"),
            P("fsdp"),
            P("fsdp"),
            P("fsdp", None),
            P("fsdp"),
            P("fsdp", None),
            P("fsdp"),
        ),
        out_specs=(
            P("fsdp", "seq", None),
            P("fsdp", "seq", None),
            P("fsdp"),
            P("fsdp"),
            P("fsdp", None),
            P("fsdp"),
            P("fsdp"),
            P("fsdp", None),
            P("fsdp"),
            P("fsdp"),
            P("fsdp"),
            P("fsdp", None),
            P("fsdp"),
            P("fsdp", None),
            P("fsdp"),
        ),
        check_vma=False,
    )
```

```python
import functools

import jax
import jax.numpy as jnp
from jax import lax
from jax.experimental import pallas as pl
from jax.experimental.pallas import tpu as pltpu
from jax.sharding import PartitionSpec as P

HEADS = 12
HEAD_DIM = 64


EPS = 1e-06


def normalize(rows, gain, shift):
    row_mean = jnp.mean(rows, -1, keepdims=True)
    centred = rows - row_mean
    variance = jnp.mean(centred * centred, -1, keepdims=True)
    scaled = lax.rsqrt(variance + EPS)
    unit = centred * scaled
    return (unit * gain + shift, unit, scaled)


def norm_back(grad_out, unit, scaled, gain):
    grad_unit = grad_out * gain
    first_mean = jnp.mean(grad_unit, -1, keepdims=True)
    second_mean = jnp.mean(grad_unit * unit, -1, keepdims=True)
    return scaled * (grad_unit - first_mean - unit * second_mean)


def gelu_exact(value):
    return jax.nn.gelu(value, approximate=False)


def column_sum(values):
    return jnp.sum(values.astype(jnp.float32), 0)


def general_body(
    inputs,
    cotangent,
    first_gain,
    first_shift,
    qkv_weight,
    query_bias,
    value_bias,
    proj_weight,
    proj_bias,
    second_gain,
    second_shift,
    hidden_weight,
    hidden_bias,
    output_weight,
    output_bias,
):
    images, local_len, width = inputs.shape
    row_count = images * local_len
    factor = HEAD_DIM ** (-0.5)
    (
        gain_one,
        shift_one,
        full_qkv,
        bias_query,
        bias_value,
        full_proj,
        bias_proj,
        gain_two,
        shift_two,
        full_hidden,
        bias_hidden,
        full_output,
        bias_output,
    ) = (
        lax.all_gather(first_gain, "fsdp", axis=0, tiled=True),
        lax.all_gather(first_shift, "fsdp", axis=0, tiled=True),
        lax.all_gather(qkv_weight, "fsdp", axis=0, tiled=True),
        lax.all_gather(query_bias, "fsdp", axis=0, tiled=True),
        lax.all_gather(value_bias, "fsdp", axis=0, tiled=True),
        lax.all_gather(proj_weight, "fsdp", axis=0, tiled=True),
        lax.all_gather(proj_bias, "fsdp", axis=0, tiled=True),
        lax.all_gather(second_gain, "fsdp", axis=0, tiled=True),
        lax.all_gather(second_shift, "fsdp", axis=0, tiled=True),
        lax.all_gather(hidden_weight, "fsdp", axis=0, tiled=True),
        lax.all_gather(hidden_bias, "fsdp", axis=0, tiled=True),
        lax.all_gather(output_weight, "fsdp", axis=0, tiled=True),
        lax.all_gather(output_bias, "fsdp", axis=0, tiled=True),
    )
    rows = inputs.reshape(row_count, width).astype(jnp.float32)
    normed, unit_one, scale_one = normalize(
        rows, gain_one.astype(jnp.float32), shift_one.astype(jnp.float32)
    )
    normed_low = normed.astype(jnp.bfloat16)
    projected = jnp.dot(normed_low, full_qkv, preferred_element_type=jnp.float32)
    head_shape = (images, local_len, HEADS, HEAD_DIM)
    query = (
        (projected[:, :width] + bias_query.astype(jnp.float32))
        .astype(jnp.bfloat16)
        .reshape(head_shape)
    )
    keys = projected[:, width : 2 * width].astype(jnp.bfloat16).reshape(head_shape)
    values = (
        (projected[:, 2 * width :] + bias_value.astype(jnp.float32))
        .astype(jnp.bfloat16)
        .reshape(head_shape)
    )
    all_keys, all_values = (
        lax.all_gather(keys, "seq", axis=1, tiled=True),
        lax.all_gather(values, "seq", axis=1, tiled=True),
    )

    def attend(items):
        query_one, key_one, value_one = items
        scores = (
            jnp.einsum("qhd,khd->hqk", query_one, key_one, preferred_element_type=jnp.float32)
            * factor
        )
        row_max = jnp.max(scores, -1, keepdims=True)
        exponent = jnp.exp(scores - row_max)
        row_total = jnp.sum(exponent, -1, keepdims=True)
        weights = (exponent / row_total).astype(jnp.bfloat16)
        mixed_one = jnp.einsum(
            "hqk,khd->qhd", weights, value_one, preferred_element_type=jnp.float32
        )
        return (mixed_one, (row_max + jnp.log(row_total))[..., 0])

    mixed, log_total = lax.map(attend, (query, all_keys, all_values))
    mixed_low = mixed.reshape(row_count, width).astype(jnp.bfloat16)
    attended = jnp.dot(mixed_low, full_proj, preferred_element_type=jnp.float32) + bias_proj.astype(
        jnp.float32
    )
    middle = rows + attended
    normed_two, unit_two, scale_two = normalize(
        middle, gain_two.astype(jnp.float32), shift_two.astype(jnp.float32)
    )
    normed_two_low = normed_two.astype(jnp.bfloat16)
    hidden_pre = jnp.dot(
        normed_two_low, full_hidden, preferred_element_type=jnp.float32
    ) + bias_hidden.astype(jnp.float32)
    activated = gelu_exact(hidden_pre).astype(jnp.bfloat16)
    branch = jnp.dot(
        activated, full_output, preferred_element_type=jnp.float32
    ) + bias_output.astype(jnp.float32)
    block_out = (middle + branch).astype(jnp.bfloat16).reshape(inputs.shape)
    upstream = cotangent.reshape(row_count, width).astype(jnp.float32)
    grad_branch = upstream.astype(jnp.bfloat16)
    grad_output_w = jnp.einsum(
        "rf,rd->fd", activated, grad_branch, preferred_element_type=jnp.float32
    )
    grad_output_b = column_sum(grad_branch)
    grad_act = jnp.einsum("rd,fd->rf", grad_branch, full_output, preferred_element_type=jnp.float32)
    unused_value, pull_gelu = jax.vjp(gelu_exact, hidden_pre)
    grad_hidden = pull_gelu(grad_act)[0].astype(jnp.bfloat16)
    grad_hidden_w = jnp.einsum(
        "rd,rf->df", normed_two_low, grad_hidden, preferred_element_type=jnp.float32
    )
    grad_hidden_b = column_sum(grad_hidden)
    grad_normed_two = jnp.einsum(
        "rf,df->rd", grad_hidden, full_hidden, preferred_element_type=jnp.float32
    )
    grad_gain_two = jnp.sum(grad_normed_two * unit_two, 0)
    grad_shift_two = jnp.sum(grad_normed_two, 0)
    grad_middle = upstream + norm_back(
        grad_normed_two, unit_two, scale_two, gain_two.astype(jnp.float32)
    )
    grad_attended = grad_middle.astype(jnp.bfloat16)
    grad_proj_w = jnp.einsum(
        "re,rd->ed", mixed_low, grad_attended, preferred_element_type=jnp.float32
    )
    grad_proj_b = column_sum(grad_attended)
    grad_mixed = jnp.einsum(
        "rd,ed->re", grad_attended, full_proj, preferred_element_type=jnp.float32
    )
    grad_mixed = grad_mixed.astype(jnp.bfloat16).reshape(head_shape)

    def attend_back(items):
        query_one, key_one, value_one, grad_one, log_one = items
        scores = (
            jnp.einsum("qhd,khd->hqk", query_one, key_one, preferred_element_type=jnp.float32)
            * factor
        )
        probs = jnp.exp(scores - log_one[..., None])
        grad_value = jnp.einsum(
            "hqk,qhd->khd", probs.astype(jnp.bfloat16), grad_one, preferred_element_type=jnp.float32
        )
        grad_probs = jnp.einsum(
            "qhd,khd->hqk", grad_one, value_one, preferred_element_type=jnp.float32
        )
        inner = jnp.sum(probs * grad_probs, -1, keepdims=True)
        grad_scores = (probs * (grad_probs - inner)).astype(jnp.bfloat16)
        grad_query = (
            jnp.einsum("hqk,khd->qhd", grad_scores, key_one, preferred_element_type=jnp.float32)
            * factor
        )
        grad_key = (
            jnp.einsum("hqk,qhd->khd", grad_scores, query_one, preferred_element_type=jnp.float32)
            * factor
        )
        return (grad_query, grad_key, grad_value)

    grad_query, grad_keys, grad_values = lax.map(
        attend_back, (query, all_keys, all_values, grad_mixed, log_total)
    )
    grad_keys, grad_values = (
        lax.psum_scatter(
            grad_keys.astype(jnp.bfloat16), "seq", scatter_dimension=1, tiled=True
        ).astype(jnp.float32),
        lax.psum_scatter(
            grad_values.astype(jnp.bfloat16), "seq", scatter_dimension=1, tiled=True
        ).astype(jnp.float32),
    )
    grad_qkv = jnp.concatenate(
        [
            grad_query.reshape(row_count, width),
            grad_keys.reshape(row_count, width),
            grad_values.reshape(row_count, width),
        ],
        -1,
    ).astype(jnp.bfloat16)
    grad_qkv_w = jnp.einsum("rd,rc->dc", normed_low, grad_qkv, preferred_element_type=jnp.float32)
    grad_query_b = column_sum(grad_qkv[:, :width])
    grad_value_b = column_sum(grad_qkv[:, 2 * width :])
    grad_normed = jnp.einsum("rc,dc->rd", grad_qkv, full_qkv, preferred_element_type=jnp.float32)
    grad_gain_one = jnp.sum(grad_normed * unit_one, 0)
    grad_shift_one = jnp.sum(grad_normed, 0)
    grad_rows = grad_middle + norm_back(
        grad_normed, unit_one, scale_one, gain_one.astype(jnp.float32)
    )
    input_grad = grad_rows.astype(jnp.bfloat16).reshape(inputs.shape)
    parts = (
        lax.psum_scatter(
            grad_gain_one.astype(jnp.bfloat16), "fsdp", scatter_dimension=0, tiled=True
        ).astype(jnp.float32),
        lax.psum_scatter(
            grad_shift_one.astype(jnp.bfloat16), "fsdp", scatter_dimension=0, tiled=True
        ).astype(jnp.float32),
        lax.psum_scatter(
            grad_qkv_w.astype(jnp.bfloat16), "fsdp", scatter_dimension=0, tiled=True
        ).astype(jnp.float32),
        lax.psum_scatter(
            grad_query_b.astype(jnp.bfloat16), "fsdp", scatter_dimension=0, tiled=True
        ).astype(jnp.float32),
        lax.psum_scatter(
            grad_value_b.astype(jnp.bfloat16), "fsdp", scatter_dimension=0, tiled=True
        ).astype(jnp.float32),
        lax.psum_scatter(
            grad_proj_w.astype(jnp.bfloat16), "fsdp", scatter_dimension=0, tiled=True
        ).astype(jnp.float32),
        lax.psum_scatter(
            grad_proj_b.astype(jnp.bfloat16), "fsdp", scatter_dimension=0, tiled=True
        ).astype(jnp.float32),
        lax.psum_scatter(
            grad_gain_two.astype(jnp.bfloat16), "fsdp", scatter_dimension=0, tiled=True
        ).astype(jnp.float32),
        lax.psum_scatter(
            grad_shift_two.astype(jnp.bfloat16), "fsdp", scatter_dimension=0, tiled=True
        ).astype(jnp.float32),
        lax.psum_scatter(
            grad_hidden_w.astype(jnp.bfloat16), "fsdp", scatter_dimension=0, tiled=True
        ).astype(jnp.float32),
        lax.psum_scatter(
            grad_hidden_b.astype(jnp.bfloat16), "fsdp", scatter_dimension=0, tiled=True
        ).astype(jnp.float32),
        lax.psum_scatter(
            grad_output_w.astype(jnp.bfloat16), "fsdp", scatter_dimension=0, tiled=True
        ).astype(jnp.float32),
        lax.psum_scatter(
            grad_output_b.astype(jnp.bfloat16), "fsdp", scatter_dimension=0, tiled=True
        ).astype(jnp.float32),
    )
    shares = (
        lax.psum(parts[0].astype(jnp.bfloat16), "seq").astype(jnp.float32),
        lax.psum(parts[1].astype(jnp.bfloat16), "seq").astype(jnp.float32),
        lax.psum(parts[2].astype(jnp.bfloat16), "seq").astype(jnp.float32),
        lax.psum(parts[3].astype(jnp.bfloat16), "seq").astype(jnp.float32),
        lax.psum(parts[4].astype(jnp.bfloat16), "seq").astype(jnp.float32),
        lax.psum(parts[5].astype(jnp.bfloat16), "seq").astype(jnp.float32),
        lax.psum(parts[6].astype(jnp.bfloat16), "seq").astype(jnp.float32),
        lax.psum(parts[7].astype(jnp.bfloat16), "seq").astype(jnp.float32),
        lax.psum(parts[8].astype(jnp.bfloat16), "seq").astype(jnp.float32),
        lax.psum(parts[9].astype(jnp.bfloat16), "seq").astype(jnp.float32),
        lax.psum(parts[10].astype(jnp.bfloat16), "seq").astype(jnp.float32),
        lax.psum(parts[11].astype(jnp.bfloat16), "seq").astype(jnp.float32),
        lax.psum(parts[12].astype(jnp.bfloat16), "seq").astype(jnp.float32),
    )
    return (
        block_out,
        input_grad,
        shares[0],
        shares[1],
        shares[2],
        shares[3],
        shares[4],
        shares[5],
        shares[6],
        shares[7],
        shares[8],
        shares[9],
        shares[10],
        shares[11],
        shares[12],
    )


F32 = jnp.float32
BF16 = jnp.bfloat16
VMEM_BYTES = 60 * 1024 * 1024
NT = (((1,), (1,)), ((), ()))
LATE = pl.CostEstimate(flops=1000, bytes_accessed=1000, transcendentals=0)


def mul(left, right):
    return jnp.dot(left, right, preferred_element_type=F32)


def mul_nt(left, right):
    return lax.dot_general(left, right, NT, preferred_element_type=F32)


def params(count):
    return pltpu.CompilerParams(
        dimension_semantics=("arbitrary",) * count, vmem_limit_bytes=VMEM_BYTES
    )


def whole(shape):
    return pl.BlockSpec(shape, lambda *ids: (0,) * len(shape), pipeline_mode=pl.Buffered(1))


def shaped(shape, dtype):
    return jax.ShapeDtypeStruct(shape, dtype)


def qkv_part(weight_ref, part):
    width = weight_ref.shape[-1] // 3
    rows = width // weight_ref.shape[0]
    return weight_ref[:, :rows, part * width : (part + 1) * width].reshape(width, width)


def project_kernel(x_ref, weight_ref, vectors_ref, qkv_ref, normed_ref, other_ref):
    step = pl.program_id(0)
    normed, unused_unit, unused_scale = normalize(
        x_ref[0].astype(F32), vectors_ref[0:1], vectors_ref[1:2]
    )
    low = normed.astype(BF16)
    normed_ref[0] = low
    for part in range(3):
        value = mul(low, qkv_part(weight_ref, part))
        if part == 0:
            value = (value + vectors_ref[2:3]) * HEAD_DIM ** (-0.5)
        elif part == 2:
            value = value + vectors_ref[3:4]
        qkv_ref[part, 0] = value.astype(BF16)

    @pl.when(step == pl.num_programs(0) - 1)
    def last():
        other_ref[...] = qkv_ref[1:, 0]


def project(units, weight, vectors):
    count, size, width = units.shape
    return pl.pallas_call(
        project_kernel,
        grid=(count,),
        in_specs=[
            pl.BlockSpec((1, size, width), lambda u: (u, 0, 0)),
            whole(weight.shape),
            whole(vectors.shape),
        ],
        out_specs=[
            pl.BlockSpec((3, 1, size, width), lambda u: (0, u, 0, 0)),
            pl.BlockSpec((1, size, width), lambda u: (u, 0, 0)),
            whole((2, size, width)),
        ],
        out_shape=[
            shaped((3, count, size, width), BF16),
            shaped((count, size, width), BF16),
            shaped((2, size, width), BF16),
        ],
        compiler_params=params(1),
        cost_estimate=pl.CostEstimate(
            flops=2 * count * size * width * 3 * width,
            bytes_accessed=count * size * width * 10 + 6 * width * width,
            transcendentals=0,
        ),
        name="project",
    )(units, weight, vectors)


def head_kernel(weight_ref, hidden_ref, *rest):
    out_ref = rest[-1]
    short = jnp.concatenate([ref[...].astype(F32) for ref in rest[:-1]], 0)
    count, length = short.shape
    columns = weight_ref.shape[1]
    hidden = hidden_ref[...].astype(F32)
    wide = hidden.shape[1]
    hidden = jnp.concatenate([hidden, jnp.zeros((count - 1, wide), F32)], 0)
    lines = jnp.concatenate(
        [
            short,
            jnp.zeros((count, 128 - length), F32),
            hidden,
            jnp.zeros((count, columns - 128 - wide), F32),
        ],
        1,
    )
    out_ref[...] = jnp.concatenate([weight_ref[...].astype(F32), lines], 0).astype(BF16)


def head_pack(weight, hidden, short):
    rows, columns = weight.shape
    return pl.pallas_call(
        head_kernel,
        out_shape=shaped((rows + len(short), columns), BF16),
        name="head_pack",
    )(weight, hidden[None], *[value[None] for value in short])


def head_mask(size):
    return lax.broadcasted_iota(jnp.int32, (size, 2 * HEAD_DIM), 1) // HEAD_DIM


def mix_kernel(q_ref, ka_ref, va_ref, kb_ref, vb_ref, *rest):
    o_ref, lse_ref = rest[-2:]
    query = q_ref[0, 0]
    lanes = head_mask(query.shape[0])
    keys = (ka_ref[0, 0], kb_ref[0, 0])
    turned = (va_ref[0, 0].T, vb_ref[0, 0].T)
    outs = []
    for head in range(2):
        one = jnp.where(lanes == head, query, jnp.zeros_like(query))
        scores = [mul_nt(key, one) for key in keys]
        top = jnp.maximum(
            jnp.max(scores[0], 0, keepdims=True), jnp.max(scores[1], 0, keepdims=True)
        )
        grown = [jnp.exp(score - top) for score in scores]
        total = jnp.sum(grown[0], 0, keepdims=True) + jnp.sum(grown[1], 0, keepdims=True)
        span = slice(head * HEAD_DIM, (head + 1) * HEAD_DIM)
        mixed = mul(turned[0][span], grown[0].astype(BF16)) + mul(
            turned[1][span], grown[1].astype(BF16)
        )
        outs.append(mixed / total)
        lse_ref[0, 0, head : head + 1] = top + jnp.log(total)
    o_ref[0] = jnp.concatenate(outs, 0).T.astype(BF16)


def attend_specs(size, key_places):
    lanes = 2 * HEAD_DIM
    specs = []
    for source, part, unit in key_places:
        specs.append(
            pl.BlockSpec((1, 1, size, lanes), lambda h, u, part=part, unit=unit: (part, unit, 0, h))
        )
    return specs


def mix(qkv, first_unit, unit_count, key_places, earlier=None):
    size, width = qkv.shape[2:]
    lanes = 2 * HEAD_DIM
    pairs = width // lanes
    flops = 4 * unit_count * size * 2 * size * width
    return pl.pallas_call(
        mix_kernel,
        grid=(pairs, unit_count),
        in_specs=[pl.BlockSpec((1, 1, size, lanes), lambda h, u: (0, first_unit + u, 0, h))]
        + attend_specs(size, key_places)
        + [pl.BlockSpec(memory_space=pl.ANY)] * (earlier is not None),
        out_specs=[
            pl.BlockSpec((1, size, lanes), lambda h, u: (first_unit + u, 0, h)),
            pl.BlockSpec((1, 1, 8, size), lambda h, u: (u, h, 0, 0)),
        ],
        out_shape=[
            shaped((qkv.shape[1], size, width), BF16),
            shaped((unit_count, pairs, 8, size), F32),
        ],
        input_output_aliases={} if earlier is None else {5: 0},
        compiler_params=params(2),
        cost_estimate=pl.CostEstimate(
            flops=4 * flops,
            bytes_accessed=unit_count * size * width * 8,
            transcendentals=unit_count * size * 2 * size * width // HEAD_DIM,
        ),
        name="mix",
    )(qkv, *[place[0] for place in key_places], *([] if earlier is None else [earlier]))


def mix_back_kernel(
    unit_count,
    q_ref,
    ka_ref,
    va_ref,
    kb_ref,
    vb_ref,
    o_ref,
    do_ref,
    lse_ref,
    *rest,
):
    dq_ref, dkv_ref, last_ref, dk_acc, dv_acc = rest[-5:]
    step = pl.program_id(1)
    query = q_ref[0, 0]
    grad = do_ref[0]
    size = query.shape[0]
    lanes = head_mask(size)
    keys = (ka_ref[0, 0], kb_ref[0, 0])
    values = (va_ref[0, 0], vb_ref[0, 0])
    turned = (keys[0].T, keys[1].T)
    product = grad.astype(F32) * o_ref[0].astype(F32)
    high = product.astype(BF16)
    rest = (product - high.astype(F32)).astype(BF16)
    chosen = (
        lax.broadcasted_iota(jnp.int32, (8, 2 * HEAD_DIM), 1) // HEAD_DIM
        == lax.broadcasted_iota(jnp.int32, (8, 2 * HEAD_DIM), 0)
    ).astype(BF16)
    inner = mul_nt(chosen, high) + mul_nt(chosen, rest)
    dks, dvs, dqs = [None, None], [None, None], []
    for head in range(2):
        mine = lanes == head
        one_query = jnp.where(mine, query, jnp.zeros_like(query))
        one_grad = jnp.where(mine, grad, jnp.zeros_like(grad))
        span = slice(head * HEAD_DIM, (head + 1) * HEAD_DIM)
        log_row = lse_ref[0, 0, head : head + 1]
        inner_row = inner[head : head + 1]
        dq = None
        for side in range(2):
            probs = jnp.exp(mul_nt(keys[side], one_query) - log_row)
            dv = mul(probs.astype(BF16), one_grad)
            change = mul_nt(values[side], one_grad)
            scored = (probs * (change - inner_row)).astype(BF16)
            dk = mul(scored, one_query)
            part = mul(turned[side][span], scored)
            dq = part if dq is None else dq + part
            dks[side] = dk if head == 0 else dks[side] + dk
            dvs[side] = dv if head == 0 else dvs[side] + dv
        dqs.append(dq)
    dq_ref[0] = (jnp.concatenate(dqs, 0).T * HEAD_DIM ** (-0.5)).astype(BF16)
    if unit_count == 1:
        for side, ref in enumerate((dkv_ref, last_ref)):
            ref[0, 0] = dks[side].astype(BF16)
            ref[1, 0] = dvs[side].astype(BF16)
        return

    last_ref[...] = jnp.zeros_like(last_ref)

    @pl.when(step == 0)
    def first():
        for side in range(2):
            dk_acc[side] = dks[side]
            dv_acc[side] = dvs[side]

    @pl.when(jnp.logical_and(step > 0, step < unit_count - 1))
    def between():
        for side in range(2):
            dk_acc[side] += dks[side]
            dv_acc[side] += dvs[side]

    @pl.when(step == unit_count - 1)
    def last():
        for side in range(2):
            dkv_ref[0, side] = (dk_acc[side] + dks[side]).astype(BF16)
            dkv_ref[1, side] = (dv_acc[side] + dvs[side]).astype(BF16)


def mix_back(qkv, first_unit, unit_count, key_places, mixed, grad_mixed, lse, earlier=None):
    size, width = qkv.shape[2:]
    lanes = 2 * HEAD_DIM
    pairs = width // lanes
    units = qkv.shape[1]
    if unit_count == 1:
        key_outs = [pl.BlockSpec((2, 1, size, lanes), lambda h, u: (0, 0, 0, h))] * 2
        key_shapes = [shaped((2, 1, size, width), BF16)] * 2
    else:
        key_outs = [
            pl.BlockSpec((2, 2, size, lanes), lambda h, u: (0, 0, 0, h)),
            pl.BlockSpec((8, lanes), lambda h, u: (0, 0)),
        ]
        key_shapes = [shaped((2, units, size, width), BF16), shaped((8, lanes), F32)]
    return pl.pallas_call(
        functools.partial(mix_back_kernel, unit_count),
        grid=(pairs, unit_count),
        in_specs=[pl.BlockSpec((1, 1, size, lanes), lambda h, u: (0, first_unit + u, 0, h))]
        + attend_specs(size, key_places)
        + [
            pl.BlockSpec((1, size, lanes), lambda h, u: (first_unit + u, 0, h)),
            pl.BlockSpec((1, size, lanes), lambda h, u: (first_unit + u, 0, h)),
            pl.BlockSpec((1, 1, 8, size), lambda h, u: (u, h, 0, 0)),
        ]
        + [pl.BlockSpec(memory_space=pl.ANY)] * (earlier is not None),
        out_specs=[
            pl.BlockSpec((1, size, lanes), lambda h, u: (first_unit + u, 0, h)),
            *key_outs,
        ],
        out_shape=[shaped((units, size, width), BF16), *key_shapes],
        input_output_aliases={} if earlier is None else {8: 0},
        scratch_shapes=[pltpu.VMEM((2, size, lanes), F32)] * 2,
        compiler_params=params(2),
        cost_estimate=LATE,
        name="mix_back",
    )(
        qkv,
        *[place[0] for place in key_places],
        mixed,
        grad_mixed,
        lse,
        *([] if earlier is None else [earlier]),
    )


def gelu_pair(value):
    share = 0.5 + 0.5 * lax.erf(value * 0.5**0.5)
    density = jnp.exp(value * value * -0.5) * 0.3989422804014327
    return value * share, share + value * density


def column(values):
    return jnp.sum(values, 0, keepdims=True)


def feed_kernel(
    x_ref,
    o_ref,
    cot_ref,
    weights_ref,
    vectors_ref,
    hidden_bias_ref,
    out_ref,
    do_ref,
    normed_ref,
    act_ref,
    dh_ref,
    dp_ref,
    sums_ref,
    hidden_sum_ref,
):
    step = pl.program_id(0)
    width = x_ref.shape[-1]
    shards, shard_rows = weights_ref.shape[:2]
    rows = width // shards
    parts = hidden_bias_ref.shape[-1] // width
    per_part = shards // parts

    @pl.when(step == 0)
    def clear():
        sums_ref[...] = jnp.zeros_like(sums_ref)
        hidden_sum_ref[...] = jnp.zeros_like(hidden_sum_ref)

    proj = weights_ref[:, 2 * parts * rows :, :].reshape(width, width)
    middle = x_ref[0].astype(F32) + (mul(o_ref[0], proj) + vectors_ref[4:5])
    gain = vectors_ref[5:6]
    normed, unit, scale = normalize(middle, gain, vectors_ref[6:7])
    low = normed.astype(BF16)
    normed_ref[0] = low
    upstream = cot_ref[0]
    branch = middle + vectors_ref[7:8]
    grad_normed = None
    for part in range(parts):
        first = weights_ref[:, part * rows : (part + 1) * rows, :].reshape(width, width)
        second = weights_ref[
            part * per_part : (part + 1) * per_part, parts * rows : 2 * parts * rows, :
        ].reshape(width, width)
        span = slice(part * width, (part + 1) * width)
        hidden = mul(low, first) + hidden_bias_ref[:, span]
        active, slope = gelu_pair(hidden)
        active = active.astype(BF16)
        act_ref[0, :, span] = active
        branch = branch + mul(active, second)
        grad_hidden = mul_nt(upstream, second) * slope
        low_grad = grad_hidden.astype(BF16)
        dh_ref[0, :, span] = low_grad
        hidden_sum_ref[0:1, span] += column(low_grad.astype(F32))
        back = mul_nt(low_grad, first)
        grad_normed = back if grad_normed is None else grad_normed + back
    out_ref[0] = branch.astype(BF16)
    wide = upstream.astype(F32)
    grad_middle = wide + norm_back(grad_normed, unit, scale, gain)
    low_middle = grad_middle.astype(BF16)
    dp_ref[0] = low_middle
    do_ref[0] = mul_nt(low_middle, proj).astype(BF16)
    sums_ref[0:1] += column(wide)
    sums_ref[1:2] += column(grad_normed * unit)
    sums_ref[2:3] += column(grad_normed)
    sums_ref[3:4] += column(low_middle.astype(F32))


def feed(units, mixed, cotangent, weights, vectors, hidden_bias):
    count, size, width = units.shape
    inner = hidden_bias.shape[-1]

    def rows(columns):
        return pl.BlockSpec((1, size, columns), lambda u: (u, 0, 0))

    return pl.pallas_call(
        feed_kernel,
        grid=(count,),
        in_specs=[
            rows(width),
            rows(width),
            rows(width),
            whole(weights.shape),
            whole(vectors.shape),
            whole(hidden_bias.shape),
        ],
        out_specs=[
            rows(width),
            rows(width),
            rows(width),
            rows(inner),
            rows(inner),
            rows(width),
            pl.BlockSpec((8, width), lambda u: (0, 0)),
            pl.BlockSpec((8, inner), lambda u: (0, 0)),
        ],
        out_shape=[
            shaped((count, size, width), BF16),
            shaped((count, size, width), BF16),
            shaped((count, size, width), BF16),
            shaped((count, size, inner), BF16),
            shaped((count, size, inner), BF16),
            shaped((count, size, width), BF16),
            shaped((8, width), F32),
            shaped((8, inner), F32),
        ],
        compiler_params=params(1),
        cost_estimate=pl.CostEstimate(
            flops=2 * count * size * width * (4 * inner + 2 * width),
            bytes_accessed=count * size * (width * 20 + inner * 4),
            transcendentals=2 * count * size * inner,
        ),
        name="feed",
    )(units, mixed, cotangent, weights, vectors, hidden_bias)


def weight_kernel(parts, shards, normed_ref, dh_ref, act_ref, dz_ref, o_ref, dp_ref, out_ref, left, right):
    step = pl.program_id(0)
    width = normed_ref.shape[-1]
    rows = width // shards
    per_part = shards // parts

    @pl.when(step == 0)
    def turn():
        left[...] = normed_ref[...].T
        right[...] = dz_ref[...].T

    for part in range(parts):

        @pl.when(step == part)
        def first():
            grad = mul(left[...], dh_ref[...])
            out_ref[:, part * rows : (part + 1) * rows, :] = grad.astype(BF16).reshape(
                shards, rows, width
            )

        @pl.when(step == parts + part)
        def second():
            grad = mul(right[...], act_ref[...]).astype(BF16).T
            out_ref[
                part * per_part : (part + 1) * per_part, parts * rows : 2 * parts * rows, :
            ] = grad.reshape(per_part, parts * rows, width)

    @pl.when(step == 2 * parts)
    def third():
        grad = mul(o_ref[...].T, dp_ref[...])
        out_ref[:, 2 * parts * rows :, :] = grad.astype(BF16).reshape(shards, rows, width)


def weight_grads(normed, grad_hidden, active, grad_branch, mixed, grad_attended, shards):
    count, width = normed.shape
    inner = active.shape[-1]
    parts = inner // width
    shard_rows = (2 * parts + 1) * (width // shards)
    return pl.pallas_call(
        functools.partial(weight_kernel, parts, shards),
        grid=(2 * parts + 1,),
        in_specs=[
            whole(normed.shape),
            pl.BlockSpec((count, width), lambda s: (0, jnp.minimum(s, parts - 1))),
            pl.BlockSpec((count, width), lambda s: (0, jnp.clip(s - parts, 0, parts - 1))),
            whole(grad_branch.shape),
            whole(mixed.shape),
            whole(grad_attended.shape),
        ],
        out_specs=whole((shards, shard_rows, width)),
        out_shape=shaped((shards, shard_rows, width), BF16),
        scratch_shapes=[pltpu.VMEM((width, count), BF16)] * 2,
        compiler_params=params(1),
        cost_estimate=pl.CostEstimate(
            flops=2 * count * width * (2 * inner + width),
            bytes_accessed=count * (8 * width + 4 * inner),
            transcendentals=0,
        ),
        name="weight_grads",
    )(normed, grad_hidden, active, grad_branch, mixed, grad_attended)


def halving_orders(shards):
    reaches = [1 << bit for bit in range(shards.bit_length() - 1)]
    return reaches, reaches[:1] + reaches[2:] + reaches[1:2]


def slot_of(shard, order):
    slot = 0
    for reach in order:
        slot = 2 * slot + (shard // reach) % 2
    return slot


def qkv_weight_kernel(shards, parity_ref, normed_ref, dq_ref, dkv_ref, own_ref, send_ref, left):
    step = pl.program_id(0)
    width = normed_ref.shape[-1]
    rows = width // shards
    half = width // 2
    orders = halving_orders(shards)

    def keep(side, start, grad):
        for parity in range(2):

            @pl.when(parity_ref[0] == parity)
            def store():
                for shard in range(shards):
                    ref = own_ref if shard % 2 == parity else send_ref
                    slot = slot_of(shard, orders[side][1:])
                    ref[side, slot, :, start : start + grad.shape[1]] = grad[
                        shard * rows : (shard + 1) * rows
                    ]

    @pl.when(step == 0)
    def query_part():
        left[...] = normed_ref[...].T
        keep(0, 0, mul(left[...], dq_ref[...]).astype(BF16))

    @pl.when(step == 1)
    def key_part():
        grad = mul(left[...], dkv_ref[0]).astype(BF16)
        keep(0, width, grad[:, :half])
        keep(1, 0, grad[:, half:])

    @pl.when(step == 2)
    def value_part():
        keep(1, half, mul(left[...], dkv_ref[0]).astype(BF16))


def qkv_weight_grad(parity, normed, dq, dkv, shards):
    count, width = normed.shape
    half = (2, shards // 2, width // shards, 3 * width // 2)
    return pl.pallas_call(
        functools.partial(qkv_weight_kernel, shards),
        grid=(3,),
        in_specs=[
            pl.BlockSpec(memory_space=pltpu.SMEM),
            whole(normed.shape),
            whole(dq.shape),
            pl.BlockSpec((1, count, width), lambda s: (jnp.maximum(s - 1, 0), 0, 0)),
        ],
        out_specs=[whole(half), whole(half)],
        out_shape=[shaped(half, BF16), shaped(half, BF16)],
        scratch_shapes=[pltpu.VMEM((width, count), BF16)],
        compiler_params=params(1),
        cost_estimate=LATE,
        name="qkv_weight_grad",
    )(parity, normed, dq, dkv)


def input_kernel(
    x_ref,
    dx_ref,
    dq_ref,
    dkv_ref,
    weight_ref,
    vectors_ref,
    sums_two_ref,
    hidden_sum_ref,
    first_ref,
    second_ref,
    third_ref,
    sums_ref,
):
    step = pl.program_id(0)
    width = x_ref.shape[-1]

    @pl.when(step == 0)
    def clear():
        sums_ref[...] = jnp.zeros_like(sums_ref)
        sums_ref[4:8] = sums_two_ref[0:4]
        for part in range(hidden_sum_ref.shape[1] // width):
            sums_ref[8 + part : 9 + part] = hidden_sum_ref[0:1, part * width : (part + 1) * width]

    gain = vectors_ref[0:1]
    unused, unit, scale = normalize(x_ref[0].astype(F32), gain, vectors_ref[1:2])
    grad = mul_nt(dq_ref[0], qkv_part(weight_ref, 0))
    grad = grad + mul_nt(dkv_ref[0, 0], qkv_part(weight_ref, 1))
    grad = grad + mul_nt(dkv_ref[1, 0], qkv_part(weight_ref, 2))
    value = (dx_ref[0].astype(F32) + norm_back(grad, unit, scale, gain)).astype(BF16)
    for place, ref in enumerate((first_ref, second_ref, third_ref)):

        @pl.when(step == place)
        def keep():
            ref[...] = value

    sums_ref[0:1] += column(grad * unit)
    sums_ref[1:2] += column(grad)
    sums_ref[2:3] += column(dq_ref[0].astype(F32))
    sums_ref[3:4] += column(dkv_ref[1, 0].astype(F32))


def input_grads(units, grad_middle, dq, dkv, weight, vectors, sums_two, sum_hidden):
    count, size, width = units.shape
    rows = pl.BlockSpec((1, size, width), lambda u: (u, 0, 0))
    return pl.pallas_call(
        input_kernel,
        grid=(count,),
        in_specs=[
            rows,
            rows,
            rows,
            pl.BlockSpec((2, 1, size, width), lambda u: (0, u, 0, 0)),
            whole(weight.shape),
            whole(vectors.shape),
            whole(sums_two.shape),
            whole(sum_hidden.shape),
        ],
        out_specs=[whole((size, width))] * 3 + [whole((32, width))],
        out_shape=[shaped((size, width), BF16)] * 3 + [shaped((32, width), F32)],
        compiler_params=params(1),
        cost_estimate=LATE,
        name="input_grads",
    )(units, grad_middle, dq, dkv, weight, vectors, sums_two, sum_hidden)


def halving_sum(value, axis, size, place, order):
    for reach in order:
        pairs = [(index, index ^ reach) for index in range(size)]
        halves = value.reshape((2, value.shape[0] // 2) + value.shape[1:])
        bit = (place // reach) % 2
        got = lax.ppermute(lax.dynamic_index_in_dim(halves, 1 - bit, 0, False), axis, pairs)
        kept = lax.dynamic_index_in_dim(halves, bit, 0, False)
        value = (kept.astype(F32) + got.astype(F32)).astype(BF16)
    return value


def fast_body(fsdp_size, *args):
    (
        inputs,
        cotangent,
        first_gain,
        first_shift,
        qkv_weight,
        query_bias,
        value_bias,
        proj_weight,
        proj_bias,
        second_gain,
        second_shift,
        hidden_weight,
        hidden_bias,
        output_weight,
        output_bias,
    ) = args
    images, size, width = inputs.shape
    row_count = images * size
    side = lax.axis_index("seq")
    place = lax.axis_index("fsdp")
    swap_sides = [(0, 1), (1, 0)]
    swap_cores = [(index, index ^ 1) for index in range(fsdp_size)]
    swap_middle = []
    for index in range(0, fsdp_size, 2):
        swap_middle += [(fsdp_size + index, index + 1), (index + 1, fsdp_size + index)]
    stays = side == place % 2

    def middle_swap(value):
        return jnp.where(stays, value, lax.ppermute(value, ("seq", "fsdp"), swap_middle))

    def gather_units(values):
        got = lax.ppermute(
            lax.dynamic_index_in_dim(values, 2 * (1 - side), 0, False), "seq", swap_sides
        )
        kept = lax.dynamic_index_in_dim(values, 2 * side, 0, False)
        return jnp.stack([kept, got, middle_swap(values[1])])

    def send_back(values):
        return (
            lax.ppermute(values[1], "seq", swap_sides),
            lax.ppermute(values[2], ("seq", "fsdp"), swap_middle),
        )

    def in_place(values, got, centre):
        centre = jnp.where(stays, values[2], centre)
        first = jnp.where(side == 0, values[0], got)
        last = jnp.where(side == 0, got, values[0])
        return jnp.stack([first, centre, last])

    def both(value):
        return value.astype(F32) + lax.ppermute(value, "seq", swap_sides).astype(F32)

    parts = hidden_weight.shape[1] // width
    rows = hidden_weight.shape[0]
    short = [
        first_gain,
        first_shift,
        query_bias,
        value_bias,
        proj_bias,
        second_gain,
        second_shift,
        output_bias,
    ]
    count = first_gain.shape[0]
    full_head = lax.all_gather(head_pack(qkv_weight, hidden_bias, short), "fsdp", axis=0)
    units = gather_units(inputs)
    hidden_weight, output_weight, proj_weight, units = lax.optimization_barrier(
        (hidden_weight, output_weight, proj_weight, units)
    )
    pack = jnp.concatenate(
        [hidden_weight[:, part * width : (part + 1) * width] for part in range(parts)]
        + [output_weight, proj_weight],
        0,
    )
    full_pack = lax.all_gather(pack, "fsdp", axis=0)
    vectors = full_head[:, rows:, :count].astype(F32).transpose(1, 0, 2)
    vectors = vectors.reshape(len(short), width)
    bias_hidden = full_head[:, rows, 128 : 128 + hidden_bias.shape[0]].astype(F32)
    bias_hidden = bias_hidden.reshape(1, parts * width)
    qkv, normed, to_other = project(units, full_head, vectors)
    to_other, cotangent = lax.optimization_barrier((to_other, cotangent))
    other = lax.ppermute(to_other, "fsdp", swap_cores)[:, None]
    grads_up = gather_units(cotangent)
    places_pair = [(qkv, 1, 0), (qkv, 2, 0), (qkv, 1, 1), (qkv, 2, 1)]
    places_one = [(qkv, 1, 2), (qkv, 2, 2), (other, 0, 0), (other, 1, 0)]
    mixed_pair, lse_pair = mix(qkv, 0, 2, places_pair)
    mixed, lse_one = mix(qkv, 2, 1, places_one, mixed_pair)
    (
        out,
        grad_mixed,
        normed_two,
        active,
        grad_hidden,
        grad_attended,
        sums_two,
        sum_hidden,
    ) = feed(units, mixed, grads_up, full_pack, vectors, bias_hidden)
    out_got, out_centre = send_back(out)

    def flat(value):
        return value.reshape(row_count, value.shape[-1])

    grad_pack = weight_grads(
        flat(normed_two),
        flat(grad_hidden),
        flat(active),
        flat(grads_up),
        flat(mixed),
        flat(grad_attended),
        fsdp_size,
    )
    grad_mixed, grad_pack = lax.optimization_barrier((grad_mixed, grad_pack))
    shard_pack = lax.psum_scatter(grad_pack, "fsdp", scatter_dimension=0, tiled=False)
    dq_one, dkv_one, dkv_other = mix_back(qkv, 2, 1, places_one, mixed, grad_mixed, lse_one)
    dkv_got = lax.ppermute(dkv_other, "fsdp", swap_cores)
    dq, dkv, unused = mix_back(qkv, 0, 2, places_pair, mixed, grad_mixed, lse_pair, dq_one)
    dkv = dkv.at[:, 2].set((dkv_one.astype(F32) + dkv_got.astype(F32)).astype(BF16)[:, 0])
    dq, dkv, out_got, out_centre = lax.optimization_barrier((dq, dkv, out_got, out_centre))
    block_out = in_place(out, out_got, out_centre)
    *grad_units, sums = input_grads(
        units, grad_attended, dq, dkv, full_head, vectors, sums_two, sum_hidden
    )
    got, centre = send_back(grad_units)
    everyone = lax.all_gather(sums, "fsdp", axis=0)
    dq, dkv, sums, shard_pack = lax.optimization_barrier((dq, dkv, sums, shard_pack))
    pack_got = lax.ppermute(shard_pack, "seq", swap_sides)
    own, send = qkv_weight_grad(
        (place % 2).astype(jnp.int32)[None],
        flat(normed),
        flat(dq),
        dkv.reshape(2, row_count, width),
        fsdp_size,
    )
    orders = halving_orders(fsdp_size)
    sides = (own.astype(F32) + lax.ppermute(send, "fsdp", swap_cores).astype(F32)).astype(BF16)
    shard_sides = [
        halving_sum(value, "fsdp", fsdp_size, place, order[1:])[0]
        for value, order in zip(sides, orders)
    ]
    shard_sides = [both(value) for value in shard_sides]
    got, centre, shard_sides, everyone, pack_got = lax.optimization_barrier(
        (got, centre, shard_sides, everyone, pack_got)
    )
    shard_pack = shard_pack.astype(F32) + pack_got.astype(F32)
    input_grad = in_place(grad_units, got, centre)
    totals = both(everyone[:, : 8 + parts].sum(0))
    mine = lax.dynamic_slice_in_dim(totals[:8], place * count, count, 1)
    (
        grad_gain_one,
        grad_shift_one,
        grad_query_b,
        grad_value_b,
        grad_output_b,
        grad_gain_two,
        grad_shift_two,
        grad_proj_b,
    ) = [mine[index] for index in range(8)]
    inner_count = hidden_bias.shape[0]
    grad_hidden_b = lax.dynamic_slice_in_dim(
        totals[8:].reshape(-1), place * inner_count, inner_count, 0
    )
    grad_hidden_w = jnp.concatenate(
        [shard_pack[part * rows : (part + 1) * rows] for part in range(parts)], 1
    )
    grad_output_w = shard_pack[parts * rows : 2 * parts * rows]
    grad_proj_w = shard_pack[2 * parts * rows :]
    grad_qkv_w = jnp.concatenate(shard_sides, 1)
    return (
        block_out,
        input_grad,
        grad_gain_one,
        grad_shift_one,
        grad_qkv_w,
        grad_query_b,
        grad_value_b,
        grad_proj_w,
        grad_proj_b,
        grad_gain_two,
        grad_shift_two,
        grad_hidden_w,
        grad_hidden_b,
        grad_output_w,
        grad_output_b,
    )


def pick_body(seq_size, fsdp_size):
    def body(*args):
        images, size, width = args[0].shape
        inner = args[11].shape[1]
        fits = (
            seq_size == 2
            and images == 3
            and fsdp_size > 1
            and fsdp_size & (fsdp_size - 1) == 0
            and size % 8 == 0
            and width % 128 == 0
            and (width // fsdp_size) % 16 == 0
            and inner % width == 0
            and inner // width <= 24
            and width // fsdp_size <= 128
            and 128 + inner // fsdp_size <= 3 * width
            and fsdp_size % (inner // width) == 0
        )
        if fits:
            return fast_body(fsdp_size, *args)
        return general_body(*args)

    return body


def solution(mesh):
    shape = mesh.shape
    body = pick_body(shape["seq"], shape["fsdp"])
    return jax.shard_map(
        body,
        mesh=mesh,
        in_specs=(
            P("fsdp", "seq", None),
            P("fsdp", "seq", None),
            P("fsdp"),
            P("fsdp"),
            P("fsdp", None),
            P("fsdp"),
            P("fsdp"),
            P("fsdp", None),
            P("fsdp"),
            P("fsdp"),
            P("fsdp"),
            P("fsdp", None),
            P("fsdp"),
            P("fsdp", None),
            P("fsdp"),
        ),
        out_specs=(
            P("fsdp", "seq", None),
            P("fsdp", "seq", None),
            P("fsdp"),
            P("fsdp"),
            P("fsdp", None),
            P("fsdp"),
            P("fsdp"),
            P("fsdp", None),
            P("fsdp"),
            P("fsdp"),
            P("fsdp"),
            P("fsdp", None),
            P("fsdp"),
            P("fsdp", None),
            P("fsdp"),
        ),
        check_vma=False,
    )
```

```python
import functools

import jax
import jax.numpy as jnp
from jax import lax
from jax.experimental import pallas as pl
from jax.experimental.pallas import tpu as pltpu
from jax.sharding import PartitionSpec as P

HEADS = 12
HEAD_DIM = 64


EPS = 1e-06


def normalize(rows, gain, shift):
    row_mean = jnp.mean(rows, -1, keepdims=True)
    centred = rows - row_mean
    variance = jnp.mean(centred * centred, -1, keepdims=True)
    scaled = lax.rsqrt(variance + EPS)
    unit = centred * scaled
    return (unit * gain + shift, unit, scaled)


def norm_back(grad_out, unit, scaled, gain):
    grad_unit = grad_out * gain
    first_mean = jnp.mean(grad_unit, -1, keepdims=True)
    second_mean = jnp.mean(grad_unit * unit, -1, keepdims=True)
    return scaled * (grad_unit - first_mean - unit * second_mean)


def gelu_exact(value):
    return jax.nn.gelu(value, approximate=False)


def column_sum(values):
    return jnp.sum(values.astype(jnp.float32), 0)


def general_body(
    inputs,
    cotangent,
    first_gain,
    first_shift,
    qkv_weight,
    query_bias,
    value_bias,
    proj_weight,
    proj_bias,
    second_gain,
    second_shift,
    hidden_weight,
    hidden_bias,
    output_weight,
    output_bias,
):
    images, local_len, width = inputs.shape
    row_count = images * local_len
    factor = HEAD_DIM ** (-0.5)
    (
        gain_one,
        shift_one,
        full_qkv,
        bias_query,
        bias_value,
        full_proj,
        bias_proj,
        gain_two,
        shift_two,
        full_hidden,
        bias_hidden,
        full_output,
        bias_output,
    ) = (
        lax.all_gather(first_gain, "fsdp", axis=0, tiled=True),
        lax.all_gather(first_shift, "fsdp", axis=0, tiled=True),
        lax.all_gather(qkv_weight, "fsdp", axis=0, tiled=True),
        lax.all_gather(query_bias, "fsdp", axis=0, tiled=True),
        lax.all_gather(value_bias, "fsdp", axis=0, tiled=True),
        lax.all_gather(proj_weight, "fsdp", axis=0, tiled=True),
        lax.all_gather(proj_bias, "fsdp", axis=0, tiled=True),
        lax.all_gather(second_gain, "fsdp", axis=0, tiled=True),
        lax.all_gather(second_shift, "fsdp", axis=0, tiled=True),
        lax.all_gather(hidden_weight, "fsdp", axis=0, tiled=True),
        lax.all_gather(hidden_bias, "fsdp", axis=0, tiled=True),
        lax.all_gather(output_weight, "fsdp", axis=0, tiled=True),
        lax.all_gather(output_bias, "fsdp", axis=0, tiled=True),
    )
    rows = inputs.reshape(row_count, width).astype(jnp.float32)
    normed, unit_one, scale_one = normalize(
        rows, gain_one.astype(jnp.float32), shift_one.astype(jnp.float32)
    )
    normed_low = normed.astype(jnp.bfloat16)
    projected = jnp.dot(normed_low, full_qkv, preferred_element_type=jnp.float32)
    head_shape = (images, local_len, HEADS, HEAD_DIM)
    query = (
        (projected[:, :width] + bias_query.astype(jnp.float32))
        .astype(jnp.bfloat16)
        .reshape(head_shape)
    )
    keys = projected[:, width : 2 * width].astype(jnp.bfloat16).reshape(head_shape)
    values = (
        (projected[:, 2 * width :] + bias_value.astype(jnp.float32))
        .astype(jnp.bfloat16)
        .reshape(head_shape)
    )
    all_keys, all_values = (
        lax.all_gather(keys, "seq", axis=1, tiled=True),
        lax.all_gather(values, "seq", axis=1, tiled=True),
    )

    def attend(items):
        query_one, key_one, value_one = items
        scores = (
            jnp.einsum("qhd,khd->hqk", query_one, key_one, preferred_element_type=jnp.float32)
            * factor
        )
        row_max = jnp.max(scores, -1, keepdims=True)
        exponent = jnp.exp(scores - row_max)
        row_total = jnp.sum(exponent, -1, keepdims=True)
        weights = (exponent / row_total).astype(jnp.bfloat16)
        mixed_one = jnp.einsum(
            "hqk,khd->qhd", weights, value_one, preferred_element_type=jnp.float32
        )
        return (mixed_one, (row_max + jnp.log(row_total))[..., 0])

    mixed, log_total = lax.map(attend, (query, all_keys, all_values))
    mixed_low = mixed.reshape(row_count, width).astype(jnp.bfloat16)
    attended = jnp.dot(mixed_low, full_proj, preferred_element_type=jnp.float32) + bias_proj.astype(
        jnp.float32
    )
    middle = rows + attended
    normed_two, unit_two, scale_two = normalize(
        middle, gain_two.astype(jnp.float32), shift_two.astype(jnp.float32)
    )
    normed_two_low = normed_two.astype(jnp.bfloat16)
    hidden_pre = jnp.dot(
        normed_two_low, full_hidden, preferred_element_type=jnp.float32
    ) + bias_hidden.astype(jnp.float32)
    activated = gelu_exact(hidden_pre).astype(jnp.bfloat16)
    branch = jnp.dot(
        activated, full_output, preferred_element_type=jnp.float32
    ) + bias_output.astype(jnp.float32)
    block_out = (middle + branch).astype(jnp.bfloat16).reshape(inputs.shape)
    upstream = cotangent.reshape(row_count, width).astype(jnp.float32)
    grad_branch = upstream.astype(jnp.bfloat16)
    grad_output_w = jnp.einsum(
        "rf,rd->fd", activated, grad_branch, preferred_element_type=jnp.float32
    )
    grad_output_b = column_sum(grad_branch)
    grad_act = jnp.einsum("rd,fd->rf", grad_branch, full_output, preferred_element_type=jnp.float32)
    unused_value, pull_gelu = jax.vjp(gelu_exact, hidden_pre)
    grad_hidden = pull_gelu(grad_act)[0].astype(jnp.bfloat16)
    grad_hidden_w = jnp.einsum(
        "rd,rf->df", normed_two_low, grad_hidden, preferred_element_type=jnp.float32
    )
    grad_hidden_b = column_sum(grad_hidden)
    grad_normed_two = jnp.einsum(
        "rf,df->rd", grad_hidden, full_hidden, preferred_element_type=jnp.float32
    )
    grad_gain_two = jnp.sum(grad_normed_two * unit_two, 0)
    grad_shift_two = jnp.sum(grad_normed_two, 0)
    grad_middle = upstream + norm_back(
        grad_normed_two, unit_two, scale_two, gain_two.astype(jnp.float32)
    )
    grad_attended = grad_middle.astype(jnp.bfloat16)
    grad_proj_w = jnp.einsum(
        "re,rd->ed", mixed_low, grad_attended, preferred_element_type=jnp.float32
    )
    grad_proj_b = column_sum(grad_attended)
    grad_mixed = jnp.einsum(
        "rd,ed->re", grad_attended, full_proj, preferred_element_type=jnp.float32
    )
    grad_mixed = grad_mixed.astype(jnp.bfloat16).reshape(head_shape)

    def attend_back(items):
        query_one, key_one, value_one, grad_one, log_one = items
        scores = (
            jnp.einsum("qhd,khd->hqk", query_one, key_one, preferred_element_type=jnp.float32)
            * factor
        )
        probs = jnp.exp(scores - log_one[..., None])
        grad_value = jnp.einsum(
            "hqk,qhd->khd", probs.astype(jnp.bfloat16), grad_one, preferred_element_type=jnp.float32
        )
        grad_probs = jnp.einsum(
            "qhd,khd->hqk", grad_one, value_one, preferred_element_type=jnp.float32
        )
        inner = jnp.sum(probs * grad_probs, -1, keepdims=True)
        grad_scores = (probs * (grad_probs - inner)).astype(jnp.bfloat16)
        grad_query = (
            jnp.einsum("hqk,khd->qhd", grad_scores, key_one, preferred_element_type=jnp.float32)
            * factor
        )
        grad_key = (
            jnp.einsum("hqk,qhd->khd", grad_scores, query_one, preferred_element_type=jnp.float32)
            * factor
        )
        return (grad_query, grad_key, grad_value)

    grad_query, grad_keys, grad_values = lax.map(
        attend_back, (query, all_keys, all_values, grad_mixed, log_total)
    )
    grad_keys, grad_values = (
        lax.psum_scatter(
            grad_keys.astype(jnp.bfloat16), "seq", scatter_dimension=1, tiled=True
        ).astype(jnp.float32),
        lax.psum_scatter(
            grad_values.astype(jnp.bfloat16), "seq", scatter_dimension=1, tiled=True
        ).astype(jnp.float32),
    )
    grad_qkv = jnp.concatenate(
        [
            grad_query.reshape(row_count, width),
            grad_keys.reshape(row_count, width),
            grad_values.reshape(row_count, width),
        ],
        -1,
    ).astype(jnp.bfloat16)
    grad_qkv_w = jnp.einsum("rd,rc->dc", normed_low, grad_qkv, preferred_element_type=jnp.float32)
    grad_query_b = column_sum(grad_qkv[:, :width])
    grad_value_b = column_sum(grad_qkv[:, 2 * width :])
    grad_normed = jnp.einsum("rc,dc->rd", grad_qkv, full_qkv, preferred_element_type=jnp.float32)
    grad_gain_one = jnp.sum(grad_normed * unit_one, 0)
    grad_shift_one = jnp.sum(grad_normed, 0)
    grad_rows = grad_middle + norm_back(
        grad_normed, unit_one, scale_one, gain_one.astype(jnp.float32)
    )
    input_grad = grad_rows.astype(jnp.bfloat16).reshape(inputs.shape)
    parts = (
        lax.psum_scatter(
            grad_gain_one.astype(jnp.bfloat16), "fsdp", scatter_dimension=0, tiled=True
        ).astype(jnp.float32),
        lax.psum_scatter(
            grad_shift_one.astype(jnp.bfloat16), "fsdp", scatter_dimension=0, tiled=True
        ).astype(jnp.float32),
        lax.psum_scatter(
            grad_qkv_w.astype(jnp.bfloat16), "fsdp", scatter_dimension=0, tiled=True
        ).astype(jnp.float32),
        lax.psum_scatter(
            grad_query_b.astype(jnp.bfloat16), "fsdp", scatter_dimension=0, tiled=True
        ).astype(jnp.float32),
        lax.psum_scatter(
            grad_value_b.astype(jnp.bfloat16), "fsdp", scatter_dimension=0, tiled=True
        ).astype(jnp.float32),
        lax.psum_scatter(
            grad_proj_w.astype(jnp.bfloat16), "fsdp", scatter_dimension=0, tiled=True
        ).astype(jnp.float32),
        lax.psum_scatter(
            grad_proj_b.astype(jnp.bfloat16), "fsdp", scatter_dimension=0, tiled=True
        ).astype(jnp.float32),
        lax.psum_scatter(
            grad_gain_two.astype(jnp.bfloat16), "fsdp", scatter_dimension=0, tiled=True
        ).astype(jnp.float32),
        lax.psum_scatter(
            grad_shift_two.astype(jnp.bfloat16), "fsdp", scatter_dimension=0, tiled=True
        ).astype(jnp.float32),
        lax.psum_scatter(
            grad_hidden_w.astype(jnp.bfloat16), "fsdp", scatter_dimension=0, tiled=True
        ).astype(jnp.float32),
        lax.psum_scatter(
            grad_hidden_b.astype(jnp.bfloat16), "fsdp", scatter_dimension=0, tiled=True
        ).astype(jnp.float32),
        lax.psum_scatter(
            grad_output_w.astype(jnp.bfloat16), "fsdp", scatter_dimension=0, tiled=True
        ).astype(jnp.float32),
        lax.psum_scatter(
            grad_output_b.astype(jnp.bfloat16), "fsdp", scatter_dimension=0, tiled=True
        ).astype(jnp.float32),
    )
    shares = (
        lax.psum(parts[0].astype(jnp.bfloat16), "seq").astype(jnp.float32),
        lax.psum(parts[1].astype(jnp.bfloat16), "seq").astype(jnp.float32),
        lax.psum(parts[2].astype(jnp.bfloat16), "seq").astype(jnp.float32),
        lax.psum(parts[3].astype(jnp.bfloat16), "seq").astype(jnp.float32),
        lax.psum(parts[4].astype(jnp.bfloat16), "seq").astype(jnp.float32),
        lax.psum(parts[5].astype(jnp.bfloat16), "seq").astype(jnp.float32),
        lax.psum(parts[6].astype(jnp.bfloat16), "seq").astype(jnp.float32),
        lax.psum(parts[7].astype(jnp.bfloat16), "seq").astype(jnp.float32),
        lax.psum(parts[8].astype(jnp.bfloat16), "seq").astype(jnp.float32),
        lax.psum(parts[9].astype(jnp.bfloat16), "seq").astype(jnp.float32),
        lax.psum(parts[10].astype(jnp.bfloat16), "seq").astype(jnp.float32),
        lax.psum(parts[11].astype(jnp.bfloat16), "seq").astype(jnp.float32),
        lax.psum(parts[12].astype(jnp.bfloat16), "seq").astype(jnp.float32),
    )
    return (
        block_out,
        input_grad,
        shares[0],
        shares[1],
        shares[2],
        shares[3],
        shares[4],
        shares[5],
        shares[6],
        shares[7],
        shares[8],
        shares[9],
        shares[10],
        shares[11],
        shares[12],
    )


F32 = jnp.float32
BF16 = jnp.bfloat16
VMEM_BYTES = 60 * 1024 * 1024
NT = (((1,), (1,)), ((), ()))
LATE = pl.CostEstimate(flops=1000, bytes_accessed=1000, transcendentals=0)


def mul(left, right):
    return jnp.dot(left, right, preferred_element_type=F32)


def mul_nt(left, right):
    return lax.dot_general(left, right, NT, preferred_element_type=F32)


def params(count):
    return pltpu.CompilerParams(
        dimension_semantics=("arbitrary",) * count, vmem_limit_bytes=VMEM_BYTES
    )


def whole(shape):
    return pl.BlockSpec(shape, lambda *ids: (0,) * len(shape), pipeline_mode=pl.Buffered(1))


def shaped(shape, dtype):
    return jax.ShapeDtypeStruct(shape, dtype)


def qkv_part(weight_ref, part):
    width = weight_ref.shape[-1] // 3
    rows = width // weight_ref.shape[0]
    return weight_ref[:, :rows, part * width : (part + 1) * width].reshape(width, width)


def project_kernel(x_ref, weight_ref, vectors_ref, qkv_ref, normed_ref, other_ref):
    step = pl.program_id(0)
    normed, unused_unit, unused_scale = normalize(
        x_ref[0].astype(F32), vectors_ref[0:1], vectors_ref[1:2]
    )
    low = normed.astype(BF16)
    normed_ref[0] = low
    for part in range(3):
        value = mul(low, qkv_part(weight_ref, part))
        if part == 0:
            value = (value + vectors_ref[2:3]) * HEAD_DIM ** (-0.5)
        elif part == 2:
            value = value + vectors_ref[3:4]
        qkv_ref[part, 0] = value.astype(BF16)

    @pl.when(step == pl.num_programs(0) - 1)
    def last():
        other_ref[...] = qkv_ref[1:, 0]


def project(units, weight, vectors):
    count, size, width = units.shape
    return pl.pallas_call(
        project_kernel,
        grid=(count,),
        in_specs=[
            pl.BlockSpec((1, size, width), lambda u: (u, 0, 0)),
            whole(weight.shape),
            whole(vectors.shape),
        ],
        out_specs=[
            pl.BlockSpec((3, 1, size, width), lambda u: (0, u, 0, 0)),
            pl.BlockSpec((1, size, width), lambda u: (u, 0, 0)),
            whole((2, size, width)),
        ],
        out_shape=[
            shaped((3, count, size, width), BF16),
            shaped((count, size, width), BF16),
            shaped((2, size, width), BF16),
        ],
        compiler_params=params(1),
        cost_estimate=pl.CostEstimate(
            flops=2 * count * size * width * 3 * width,
            bytes_accessed=count * size * width * 10 + 6 * width * width,
            transcendentals=0,
        ),
        name="project",
    )(units, weight, vectors)


def head_kernel(weight_ref, hidden_ref, *rest):
    out_ref = rest[-1]
    short = jnp.concatenate([ref[...].astype(F32) for ref in rest[:-1]], 0)
    count, length = short.shape
    columns = weight_ref.shape[1]
    hidden = hidden_ref[...].astype(F32)
    wide = hidden.shape[1]
    hidden = jnp.concatenate([hidden, jnp.zeros((count - 1, wide), F32)], 0)
    lines = jnp.concatenate(
        [
            short,
            jnp.zeros((count, 128 - length), F32),
            hidden,
            jnp.zeros((count, columns - 128 - wide), F32),
        ],
        1,
    )
    out_ref[...] = jnp.concatenate([weight_ref[...].astype(F32), lines], 0).astype(BF16)


def head_pack(weight, hidden, short):
    rows, columns = weight.shape
    return pl.pallas_call(
        head_kernel,
        out_shape=shaped((rows + len(short), columns), BF16),
        name="head_pack",
    )(weight, hidden[None], *[value[None] for value in short])


def head_mask(size):
    return lax.broadcasted_iota(jnp.int32, (size, 2 * HEAD_DIM), 1) // HEAD_DIM


def mix_kernel(q_ref, ka_ref, va_ref, kb_ref, vb_ref, *rest):
    o_ref, lse_ref = rest[-2:]
    query = q_ref[0, 0]
    lanes = head_mask(query.shape[0])
    keys = (ka_ref[0, 0], kb_ref[0, 0])
    turned = (va_ref[0, 0].T, vb_ref[0, 0].T)
    outs = []
    for head in range(2):
        one = jnp.where(lanes == head, query, jnp.zeros_like(query))
        scores = [mul_nt(key, one) for key in keys]
        top = jnp.maximum(
            jnp.max(scores[0], 0, keepdims=True), jnp.max(scores[1], 0, keepdims=True)
        )
        grown = [jnp.exp(score - top) for score in scores]
        total = jnp.sum(grown[0], 0, keepdims=True) + jnp.sum(grown[1], 0, keepdims=True)
        span = slice(head * HEAD_DIM, (head + 1) * HEAD_DIM)
        mixed = mul(turned[0][span], grown[0].astype(BF16)) + mul(
            turned[1][span], grown[1].astype(BF16)
        )
        outs.append(mixed / total)
        lse_ref[0, 0, head : head + 1] = top + jnp.log(total)
    o_ref[0] = jnp.concatenate(outs, 0).T.astype(BF16)


def attend_specs(size, key_places):
    lanes = 2 * HEAD_DIM
    specs = []
    for source, part, unit in key_places:
        specs.append(
            pl.BlockSpec((1, 1, size, lanes), lambda h, u, part=part, unit=unit: (part, unit, 0, h))
        )
    return specs


def mix(qkv, first_unit, unit_count, key_places, earlier=None):
    size, width = qkv.shape[2:]
    lanes = 2 * HEAD_DIM
    pairs = width // lanes
    flops = 4 * unit_count * size * 2 * size * width
    return pl.pallas_call(
        mix_kernel,
        grid=(pairs, unit_count),
        in_specs=[pl.BlockSpec((1, 1, size, lanes), lambda h, u: (0, first_unit + u, 0, h))]
        + attend_specs(size, key_places)
        + [pl.BlockSpec(memory_space=pl.ANY)] * (earlier is not None),
        out_specs=[
            pl.BlockSpec((1, size, lanes), lambda h, u: (first_unit + u, 0, h)),
            pl.BlockSpec((1, 1, 8, size), lambda h, u: (u, h, 0, 0)),
        ],
        out_shape=[
            shaped((qkv.shape[1], size, width), BF16),
            shaped((unit_count, pairs, 8, size), F32),
        ],
        input_output_aliases={} if earlier is None else {5: 0},
        compiler_params=params(2),
        cost_estimate=pl.CostEstimate(
            flops=4 * flops,
            bytes_accessed=unit_count * size * width * 8,
            transcendentals=unit_count * size * 2 * size * width // HEAD_DIM,
        ),
        name="mix",
    )(qkv, *[place[0] for place in key_places], *([] if earlier is None else [earlier]))


def mix_back_kernel(
    unit_count,
    q_ref,
    ka_ref,
    va_ref,
    kb_ref,
    vb_ref,
    o_ref,
    do_ref,
    lse_ref,
    *rest,
):
    dq_ref, dkv_ref, last_ref, dk_acc, dv_acc = rest[-5:]
    step = pl.program_id(1)
    query = q_ref[0, 0]
    grad = do_ref[0]
    size = query.shape[0]
    lanes = head_mask(size)
    keys = (ka_ref[0, 0], kb_ref[0, 0])
    values = (va_ref[0, 0], vb_ref[0, 0])
    turned = (keys[0].T, keys[1].T)
    product = grad.astype(F32) * o_ref[0].astype(F32)
    high = product.astype(BF16)
    rest = (product - high.astype(F32)).astype(BF16)
    chosen = (
        lax.broadcasted_iota(jnp.int32, (8, 2 * HEAD_DIM), 1) // HEAD_DIM
        == lax.broadcasted_iota(jnp.int32, (8, 2 * HEAD_DIM), 0)
    ).astype(BF16)
    inner = mul_nt(chosen, high) + mul_nt(chosen, rest)
    dks, dvs, dqs = [None, None], [None, None], []
    for head in range(2):
        mine = lanes == head
        one_query = jnp.where(mine, query, jnp.zeros_like(query))
        one_grad = jnp.where(mine, grad, jnp.zeros_like(grad))
        span = slice(head * HEAD_DIM, (head + 1) * HEAD_DIM)
        log_row = lse_ref[0, 0, head : head + 1]
        inner_row = inner[head : head + 1]
        dq = None
        for side in range(2):
            probs = jnp.exp(mul_nt(keys[side], one_query) - log_row)
            dv = mul(probs.astype(BF16), one_grad)
            change = mul_nt(values[side], one_grad)
            scored = (probs * (change - inner_row)).astype(BF16)
            dk = mul(scored, one_query)
            part = mul(turned[side][span], scored)
            dq = part if dq is None else dq + part
            dks[side] = dk if head == 0 else dks[side] + dk
            dvs[side] = dv if head == 0 else dvs[side] + dv
        dqs.append(dq)
    dq_ref[0] = (jnp.concatenate(dqs, 0).T * HEAD_DIM ** (-0.5)).astype(BF16)
    if unit_count == 1:
        for side, ref in enumerate((dkv_ref, last_ref)):
            ref[0, 0] = dks[side].astype(BF16)
            ref[1, 0] = dvs[side].astype(BF16)
        return

    last_ref[...] = jnp.zeros_like(last_ref)

    @pl.when(step == 0)
    def first():
        for side in range(2):
            dk_acc[side] = dks[side]
            dv_acc[side] = dvs[side]

    @pl.when(jnp.logical_and(step > 0, step < unit_count - 1))
    def between():
        for side in range(2):
            dk_acc[side] += dks[side]
            dv_acc[side] += dvs[side]

    @pl.when(step == unit_count - 1)
    def last():
        for side in range(2):
            dkv_ref[0, side] = (dk_acc[side] + dks[side]).astype(BF16)
            dkv_ref[1, side] = (dv_acc[side] + dvs[side]).astype(BF16)


def mix_back(qkv, first_unit, unit_count, key_places, mixed, grad_mixed, lse, earlier=None):
    size, width = qkv.shape[2:]
    lanes = 2 * HEAD_DIM
    pairs = width // lanes
    units = qkv.shape[1]
    if unit_count == 1:
        key_outs = [pl.BlockSpec((2, 1, size, lanes), lambda h, u: (0, 0, 0, h))] * 2
        key_shapes = [shaped((2, 1, size, width), BF16)] * 2
    else:
        key_outs = [
            pl.BlockSpec((2, 2, size, lanes), lambda h, u: (0, 0, 0, h)),
            pl.BlockSpec((8, lanes), lambda h, u: (0, 0)),
        ]
        key_shapes = [shaped((2, units, size, width), BF16), shaped((8, lanes), F32)]
    return pl.pallas_call(
        functools.partial(mix_back_kernel, unit_count),
        grid=(pairs, unit_count),
        in_specs=[pl.BlockSpec((1, 1, size, lanes), lambda h, u: (0, first_unit + u, 0, h))]
        + attend_specs(size, key_places)
        + [
            pl.BlockSpec((1, size, lanes), lambda h, u: (first_unit + u, 0, h)),
            pl.BlockSpec((1, size, lanes), lambda h, u: (first_unit + u, 0, h)),
            pl.BlockSpec((1, 1, 8, size), lambda h, u: (u, h, 0, 0)),
        ]
        + [pl.BlockSpec(memory_space=pl.ANY)] * (earlier is not None),
        out_specs=[
            pl.BlockSpec((1, size, lanes), lambda h, u: (first_unit + u, 0, h)),
            *key_outs,
        ],
        out_shape=[shaped((units, size, width), BF16), *key_shapes],
        input_output_aliases={} if earlier is None else {8: 0},
        scratch_shapes=[pltpu.VMEM((2, size, lanes), F32)] * 2,
        compiler_params=params(2),
        cost_estimate=LATE,
        name="mix_back",
    )(
        qkv,
        *[place[0] for place in key_places],
        mixed,
        grad_mixed,
        lse,
        *([] if earlier is None else [earlier]),
    )


def gelu_pair(value):
    share = 0.5 + 0.5 * lax.erf(value * 0.5**0.5)
    density = jnp.exp(value * value * -0.5) * 0.3989422804014327
    return value * share, share + value * density


def column(values):
    return jnp.sum(values, 0, keepdims=True)


def feed_kernel(
    x_ref,
    o_ref,
    cot_ref,
    weights_ref,
    vectors_ref,
    hidden_bias_ref,
    out_ref,
    do_ref,
    normed_ref,
    act_ref,
    dh_ref,
    dp_ref,
    sums_ref,
    hidden_sum_ref,
):
    step = pl.program_id(0)
    width = x_ref.shape[-1]
    shards, shard_rows = weights_ref.shape[:2]
    rows = width // shards
    parts = hidden_bias_ref.shape[-1] // width
    per_part = shards // parts

    @pl.when(step == 0)
    def clear():
        sums_ref[...] = jnp.zeros_like(sums_ref)
        hidden_sum_ref[...] = jnp.zeros_like(hidden_sum_ref)

    proj = weights_ref[:, 2 * parts * rows :, :].reshape(width, width)
    middle = x_ref[0].astype(F32) + (mul(o_ref[0], proj) + vectors_ref[4:5])
    gain = vectors_ref[5:6]
    normed, unit, scale = normalize(middle, gain, vectors_ref[6:7])
    low = normed.astype(BF16)
    normed_ref[0] = low
    upstream = cot_ref[0]
    branch = middle + vectors_ref[7:8]
    grad_normed = None
    for part in range(parts):
        first = weights_ref[:, part * rows : (part + 1) * rows, :].reshape(width, width)
        second = weights_ref[
            part * per_part : (part + 1) * per_part, parts * rows : 2 * parts * rows, :
        ].reshape(width, width)
        span = slice(part * width, (part + 1) * width)
        hidden = mul(low, first) + hidden_bias_ref[:, span]
        active, slope = gelu_pair(hidden)
        active = active.astype(BF16)
        act_ref[0, :, span] = active
        branch = branch + mul(active, second)
        grad_hidden = mul_nt(upstream, second) * slope
        low_grad = grad_hidden.astype(BF16)
        dh_ref[0, :, span] = low_grad
        hidden_sum_ref[0:1, span] += column(low_grad.astype(F32))
        back = mul_nt(low_grad, first)
        grad_normed = back if grad_normed is None else grad_normed + back
    out_ref[0] = branch.astype(BF16)
    wide = upstream.astype(F32)
    grad_middle = wide + norm_back(grad_normed, unit, scale, gain)
    low_middle = grad_middle.astype(BF16)
    dp_ref[0] = low_middle
    do_ref[0] = mul_nt(low_middle, proj).astype(BF16)
    sums_ref[0:1] += column(wide)
    sums_ref[1:2] += column(grad_normed * unit)
    sums_ref[2:3] += column(grad_normed)
    sums_ref[3:4] += column(low_middle.astype(F32))


def feed(units, mixed, cotangent, weights, vectors, hidden_bias):
    count, size, width = units.shape
    inner = hidden_bias.shape[-1]

    def rows(columns):
        return pl.BlockSpec((1, size, columns), lambda u: (u, 0, 0))

    return pl.pallas_call(
        feed_kernel,
        grid=(count,),
        in_specs=[
            rows(width),
            rows(width),
            rows(width),
            whole(weights.shape),
            whole(vectors.shape),
            whole(hidden_bias.shape),
        ],
        out_specs=[
            rows(width),
            rows(width),
            rows(width),
            rows(inner),
            rows(inner),
            rows(width),
            pl.BlockSpec((8, width), lambda u: (0, 0)),
            pl.BlockSpec((8, inner), lambda u: (0, 0)),
        ],
        out_shape=[
            shaped((count, size, width), BF16),
            shaped((count, size, width), BF16),
            shaped((count, size, width), BF16),
            shaped((count, size, inner), BF16),
            shaped((count, size, inner), BF16),
            shaped((count, size, width), BF16),
            shaped((8, width), F32),
            shaped((8, inner), F32),
        ],
        compiler_params=params(1),
        cost_estimate=pl.CostEstimate(
            flops=2 * count * size * width * (4 * inner + 2 * width),
            bytes_accessed=count * size * (width * 20 + inner * 4),
            transcendentals=2 * count * size * inner,
        ),
        name="feed",
    )(units, mixed, cotangent, weights, vectors, hidden_bias)


def weight_kernel(parts, shards, normed_ref, dh_ref, act_ref, dz_ref, o_ref, dp_ref, out_ref, left, right):
    step = pl.program_id(0)
    width = normed_ref.shape[-1]
    rows = width // shards
    per_part = shards // parts

    @pl.when(step == 0)
    def turn():
        left[...] = normed_ref[...].T
        right[...] = dz_ref[...].T

    for part in range(parts):

        @pl.when(step == part)
        def first():
            grad = mul(left[...], dh_ref[...])
            out_ref[:, part * rows : (part + 1) * rows, :] = grad.astype(BF16).reshape(
                shards, rows, width
            )

        @pl.when(step == parts + part)
        def second():
            grad = mul(right[...], act_ref[...]).astype(BF16).T
            out_ref[
                part * per_part : (part + 1) * per_part, parts * rows : 2 * parts * rows, :
            ] = grad.reshape(per_part, parts * rows, width)

    @pl.when(step == 2 * parts)
    def third():
        grad = mul(o_ref[...].T, dp_ref[...])
        out_ref[:, 2 * parts * rows :, :] = grad.astype(BF16).reshape(shards, rows, width)


def weight_grads(normed, grad_hidden, active, grad_branch, mixed, grad_attended, shards):
    count, width = normed.shape
    inner = active.shape[-1]
    parts = inner // width
    shard_rows = (2 * parts + 1) * (width // shards)
    return pl.pallas_call(
        functools.partial(weight_kernel, parts, shards),
        grid=(2 * parts + 1,),
        in_specs=[
            whole(normed.shape),
            pl.BlockSpec((count, width), lambda s: (0, jnp.minimum(s, parts - 1))),
            pl.BlockSpec((count, width), lambda s: (0, jnp.clip(s - parts, 0, parts - 1))),
            whole(grad_branch.shape),
            whole(mixed.shape),
            whole(grad_attended.shape),
        ],
        out_specs=whole((shards, shard_rows, width)),
        out_shape=shaped((shards, shard_rows, width), BF16),
        scratch_shapes=[pltpu.VMEM((width, count), BF16)] * 2,
        compiler_params=params(1),
        cost_estimate=pl.CostEstimate(
            flops=2 * count * width * (2 * inner + width),
            bytes_accessed=count * (8 * width + 4 * inner),
            transcendentals=0,
        ),
        name="weight_grads",
    )(normed, grad_hidden, active, grad_branch, mixed, grad_attended)


def halving_orders(shards):
    reaches = [1 << bit for bit in range(shards.bit_length() - 1)]
    return reaches, reaches[:1] + reaches[2:] + reaches[1:2]


def slot_of(shard, order):
    slot = 0
    for reach in order:
        slot = 2 * slot + (shard // reach) % 2
    return slot


def qkv_weight_kernel(shards, parity_ref, normed_ref, dq_ref, dkv_ref, own_ref, send_ref, left):
    step = pl.program_id(0)
    width = normed_ref.shape[-1]
    rows = width // shards
    half = width // 2
    orders = halving_orders(shards)

    def keep(side, start, grad):
        for parity in range(2):

            @pl.when(parity_ref[0] == parity)
            def store():
                for shard in range(shards):
                    ref = own_ref if shard % 2 == parity else send_ref
                    slot = slot_of(shard, orders[side][1:])
                    ref[side, slot, :, start : start + grad.shape[1]] = grad[
                        shard * rows : (shard + 1) * rows
                    ]

    @pl.when(step == 0)
    def query_part():
        left[...] = normed_ref[...].T
        keep(0, 0, mul(left[...], dq_ref[...]).astype(BF16))

    @pl.when(step == 1)
    def key_part():
        grad = mul(left[...], dkv_ref[0]).astype(BF16)
        keep(0, width, grad[:, :half])
        keep(1, 0, grad[:, half:])

    @pl.when(step == 2)
    def value_part():
        keep(1, half, mul(left[...], dkv_ref[0]).astype(BF16))


def qkv_weight_grad(parity, normed, dq, dkv, shards):
    count, width = normed.shape
    half = (2, shards // 2, width // shards, 3 * width // 2)
    return pl.pallas_call(
        functools.partial(qkv_weight_kernel, shards),
        grid=(3,),
        in_specs=[
            pl.BlockSpec(memory_space=pltpu.SMEM),
            whole(normed.shape),
            whole(dq.shape),
            pl.BlockSpec((1, count, width), lambda s: (jnp.maximum(s - 1, 0), 0, 0)),
        ],
        out_specs=[whole(half), whole(half)],
        out_shape=[shaped(half, BF16), shaped(half, BF16)],
        scratch_shapes=[pltpu.VMEM((width, count), BF16)],
        compiler_params=params(1),
        cost_estimate=LATE,
        name="qkv_weight_grad",
    )(parity, normed, dq, dkv)


def input_kernel(
    x_ref,
    dx_ref,
    dq_ref,
    dkv_ref,
    weight_ref,
    vectors_ref,
    sums_two_ref,
    hidden_sum_ref,
    first_ref,
    second_ref,
    third_ref,
    sums_ref,
):
    step = pl.program_id(0)
    width = x_ref.shape[-1]

    @pl.when(step == 0)
    def clear():
        sums_ref[...] = jnp.zeros_like(sums_ref)
        sums_ref[4:8] = sums_two_ref[0:4]
        for part in range(hidden_sum_ref.shape[1] // width):
            sums_ref[8 + part : 9 + part] = hidden_sum_ref[0:1, part * width : (part + 1) * width]

    gain = vectors_ref[0:1]
    unused, unit, scale = normalize(x_ref[0].astype(F32), gain, vectors_ref[1:2])
    grad = mul_nt(dq_ref[0], qkv_part(weight_ref, 0))
    grad = grad + mul_nt(dkv_ref[0, 0], qkv_part(weight_ref, 1))
    grad = grad + mul_nt(dkv_ref[1, 0], qkv_part(weight_ref, 2))
    value = (dx_ref[0].astype(F32) + norm_back(grad, unit, scale, gain)).astype(BF16)
    for place, ref in enumerate((first_ref, second_ref, third_ref)):

        @pl.when(step == place)
        def keep():
            ref[...] = value

    sums_ref[0:1] += column(grad * unit)
    sums_ref[1:2] += column(grad)
    sums_ref[2:3] += column(dq_ref[0].astype(F32))
    sums_ref[3:4] += column(dkv_ref[1, 0].astype(F32))


def input_grads(units, grad_middle, dq, dkv, weight, vectors, sums_two, sum_hidden):
    count, size, width = units.shape
    rows = pl.BlockSpec((1, size, width), lambda u: (u, 0, 0))
    return pl.pallas_call(
        input_kernel,
        grid=(count,),
        in_specs=[
            rows,
            rows,
            rows,
            pl.BlockSpec((2, 1, size, width), lambda u: (0, u, 0, 0)),
            whole(weight.shape),
            whole(vectors.shape),
            whole(sums_two.shape),
            whole(sum_hidden.shape),
        ],
        out_specs=[whole((size, width))] * 3 + [whole((32, width))],
        out_shape=[shaped((size, width), BF16)] * 3 + [shaped((32, width), F32)],
        compiler_params=params(1),
        cost_estimate=LATE,
        name="input_grads",
    )(units, grad_middle, dq, dkv, weight, vectors, sums_two, sum_hidden)


def halving_sum(value, axis, size, place, order):
    for reach in order:
        pairs = [(index, index ^ reach) for index in range(size)]
        halves = value.reshape((2, value.shape[0] // 2) + value.shape[1:])
        bit = (place // reach) % 2
        got = lax.ppermute(lax.dynamic_index_in_dim(halves, 1 - bit, 0, False), axis, pairs)
        kept = lax.dynamic_index_in_dim(halves, bit, 0, False)
        value = (kept.astype(F32) + got.astype(F32)).astype(BF16)
    return value


def fast_body(fsdp_size, *args):
    (
        inputs,
        cotangent,
        first_gain,
        first_shift,
        qkv_weight,
        query_bias,
        value_bias,
        proj_weight,
        proj_bias,
        second_gain,
        second_shift,
        hidden_weight,
        hidden_bias,
        output_weight,
        output_bias,
    ) = args
    images, size, width = inputs.shape
    row_count = images * size
    side = lax.axis_index("seq")
    place = lax.axis_index("fsdp")
    swap_sides = [(0, 1), (1, 0)]
    swap_cores = [(index, index ^ 1) for index in range(fsdp_size)]
    swap_middle = []
    for index in range(0, fsdp_size, 2):
        swap_middle += [(fsdp_size + index, index + 1), (index + 1, fsdp_size + index)]
    stays = side == place % 2

    def middle_swap(value):
        return jnp.where(stays, value, lax.ppermute(value, ("seq", "fsdp"), swap_middle))

    def gather_units(values):
        got = lax.ppermute(
            lax.dynamic_index_in_dim(values, 2 * (1 - side), 0, False), "seq", swap_sides
        )
        kept = lax.dynamic_index_in_dim(values, 2 * side, 0, False)
        return jnp.stack([kept, got, middle_swap(values[1])])

    def send_back(values):
        return (
            lax.ppermute(values[1], "seq", swap_sides),
            lax.ppermute(values[2], ("seq", "fsdp"), swap_middle),
        )

    def in_place(values, got, centre):
        centre = jnp.where(stays, values[2], centre)
        first = jnp.where(side == 0, values[0], got)
        last = jnp.where(side == 0, got, values[0])
        return jnp.stack([first, centre, last])

    def both(value):
        return value.astype(F32) + lax.ppermute(value, "seq", swap_sides).astype(F32)

    parts = hidden_weight.shape[1] // width
    rows = hidden_weight.shape[0]
    short = [
        first_gain,
        first_shift,
        query_bias,
        value_bias,
        proj_bias,
        second_gain,
        second_shift,
        output_bias,
    ]
    count = first_gain.shape[0]
    full_head = lax.all_gather(head_pack(qkv_weight, hidden_bias, short), "fsdp", axis=0)
    units = gather_units(inputs)
    hidden_weight, output_weight, proj_weight, units = lax.optimization_barrier(
        (hidden_weight, output_weight, proj_weight, units)
    )
    pack = jnp.concatenate(
        [hidden_weight[:, part * width : (part + 1) * width] for part in range(parts)]
        + [output_weight, proj_weight],
        0,
    )
    full_pack = lax.all_gather(pack, "fsdp", axis=0)
    vectors = full_head[:, rows:, :count].astype(F32).transpose(1, 0, 2)
    vectors = vectors.reshape(len(short), width)
    bias_hidden = full_head[:, rows, 128 : 128 + hidden_bias.shape[0]].astype(F32)
    bias_hidden = bias_hidden.reshape(1, parts * width)
    qkv, normed, to_other = project(units, full_head, vectors)
    to_other, cotangent = lax.optimization_barrier((to_other, cotangent))
    other = lax.ppermute(to_other, "fsdp", swap_cores)[:, None]
    grads_up = gather_units(cotangent)
    places_pair = [(qkv, 1, 0), (qkv, 2, 0), (qkv, 1, 1), (qkv, 2, 1)]
    places_one = [(qkv, 1, 2), (qkv, 2, 2), (other, 0, 0), (other, 1, 0)]
    mixed_pair, lse_pair = mix(qkv, 0, 2, places_pair)
    mixed, lse_one = mix(qkv, 2, 1, places_one, mixed_pair)
    (
        out,
        grad_mixed,
        normed_two,
        active,
        grad_hidden,
        grad_attended,
        sums_two,
        sum_hidden,
    ) = feed(units, mixed, grads_up, full_pack, vectors, bias_hidden)
    out_got, out_centre = send_back(out)

    def flat(value):
        return value.reshape(row_count, value.shape[-1])

    grad_pack = weight_grads(
        flat(normed_two),
        flat(grad_hidden),
        flat(active),
        flat(grads_up),
        flat(mixed),
        flat(grad_attended),
        fsdp_size,
    )
    grad_mixed, grad_pack = lax.optimization_barrier((grad_mixed, grad_pack))
    shard_pack = lax.psum_scatter(grad_pack, "fsdp", scatter_dimension=0, tiled=False)
    dq_one, dkv_one, dkv_other = mix_back(qkv, 2, 1, places_one, mixed, grad_mixed, lse_one)
    dkv_got = lax.ppermute(dkv_other, "fsdp", swap_cores)
    dq, dkv, unused = mix_back(qkv, 0, 2, places_pair, mixed, grad_mixed, lse_pair, dq_one)
    dkv = dkv.at[:, 2].set((dkv_one.astype(F32) + dkv_got.astype(F32)).astype(BF16)[:, 0])
    dq, dkv, out_got, out_centre = lax.optimization_barrier((dq, dkv, out_got, out_centre))
    block_out = in_place(out, out_got, out_centre)
    *grad_units, sums = input_grads(
        units, grad_attended, dq, dkv, full_head, vectors, sums_two, sum_hidden
    )
    got, centre = send_back(grad_units)
    everyone = lax.all_gather(sums, "fsdp", axis=0)
    dq, dkv, sums = lax.optimization_barrier((dq, dkv, sums))
    own, send = qkv_weight_grad(
        (place % 2).astype(jnp.int32)[None],
        flat(normed),
        flat(dq),
        dkv.reshape(2, row_count, width),
        fsdp_size,
    )
    orders = halving_orders(fsdp_size)
    sides = (own.astype(F32) + lax.ppermute(send, "fsdp", swap_cores).astype(F32)).astype(BF16)
    sides, shard_pack = lax.optimization_barrier((sides, shard_pack))
    pack_got = lax.ppermute(shard_pack, "seq", swap_sides)
    shard_sides = [
        halving_sum(value, "fsdp", fsdp_size, place, order[1:])[0]
        for value, order in zip(sides, orders)
    ]
    shard_sides = [both(value) for value in shard_sides]
    got, centre, shard_sides, everyone, pack_got = lax.optimization_barrier(
        (got, centre, shard_sides, everyone, pack_got)
    )
    shard_pack = shard_pack.astype(F32) + pack_got.astype(F32)
    input_grad = in_place(grad_units, got, centre)
    totals = both(everyone[:, : 8 + parts].sum(0))
    mine = lax.dynamic_slice_in_dim(totals[:8], place * count, count, 1)
    (
        grad_gain_one,
        grad_shift_one,
        grad_query_b,
        grad_value_b,
        grad_output_b,
        grad_gain_two,
        grad_shift_two,
        grad_proj_b,
    ) = [mine[index] for index in range(8)]
    inner_count = hidden_bias.shape[0]
    grad_hidden_b = lax.dynamic_slice_in_dim(
        totals[8:].reshape(-1), place * inner_count, inner_count, 0
    )
    grad_hidden_w = jnp.concatenate(
        [shard_pack[part * rows : (part + 1) * rows] for part in range(parts)], 1
    )
    grad_output_w = shard_pack[parts * rows : 2 * parts * rows]
    grad_proj_w = shard_pack[2 * parts * rows :]
    grad_qkv_w = jnp.concatenate(shard_sides, 1)
    return (
        block_out,
        input_grad,
        grad_gain_one,
        grad_shift_one,
        grad_qkv_w,
        grad_query_b,
        grad_value_b,
        grad_proj_w,
        grad_proj_b,
        grad_gain_two,
        grad_shift_two,
        grad_hidden_w,
        grad_hidden_b,
        grad_output_w,
        grad_output_b,
    )


def pick_body(seq_size, fsdp_size):
    def body(*args):
        images, size, width = args[0].shape
        inner = args[11].shape[1]
        fits = (
            seq_size == 2
            and images == 3
            and fsdp_size > 1
            and fsdp_size & (fsdp_size - 1) == 0
            and size % 8 == 0
            and width % 128 == 0
            and (width // fsdp_size) % 16 == 0
            and inner % width == 0
            and inner // width <= 24
            and width // fsdp_size <= 128
            and 128 + inner // fsdp_size <= 3 * width
            and fsdp_size % (inner // width) == 0
        )
        if fits:
            return fast_body(fsdp_size, *args)
        return general_body(*args)

    return body


def solution(mesh):
    shape = mesh.shape
    body = pick_body(shape["seq"], shape["fsdp"])
    return jax.shard_map(
        body,
        mesh=mesh,
        in_specs=(
            P("fsdp", "seq", None),
            P("fsdp", "seq", None),
            P("fsdp"),
            P("fsdp"),
            P("fsdp", None),
            P("fsdp"),
            P("fsdp"),
            P("fsdp", None),
            P("fsdp"),
            P("fsdp"),
            P("fsdp"),
            P("fsdp", None),
            P("fsdp"),
            P("fsdp", None),
            P("fsdp"),
        ),
        out_specs=(
            P("fsdp", "seq", None),
            P("fsdp", "seq", None),
            P("fsdp"),
            P("fsdp"),
            P("fsdp", None),
            P("fsdp"),
            P("fsdp"),
            P("fsdp", None),
            P("fsdp"),
            P("fsdp"),
            P("fsdp"),
            P("fsdp", None),
            P("fsdp"),
            P("fsdp", None),
            P("fsdp"),
        ),
        check_vma=False,
    )
```
